32 devices in a mesh: rep: 2 (over y), tp: 4 (over z), ad: 4 (over x, core).
Axes of the slice: x: 2, y: 2, z: 4, core: 2. Of those that a mesh axis runs over, the one named last changes fastest.
Arguments:
- activations: bfloat16 [4096, 8192], P(('rep', 'ad'), 'tp'), parts along dimension 0, may hold values from -6 to 6
- adapter_of_row: int32 [4096], P(('rep', 'ad')), parts along dimension 0, may hold values from 0 to 4095, as said below
- adapter_resident_slot: int32 [8192], P('rep'), parts along dimension 0, may hold values from -1 to 31, as said below
- key_value_weight: bfloat16 [8192, 2048], P('tp'), may hold values from -0.09375 to 0.09375
- resident_down_factors: bfloat16 [16384, 2048], P(('rep', 'tp'), 'ad'), parts along dimension 0, may hold values from -0.0625 to 0.0625
- resident_up_factors: bfloat16 [4096, 2048], P(('rep', 'ad'), 'tp'), parts along dimension 0, may hold values from -0.75 to 0.75
Outputs:
- kv_out: bfloat16 [4096, 2048], P(('rep', 'ad'), 'tp'), parts along dimension 0
The draws below stay inside these ranges and needn't reach their ends.
There are 2 independent parts, one for each index of `rep`. The reference program is written for one: setup_inputs(seed, part) draws one part's arguments, and reference() takes and returns one part's arrays. A program takes and returns all parts, laid end to end along the dimension named above; an argument that names none is the same for every part. Nothing has to cross between parts.
Inputs may be any that keep to these rules, and one draw needn't show every extreme that they name: `adapter_of_row`: every row names a resident adapter. Of the rows owned by one index of ad, at most 128 have their slot on any one index of ad; in every draw there is one index of ad (which one is drawn) that receives exactly 128 rows from every index of ad. `adapter_resident_slot`: exactly 32 adapters are resident, each slot 0 to 31 holding one; all others are -1.
All inputs are finite; a program needn't handle non-finite values.
Results may differ from the reference program's by a relative error of at most 0.014.
Values may be sent and summed in bfloat16 or wider, within the bound.
No kernel may reach another device: no remote copies, remote signals or barrier semaphores. Data moves between devices by JAX's collectives and lax.ppermute only.
A program may use at most 64 MiB of HBM per device.

```python
import jax
import jax.numpy as jnp
from jax import lax

MODEL_WIDTH = 8192
ADAPTER_RANK = 64
ADAPTERS = 4096
SLOTS = 8
ROWS_DEV = 512
KEY_VALUE_COLUMNS = 2048
CAP = 128
GROUP_RESIDENTS = 32
ROWS = 2048
N_TP = 4


def routing(key):
    key_chosen, key_hot, key_owners = jax.random.split(key, 3)
    holders = GROUP_RESIDENTS // SLOTS
    chosen = jax.random.permutation(key_chosen, ADAPTERS)[:GROUP_RESIDENTS].astype(jnp.int32)
    adapter_resident_slot = jnp.full((ADAPTERS,), -1, jnp.int32).at[chosen].set(jnp.arange(GROUP_RESIDENTS, dtype=jnp.int32))
    hot_holder = jax.random.randint(key_hot, (), 0, holders, dtype=jnp.int32)

    def owner_rows(owner_key):
        key_order, key_local, key_shuffle = jax.random.split(owner_key, 3)
        order = jax.random.permutation(key_order, (holders - 1) * CAP)[:ROWS_DEV - CAP].astype(jnp.int32)
        others = order // CAP
        others = others + (others >= hot_holder).astype(jnp.int32)
        holder = jnp.concatenate([jnp.full((CAP,), hot_holder, jnp.int32), others])
        local_slot = jax.random.randint(key_local, (ROWS_DEV,), 0, SLOTS, dtype=jnp.int32)
        shuffle = jax.random.permutation(key_shuffle, ROWS_DEV)
        return (holder * SLOTS + local_slot)[shuffle]
    slots_used = jax.vmap(owner_rows)(jax.random.split(key_owners, holders)).reshape(-1)
    adapter_of_row = chosen[slots_used]
    return (adapter_of_row, adapter_resident_slot)


def draw_adapter_of_row(key, part):
    return routing(key)[0]


def draw_adapter_resident_slot(key, part):
    return routing(key)[1]


def strengthened(values, key, source, target, parts, factor):
    def block_of(dim):
        return (jnp.arange(values.shape[dim]) // (values.shape[dim] // parts)).reshape((-1,) + (1,) * (values.ndim - 1 - dim))

    near = jax.random.permutation(key, parts)[block_of(target)]
    second = (block_of(target) + parts // 2) % parts
    return jnp.where((block_of(source) == near) | (block_of(source) == second), factor * values, values)


def shard_levels(stream_key, shape, cuts, smallest, high):
    loudness, own = 1.0, jax.random.fold_in(stream_key, 6)
    for axis_at, blocks in cuts:
        heights = jnp.exp(jax.random.uniform(jax.random.fold_in(own, axis_at), (blocks,), jnp.float32, smallest / len(cuts), high / len(cuts)))
        loudness = loudness * jnp.repeat(heights, shape[axis_at] // blocks).reshape([-1 if axis == axis_at else 1 for axis in range(len(shape))])
    return loudness


def bell_draw(key, dims, width, most, cuts=(), kind=jnp.bfloat16):
    loudness = shard_levels(key, dims, cuts, -0.22, 0.18) if cuts else 1.0
    entries = jax.random.normal(key, dims, jnp.float32) * width * loudness
    return jnp.minimum(jnp.maximum(entries, -most), most).astype(kind)


def bell_draw_with(key, dims, width, bound, pieces, heavy, kind=jnp.bfloat16):
    array = width * jax.random.normal(key, dims, jnp.float32)
    if pieces:
        array = array * shard_levels(key, dims, pieces, -0.22, 0.18)
    return jnp.clip(strengthened(array, jax.random.fold_in(key, 3), *heavy), -bound, bound).astype(kind)


def setup_inputs(seed: int = 0, part: int = 0) -> dict:
    seeds = jax.random.split(jax.random.key(seed), 7)
    part_keys = jax.random.split(jax.random.fold_in(seeds[6], part), 7)
    return {
        "activations": bell_draw(part_keys[0], (ROWS, MODEL_WIDTH), 1.0, 6.0, ((0, 4), (1, 4))),
        "adapter_of_row": draw_adapter_of_row(jax.random.fold_in(jax.random.fold_in(seeds[6], part), 71), part),
        "adapter_resident_slot": draw_adapter_resident_slot(jax.random.fold_in(jax.random.fold_in(seeds[6], part), 71), part),
        "key_value_weight": bell_draw_with(seeds[3], (MODEL_WIDTH, KEY_VALUE_COLUMNS), MODEL_WIDTH ** -0.5, 0.09375, ((0, 4),), (0, 1, 4, 2.0)),
        "resident_down_factors": bell_draw(part_keys[4], (MODEL_WIDTH, GROUP_RESIDENTS * ADAPTER_RANK), MODEL_WIDTH ** -0.5, 0.0625, ((0, 4), (1, 4))),
        "resident_up_factors": bell_draw(part_keys[5], (GROUP_RESIDENTS * ADAPTER_RANK, KEY_VALUE_COLUMNS), ADAPTER_RANK ** -0.5, 0.75, ((0, 4), (1, 4))),
    }


def reference(activations, adapter_of_row, adapter_resident_slot, key_value_weight, resident_down_factors, resident_up_factors):
    row_total, input_features = activations.shape
    key_value_total = key_value_weight.shape[1]
    block_width = input_features // N_TP

    def add_block(running, block_index):
        offset = block_index * block_width
        x_block = lax.dynamic_slice_in_dim(activations, offset, block_width, 1)
        w_block = lax.dynamic_slice_in_dim(key_value_weight, offset, block_width, 0)
        partial_result = jnp.dot(x_block, w_block, preferred_element_type=jnp.float32).astype(jnp.bfloat16)
        partial_result = lax.optimization_barrier(partial_result).astype(jnp.float32)
        return running + partial_result, None

    base_sum, unused = lax.scan(add_block, jnp.zeros((row_total, key_value_total), jnp.float32), jnp.arange(N_TP, dtype=jnp.int32))

    slot_of_row = adapter_resident_slot[adapter_of_row].astype(jnp.int32)
    down_factor_table = resident_down_factors.reshape(input_features, GROUP_RESIDENTS, ADAPTER_RANK)
    up_factor_table = resident_up_factors.reshape(GROUP_RESIDENTS, ADAPTER_RANK, key_value_total)
    group_rows = min(64, row_total)
    device_groups = row_total // group_rows

    def adapter_block(carried_state, group_number):
        offset = group_number * group_rows
        x_group = lax.dynamic_slice_in_dim(activations, offset, group_rows, 0).astype(jnp.float32)
        slot_group = lax.dynamic_slice_in_dim(slot_of_row, offset, group_rows, 0)
        down_rows = jnp.take(down_factor_table, slot_group, axis=1).astype(jnp.float32)
        shrink = jnp.einsum("gd,dgk->gk", x_group, down_rows).astype(jnp.bfloat16)
        shrink = lax.optimization_barrier(shrink).astype(jnp.float32)
        up_rows = jnp.take(up_factor_table, slot_group, axis=0).astype(jnp.float32)
        row_updates = jnp.einsum("gk,gkv->gv", shrink, up_rows).astype(jnp.bfloat16)
        return carried_state, row_updates

    discarded_carry, row_updates = lax.scan(adapter_block, jnp.zeros((), jnp.int32), jnp.arange(device_groups, dtype=jnp.int32))
    row_updates = lax.optimization_barrier(row_updates.reshape(row_total, key_value_total)).astype(jnp.float32)
    return (base_sum + row_updates).astype(jnp.bfloat16)
```

```python
import functools

import jax
import jax.numpy as jnp
from jax import lax
from jax.experimental import pallas as pl
from jax.experimental.pallas import tpu as pltpu
from jax.sharding import PartitionSpec as P

ADAPTER_RANK = 64
LANES = 128
VMEM_BYTES = 32 * 1024 * 1024

bf16 = jnp.bfloat16
f32 = jnp.float32
i32 = jnp.int32


def params():
    return pltpu.CompilerParams(vmem_limit_bytes=VMEM_BYTES)


def cost(flops, nbytes):
    return pl.CostEstimate(flops=flops, bytes_accessed=nbytes, transcendentals=0)


def dot(a, b, contract=((1,), (0,))):
    return lax.dot_general(a, b, (contract, ((), ())), preferred_element_type=f32)


def iota(shape, dim):
    return lax.broadcasted_iota(i32, shape, dim)


def sort_body(slots, capacity, me_ref, ids_ref, table_ref, x_ref, place_ref, *outs):
    rows, features = x_ref.shape
    holders = len(outs)
    ids = ids_ref[...]
    table = table_ref[...].astype(f32).astype(bf16)
    low = (iota((LANES, rows), 0) == (ids & (LANES - 1))).astype(f32).astype(bf16)
    high = iota((table.shape[0], rows), 0) == lax.shift_right_logical(ids, 7)
    slot = jnp.sum(jnp.where(high, dot(table, low), 0.0), axis=0, keepdims=True).astype(i32)
    holder = lax.div(slot, slots)
    tag = (slot - holder * slots + 1).astype(f32)
    partner = holder ^ me_ref[0]
    mine = iota((max(8, holders), rows), 0) == partner
    earlier = (iota((rows, rows), 0) < iota((rows, rows), 1)).astype(f32).astype(bf16)
    before = dot(mine.astype(f32).astype(bf16), earlier)
    rank = jnp.sum(jnp.where(mine, before, 0.0), axis=0, keepdims=True).astype(i32)
    place = partner * capacity + rank
    place_ref[...] = jnp.broadcast_to(place, place_ref.shape)
    tags = jnp.broadcast_to(tag, (LANES, rows)).astype(bf16)
    x = x_ref[...]
    for j, out in enumerate(outs):
        pick = (iota((capacity, rows), 0) + j * capacity == place).astype(f32).astype(bf16)
        out[:, :features] = dot(pick, x).astype(bf16)
        out[:, features:] = dot(pick, tags, ((1,), (1,))).astype(bf16)


def sort_rows(me, ids, table, x, holders, slots, capacity):
    rows, features = x.shape
    out = jax.ShapeDtypeStruct((capacity, features + LANES), bf16)
    return pl.pallas_call(
        functools.partial(sort_body, slots, capacity),
        out_shape=[jax.ShapeDtypeStruct((8, rows), i32)] + [out] * holders,
        in_specs=[pl.BlockSpec(memory_space=pltpu.SMEM)] + [pl.BlockSpec(memory_space=pltpu.VMEM)] * 3,
        out_specs=[pl.BlockSpec(memory_space=pltpu.VMEM)] * (holders + 1),
        compiler_params=params(),
        cost_estimate=cost(2 * holders * capacity * rows * features, 4 * rows * features),
        name="sort_rows",
    )(me.reshape(1), ids.reshape(1, rows), table.reshape(-1, LANES), x)


def base_body(order_ref, x_ref, w_ref, out_ref):
    out_ref[...] = dot(x_ref[...], w_ref[...]).astype(bf16)


def base_blocks(order, x, weight, width, tile):
    rows, features = x.shape
    count = order.shape[0]
    tiles = width // tile
    return pl.pallas_call(
        base_body,
        out_shape=jax.ShapeDtypeStruct((count, rows, width), bf16),
        grid_spec=pltpu.PrefetchScalarGridSpec(
            num_scalar_prefetch=1,
            grid=(count, tiles),
            in_specs=[
                pl.BlockSpec((rows, features), lambda b, t, order: (0, 0)),
                pl.BlockSpec((features, tile), lambda b, t, order: (0, order[b] * tiles + t)),
            ],
            out_specs=pl.BlockSpec((None, rows, tile), lambda b, t, order: (b, 0, t)),
        ),
        compiler_params=params(),
        cost_estimate=cost(2 * count * rows * features * width, 2 * (rows + count * width) * features),
        name="base_blocks",
    )(order, x, weight)


def slot_mask(tag, group):
    lane = iota(tag.shape, 1)
    return tag == jnp.where(lane < ADAPTER_RANK, 2 * group + 1, 2 * group + 2).astype(f32)


def shrink_body(down_ref, *refs):
    parts, out = refs[:-1], refs[-1]
    features, width = down_ref.shape
    down = down_ref[...]
    capacity = parts[0].shape[0]
    half = len(parts) // 2
    sums = []
    for part in parts:
        full = dot(part[:, :features], down)
        tag = part[:, features:].astype(f32)
        total = jnp.zeros((capacity, LANES), f32)
        for group in range(width // LANES):
            total += jnp.where(slot_mask(tag, group), full[:, group * LANES:(group + 1) * LANES], 0.0)
        sums.append(total + pltpu.roll(total, ADAPTER_RANK, 1))
    first = iota((capacity, LANES), 1) < ADAPTER_RANK
    for k in range(half):
        out[k * capacity:(k + 1) * capacity, :] = jnp.where(first, sums[k], sums[k + half]).astype(bf16)


def shrink_partial(parts, down):
    features, width = down.shape
    capacity = parts[0].shape[0]
    total = len(parts) * capacity
    return pl.pallas_call(
        shrink_body,
        out_shape=jax.ShapeDtypeStruct((total // 2, LANES), bf16),
        compiler_params=params(),
        cost_estimate=cost(2 * total * features * width, 2 * features * (total + width)),
        name="shrink_partial",
    )(down, *parts)


def expand_body(count, one_ref, two_ref, up_ref, *refs):
    tags, outs = refs[:count], refs[count:]
    capacity = outs[0].shape[0]
    half = count // 2
    shrink = (one_ref[...].astype(f32) + two_ref[...].astype(f32)).astype(bf16).astype(f32)
    up = up_ref[...]
    first = iota((capacity, LANES), 1) < ADAPTER_RANK
    for k in range(count):
        rows = shrink[(k % half) * capacity:(k % half + 1) * capacity]
        turned = pltpu.roll(rows, ADAPTER_RANK, 1)
        rows = jnp.where(first, rows, turned) if k < half else jnp.where(first, turned, rows)
        tag = tags[k][...].astype(f32)
        spread = [
            jnp.where(slot_mask(tag, group), rows, 0.0).astype(bf16) for group in range(up.shape[0] // LANES)
        ]
        outs[k][...] = dot(jnp.concatenate(spread, axis=1), up).astype(bf16)


def expand(one, two, up, parts):
    capacity, width = parts[0].shape
    count = len(parts)
    tag_block = pl.BlockSpec((capacity, LANES), lambda i: (0, width // LANES - 1))
    whole = lambda a: pl.BlockSpec(a.shape, lambda i: (0, 0))
    columns = up.shape[1]
    return pl.pallas_call(
        functools.partial(expand_body, count),
        grid=(1,),
        out_shape=[jax.ShapeDtypeStruct((capacity, columns), bf16)] * count,
        in_specs=[whole(one), whole(two), whole(up)] + [tag_block] * count,
        out_specs=[pl.BlockSpec((capacity, columns), lambda i: (0, 0))] * count,
        compiler_params=params(),
        cost_estimate=cost(2 * count * capacity * up.size, 2 * (up.size + count * capacity * columns)),
        name="expand",
    )(one, two, up, *parts)


def finish_body(count, place_ref, *refs):
    deltas, sums, out = refs[:count], refs[count:-1], refs[-1]
    rows = out.shape[0]
    place = place_ref[0:1, :]
    capacity = deltas[0].shape[0]
    total = sums[0][...].astype(f32)
    for term in sums[1:]:
        total += term[...].astype(f32)
    own = jnp.zeros(out.shape, f32)
    for j, delta in enumerate(deltas):
        pick = (iota((capacity, rows), 0) + j * capacity == place).astype(f32).astype(bf16)
        own += dot(pick, delta[...], ((0,), (0,)))
    out[...] = (total + own).astype(bf16)


def finish(place, deltas, sums, own):
    rows, columns = own.shape[1:]
    count = len(deltas)
    return pl.pallas_call(
        functools.partial(finish_body, count),
        grid=(1,),
        out_shape=jax.ShapeDtypeStruct((rows, columns), bf16),
        in_specs=[pl.BlockSpec(place.shape, lambda i: (0, 0))]
        + [pl.BlockSpec(d.shape, lambda i: (0, 0)) for d in deltas]
        + [pl.BlockSpec((None, rows, columns), lambda i: (own.shape[0] - 1, 0, 0))]
        + [pl.BlockSpec((rows, columns), lambda i: (0, 0)) for s in sums],
        out_specs=pl.BlockSpec((rows, columns), lambda i: (0, 0)),
        compiler_params=params(),
        cost_estimate=cost(2 * rows * rows * columns, 12 * rows * columns),
        name="finish",
    )(place, *deltas, own, *sums)


def both(a, b):
    return (a.astype(f32) + b.astype(f32)).astype(bf16)


def swap(value, axis, bit):
    return lax.ppermute(value, axis, [(i, i ^ bit) for i in range(lax.axis_size(axis))])


ORDER = ((3, 2, 1, 0), (3, 2, 0, 1), (0, 1, 3, 2), (0, 1, 2, 3))
EDGE = [(0, 1), (3, 2)]
MIDDLE = [(1, 2), (2, 1)]


def base_terms(x, weight, width):
    if lax.axis_size("tp") != len(ORDER):
        full = dot(x, weight).astype(bf16)
        return [], lax.psum_scatter(full, "tp", scatter_dimension=1, tiled=True)[None]
    order = jnp.array(ORDER, i32)[lax.axis_index("tp")]
    tile = min(width, 256)
    first = base_blocks(order[:1], x, weight, width, tile)[0]
    rest = base_blocks(order[1:], x, weight, width, tile)
    edge0 = lax.ppermute(first, "tp", EDGE)
    edge1 = lax.ppermute(rest[0], "tp", EDGE)
    middle0 = lax.ppermute(both(first, edge0), "tp", MIDDLE)
    middle1 = lax.ppermute(both(rest[0], edge1), "tp", MIDDLE)
    last = swap(both(rest[1], middle0), "tp", 1)
    return [middle1, last], rest


def shards(x, ids, table, weight, down, up):
    holders = lax.axis_size("ad")
    rows = x.shape[0]
    capacity = rows // 4
    slots = up.shape[0] // ADAPTER_RANK
    place, *send = sort_rows(lax.axis_index("ad"), ids, table, x, holders, slots, capacity)
    parts = [send[0]] + [swap(send[j], "ad", j) for j in range(1, holders)]
    sums, own = base_terms(x, weight, up.shape[1])
    mine = shrink_partial(parts, down)
    bit = 1
    while bit < lax.axis_size("tp"):
        other = swap(mine, "tp", bit)
        bit *= 2
        if bit < lax.axis_size("tp"):
            mine = both(mine, other)
    deltas = expand(mine, other, up, parts)
    back = [deltas[0]] + [swap(deltas[j], "ad", j) for j in range(1, holders)]
    return finish(place, back, sums, own)


def solution(mesh):
    in_specs = (
        P(("rep", "ad"), "tp"),
        P(("rep", "ad")),
        P("rep"),
        P("tp", None),
        P(("rep", "tp"), "ad"),
        P(("rep", "ad"), "tp"),
    )
    out_specs = P(("rep", "ad"), "tp")
    return jax.shard_map(shards, mesh=mesh, in_specs=in_specs, out_specs=out_specs, check_vma=False)
```

```python
import functools

import jax
import jax.numpy as jnp
from jax import lax
from jax.experimental import pallas as pl
from jax.experimental.pallas import tpu as pltpu
from jax.sharding import PartitionSpec as P

ADAPTER_RANK = 64
LANES = 128
VMEM_BYTES = 32 * 1024 * 1024

bf16 = jnp.bfloat16
f32 = jnp.float32
i32 = jnp.int32


def params():
    return pltpu.CompilerParams(vmem_limit_bytes=VMEM_BYTES)


def cost(flops, nbytes):
    return pl.CostEstimate(flops=flops, bytes_accessed=nbytes, transcendentals=0)


def dot(a, b, contract=((1,), (0,))):
    return lax.dot_general(a, b, (contract, ((), ())), preferred_element_type=f32)


def in_hbm(a):
    return pltpu.with_memory_space_constraint(a, pltpu.HBM)


def iota(shape, dim):
    return lax.broadcasted_iota(i32, shape, dim)


def places(slots, capacity, holders, me, ids, table):
    rows = ids.shape[1]
    low = (iota((LANES, rows), 0) == (ids & (LANES - 1))).astype(f32).astype(bf16)
    high = iota((table.shape[0], rows), 0) == lax.shift_right_logical(ids, 7)
    found = dot(table.astype(f32).astype(bf16), low)
    slot = jnp.sum(jnp.where(high, found, 0.0), axis=0, keepdims=True).astype(i32)
    holder = lax.div(slot, slots)
    tag = (slot - holder * slots + 1).astype(f32)
    partner = holder ^ me
    mine = iota((max(8, holders), rows), 0) == partner
    earlier = (iota((rows, rows), 0) < iota((rows, rows), 1)).astype(f32).astype(bf16)
    before = dot(mine.astype(f32).astype(bf16), earlier)
    rank = jnp.sum(jnp.where(mine, before, 0.0), axis=0, keepdims=True).astype(i32)
    return partner * capacity + rank, tag


def head_body(slots, capacity, holders, block, me_ref, z_ref, ids_hbm, table_hbm, x_hbm, w_hbm, place_ref, *refs):
    outs = refs[:holders]
    if block:
        first_ref, x_buf, ids_buf, table_buf, x_sem, i_sem, w_buf, w_sem = refs[holders:]
    else:
        x_buf, ids_buf, table_buf, x_sem, i_sem = refs[holders:]
    rows, features = x_buf.shape
    chunks = x_sem.shape[0]
    step = features // chunks

    def x_copy(c):
        part = pl.ds(c * step, step)
        return pltpu.make_async_copy(x_hbm.at[:, part], x_buf.at[:, part], x_sem.at[c])

    small = [
        pltpu.make_async_copy(ids_hbm, ids_buf, i_sem.at[0]),
        pltpu.make_async_copy(table_hbm, table_buf, i_sem.at[1]),
    ]
    for copy in small:
        copy.start()
    for c in range(chunks):
        x_copy(c).start()
    if block:
        column = pl.multiple_of(jnp.where(z_ref[0] < 2, 3, 0) * block, block)
        w_copy = pltpu.make_async_copy(w_hbm.at[:, pl.ds(column, block)], w_buf, w_sem)
        w_copy.start()
    for copy in small:
        copy.wait()
    place, tag = places(slots, capacity, holders, me_ref[0], ids_buf[...], table_buf[...])
    place_ref[...] = jnp.broadcast_to(place, place_ref.shape)
    pick = (iota((holders * capacity, rows), 0) == place).astype(f32).astype(bf16)
    tags = dot(pick, jnp.broadcast_to(tag, (LANES, rows)).astype(bf16), ((1,), (1,))).astype(bf16)
    for j, out in enumerate(outs):
        out[:, features:] = tags[j * capacity:(j + 1) * capacity]
    for c in range(chunks):
        x_copy(c).wait()
        moved = dot(pick, x_buf[:, c * step:(c + 1) * step]).astype(bf16)
        for j, out in enumerate(outs):
            out[:, c * step:(c + 1) * step] = moved[j * capacity:(j + 1) * capacity]
    if block:
        w_copy.wait()
        first_ref[...] = dot(x_buf[...], w_buf[...]).astype(bf16)


def head(me, z, ids, table, x, weight, holders, slots, capacity, block):
    rows, features = x.shape
    chunks = max(1, features // 512)
    smem, vmem, hbm = (pl.BlockSpec(memory_space=m) for m in (pltpu.SMEM, pltpu.VMEM, pltpu.HBM))
    shapes = [jax.ShapeDtypeStruct((8, rows), i32)]
    shapes += [jax.ShapeDtypeStruct((capacity, features + LANES), bf16)] * holders
    ids = ids.reshape(1, rows)
    table = table.reshape(-1, LANES)
    scratch = [pltpu.VMEM((rows, features), bf16), pltpu.VMEM(ids.shape, i32), pltpu.VMEM(table.shape, i32)]
    scratch += [pltpu.SemaphoreType.DMA((chunks,)), pltpu.SemaphoreType.DMA((2,))]
    if block:
        shapes.append(jax.ShapeDtypeStruct((rows, block), bf16))
        scratch += [pltpu.VMEM((features, block), bf16), pltpu.SemaphoreType.DMA(())]
    return pl.pallas_call(
        functools.partial(head_body, slots, capacity, holders, block),
        out_shape=shapes,
        in_specs=[smem, smem, hbm, hbm, hbm, hbm],
        out_specs=[vmem] * len(shapes),
        scratch_shapes=scratch,
        compiler_params=params(),
        cost_estimate=cost(2 * (holders * capacity + block) * rows * features, 4 * rows * features),
        name="head",
    )(me.reshape(1), z.reshape(1), in_hbm(ids), in_hbm(table), in_hbm(x), in_hbm(weight))


def rest_body(z_ref, place_ref, x_ref, w_ref, second, third, own, unsort):
    z = z_ref[0]
    width = own.shape[1]
    x = x_ref[...]
    for block, out in ((jnp.where(z < 2, 2, 1), second), (z ^ 1, third), (z, own)):
        column = pl.multiple_of(block * width, width)
        out[...] = dot(x, w_ref[:, pl.ds(column, width)]).astype(bf16)
    unsort_matrix(place_ref, unsort)


def unsort_matrix(place_ref, unsort):
    rows, total = unsort.shape
    place = jnp.broadcast_to(place_ref[0:1, :].astype(f32), (LANES, rows)).T
    lane = iota((rows, LANES), 1).astype(f32)
    for k in range(total // LANES):
        unsort[:, k * LANES:(k + 1) * LANES] = (place == lane + float(k * LANES)).astype(f32).astype(bf16)


def rest(z, place, x, weight, width, total):
    rows, features = x.shape
    smem, vmem = (pl.BlockSpec(memory_space=m) for m in (pltpu.SMEM, pltpu.VMEM))
    return pl.pallas_call(
        rest_body,
        out_shape=[jax.ShapeDtypeStruct((rows, width), bf16)] * 3 + [jax.ShapeDtypeStruct((rows, total), bf16)],
        in_specs=[smem, vmem, vmem, vmem],
        out_specs=[vmem] * 4,
        compiler_params=params(),
        cost_estimate=cost(6 * rows * features * width, 2 * features * (rows + 4 * width)),
        name="rest",
    )(z.reshape(1), place, x, weight)


def unsort_only(place, total):
    return pl.pallas_call(
        unsort_matrix,
        out_shape=jax.ShapeDtypeStruct((place.shape[1], total), bf16),
        compiler_params=params(),
        name="unsort",
    )(place)


def slot_mask(tag, group):
    lane = iota(tag.shape, 1)
    return tag == jnp.where(lane < ADAPTER_RANK, 2 * group + 1, 2 * group + 2).astype(f32)


def shrink_body(down_ref, *refs):
    parts, out = refs[:-1], refs[-1]
    features, width = down_ref.shape
    capacity = parts[0].shape[0]
    half = capacity // 2
    first = iota((half, LANES), 1) < ADAPTER_RANK
    for k, part in enumerate(parts):
        full = dot(part[:, :features], down_ref[...])
        tag = part[:, features:].astype(f32)
        total = jnp.zeros((capacity, LANES), f32)
        for group in range(width // LANES):
            total += jnp.where(slot_mask(tag, group), full[:, group * LANES:(group + 1) * LANES], 0.0)
        total += pltpu.roll(total, ADAPTER_RANK, 1)
        out[k * half:(k + 1) * half, :] = jnp.where(first, total[:half], total[half:]).astype(bf16)


def shrink_partial(parts, down):
    features, width = down.shape
    capacity = parts[0].shape[0]
    total = len(parts) * capacity
    return pl.pallas_call(
        shrink_body,
        out_shape=jax.ShapeDtypeStruct((total // 2, LANES), bf16),
        compiler_params=params(),
        cost_estimate=cost(2 * total * features * width, 2 * features * (total + width)),
        name="shrink_partial",
    )(down, *parts)


def expand_body(count, one_ref, two_ref, up_ref, *refs):
    tags, outs = refs[:count], refs[count:]
    capacity = outs[0].shape[0]
    half = capacity // 2
    up = up_ref[...]
    first = iota((half, LANES), 1) < ADAPTER_RANK
    for k in range(count):
        part = pl.ds(k * half, half)
        shrink = (one_ref[part, :].astype(f32) + two_ref[part, :].astype(f32)).astype(bf16).astype(f32)
        turned = pltpu.roll(shrink, ADAPTER_RANK, 1)
        rows = jnp.concatenate([jnp.where(first, shrink, turned), jnp.where(first, turned, shrink)], axis=0)
        tag = tags[k][...].astype(f32)
        spread = [
            jnp.where(slot_mask(tag, group), rows, 0.0).astype(bf16) for group in range(up.shape[0] // LANES)
        ]
        outs[k][...] = dot(jnp.concatenate(spread, axis=1), up).astype(bf16)


def expand(one, two, up, parts):
    capacity, width = parts[0].shape
    count = len(parts)
    tag_block = pl.BlockSpec((capacity, LANES), lambda i: (0, width // LANES - 1))
    whole = lambda a: pl.BlockSpec(a.shape, lambda i: (0, 0))
    columns = up.shape[1]
    return pl.pallas_call(
        functools.partial(expand_body, count),
        grid=(1,),
        out_shape=[jax.ShapeDtypeStruct((capacity, columns), bf16)] * count,
        in_specs=[whole(one), whole(two), whole(up)] + [tag_block] * count,
        out_specs=[pl.BlockSpec((capacity, columns), lambda i: (0, 0))] * count,
        compiler_params=params(),
        cost_estimate=cost(2 * count * capacity * up.size, 2 * (up.size + count * capacity * columns)),
        name="expand",
    )(one, two, up, *parts)


def finish_body(count, unsort_ref, *refs):
    deltas, sums, out = refs[:count], refs[count:-1], refs[-1]
    capacity = deltas[0].shape[0]
    total = sums[0][...].astype(f32)
    for term in sums[1:]:
        total += term[...].astype(f32)
    own = dot(unsort_ref[...], jnp.concatenate([d[...] for d in deltas], axis=0))
    out[...] = (total + own).astype(bf16)


def finish(unsort, deltas, sums):
    rows, columns = sums[0].shape
    return pl.pallas_call(
        functools.partial(finish_body, len(deltas)),
        out_shape=jax.ShapeDtypeStruct((rows, columns), bf16),
        compiler_params=params(),
        cost_estimate=cost(2 * rows * unsort.shape[1] * columns, 12 * rows * columns),
        name="finish",
    )(unsort, *deltas, *sums)


def both(a, b):
    return (a.astype(f32) + b.astype(f32)).astype(bf16)


def after(value, *others):
    return lax.optimization_barrier((value,) + others)[0]


def swap(value, axis, bit):
    return lax.ppermute(value, axis, [(i, i ^ bit) for i in range(lax.axis_size(axis))])


EDGE = [(0, 1), (3, 2)]
MIDDLE = [(1, 2), (2, 1)]
OUTER = [(1, 0), (2, 3)]


def tp_sums(mine):
    bit = 1
    while True:
        other = swap(mine, "tp", bit)
        bit *= 2
        if bit >= lax.axis_size("tp"):
            return mine, other
        mine = both(mine, other)


def shards(x, ids, table, weight, down, up):
    holders = lax.axis_size("ad")
    rows = x.shape[0]
    capacity = rows // 4
    slots = up.shape[0] // ADAPTER_RANK
    width = up.shape[1]
    me, z = lax.axis_index("ad"), lax.axis_index("tp")
    line = lax.axis_size("tp") == 4
    place, *send = head(me, z, ids, table, x, weight, holders, slots, capacity, width if line else 0)
    total = holders * capacity
    if line:
        first = send.pop()
        edge0 = lax.ppermute(first, "tp", EDGE)
        parts = [send[0]] + [swap(send[j], "ad", j) for j in range(1, holders)]
        second, third, own, unsort = rest(z, place, x, weight, width, total)
        edge1 = lax.ppermute(second, "tp", EDGE)
        inner = both(first, edge0)
        middle0 = lax.ppermute(inner, "tp", MIDDLE)
        parts[2] = after(parts[2], inner)
    else:
        parts = [send[0]] + [swap(send[j], "ad", j) for j in range(1, holders)]
        unsort = unsort_only(place, total)
        full = dot(x, weight).astype(bf16)
        sums = [lax.psum_scatter(full, "tp", scatter_dimension=1, tiled=True)]
    early, late = parts[:-1], parts[-1:]
    one, two = tp_sums(shrink_partial(early, down))
    deltas = expand(one, two, up, early)
    back = [deltas[0]] + [swap(deltas[j], "ad", j) for j in range(1, holders - 1)]
    if line:
        edge2 = lax.ppermute(after(third, two), "tp", EDGE)
        middle1 = lax.ppermute(both(second, edge1), "tp", MIDDLE)
        outer = lax.ppermute(both(after(third, parts[-1]), middle0), "tp", OUTER)
        sums = [own, middle1, edge2, outer]
    late = [after(late[0], *deltas)]
    one, two = tp_sums(shrink_partial(late, down))
    back.append(swap(expand(one, two, up, late)[0], "ad", holders - 1))
    return finish(unsort, back, sums)


def solution(mesh):
    in_specs = (
        P(("rep", "ad"), "tp"),
        P(("rep", "ad")),
        P("rep"),
        P("tp", None),
        P(("rep", "tp"), "ad"),
        P(("rep", "ad"), "tp"),
    )
    out_specs = P(("rep", "ad"), "tp")
    return jax.shard_map(shards, mesh=mesh, in_specs=in_specs, out_specs=out_specs, check_vma=False)
```

```python
import functools

import jax
import jax.numpy as jnp
from jax import lax
from jax.experimental import pallas as pl
from jax.experimental.pallas import tpu as pltpu
from jax.sharding import PartitionSpec as P

ADAPTER_RANK = 64
LANES = 128
VMEM_BYTES = 32 * 1024 * 1024

bf16 = jnp.bfloat16
f32 = jnp.float32
i32 = jnp.int32


def params():
    return pltpu.CompilerParams(vmem_limit_bytes=VMEM_BYTES)


def cost(flops, nbytes):
    return pl.CostEstimate(flops=flops, bytes_accessed=nbytes, transcendentals=0)


def dot(a, b, contract=((1,), (0,))):
    return lax.dot_general(a, b, (contract, ((), ())), preferred_element_type=f32)


def in_hbm(a):
    return pltpu.with_memory_space_constraint(a, pltpu.HBM)


def iota(shape, dim):
    return lax.broadcasted_iota(i32, shape, dim)


def places(slots, capacity, holders, me, ids, table):
    rows = ids.shape[1]
    low = (iota((LANES, rows), 0) == (ids & (LANES - 1))).astype(f32).astype(bf16)
    high = iota((table.shape[0], rows), 0) == lax.shift_right_logical(ids, 7)
    found = dot(table.astype(f32).astype(bf16), low)
    slot = jnp.sum(jnp.where(high, found, 0.0), axis=0, keepdims=True).astype(i32)
    holder = lax.div(slot, slots)
    tag = (slot - holder * slots + 1).astype(f32)
    partner = holder ^ me
    mine = iota((max(8, holders), rows), 0) == partner
    earlier = (iota((rows, rows), 0) < iota((rows, rows), 1)).astype(f32).astype(bf16)
    before = dot(mine.astype(f32).astype(bf16), earlier)
    rank = jnp.sum(jnp.where(mine, before, 0.0), axis=0, keepdims=True).astype(i32)
    return partner * capacity + rank, tag


def sort_body(slots, capacity, holders, me_ref, ids_hbm, table_hbm, x_hbm, place_ref, *refs):
    outs, (ids_buf, table_buf, x_buf, small_sem, x_sem) = refs[:holders], refs[holders:]
    rows, features = x_buf.shape
    chunks = x_sem.shape[0]
    step = features // chunks
    small = [
        pltpu.make_async_copy(ids_hbm, ids_buf, small_sem.at[0]),
        pltpu.make_async_copy(table_hbm, table_buf, small_sem.at[1]),
    ]
    copies = []
    for c in range(chunks):
        part = pl.ds(c * step, step)
        copies.append(pltpu.make_async_copy(x_hbm.at[:, part], x_buf.at[:, part], x_sem.at[c]))
    for copy in small + copies:
        copy.start()
    for copy in small:
        copy.wait()
    place, tag = places(slots, capacity, holders, me_ref[0], ids_buf[...], table_buf[...])
    place_ref[...] = jnp.broadcast_to(place, place_ref.shape)
    pick = (iota((holders * capacity, rows), 0) == place).astype(f32).astype(bf16)
    tags = dot(pick, jnp.broadcast_to(tag, (LANES, rows)).astype(bf16), ((1,), (1,))).astype(bf16)
    for j, out in enumerate(outs):
        out[:, features:] = tags[j * capacity:(j + 1) * capacity]
    for c in range(chunks):
        copies[c].wait()
        moved = dot(pick, x_buf[:, c * step:(c + 1) * step]).astype(bf16)
        for j, out in enumerate(outs):
            out[:, c * step:(c + 1) * step] = moved[j * capacity:(j + 1) * capacity]


def sort_rows(me, ids, table, x, holders, slots, capacity):
    rows, features = x.shape
    ids, table = ids.reshape(1, rows), table.reshape(-1, LANES)
    chunks = max(1, features // 512)
    smem, vmem, hbm = (pl.BlockSpec(memory_space=m) for m in (pltpu.SMEM, pltpu.VMEM, pltpu.HBM))
    shapes = [jax.ShapeDtypeStruct((8, rows), i32)]
    shapes += [jax.ShapeDtypeStruct((capacity, features + LANES), bf16)] * holders
    return pl.pallas_call(
        functools.partial(sort_body, slots, capacity, holders),
        out_shape=shapes,
        in_specs=[smem, hbm, hbm, hbm],
        out_specs=[vmem] * len(shapes),
        scratch_shapes=[
            pltpu.VMEM(ids.shape, i32),
            pltpu.VMEM(table.shape, i32),
            pltpu.VMEM((rows, features), bf16),
            pltpu.SemaphoreType.DMA((2,)),
            pltpu.SemaphoreType.DMA((chunks,)),
        ],
        compiler_params=params(),
        cost_estimate=cost(2 * holders * capacity * rows * features, 4 * rows * features),
        name="sort_rows",
    )(me.reshape(1), in_hbm(ids), in_hbm(table), in_hbm(x))


def first_body(z_ref, x_ref, w_hbm, out, w_buf, sem):
    features, width = w_buf.shape
    chunks = sem.shape[0]
    step = features // chunks
    column = pl.multiple_of(jnp.where(z_ref[0] < 2, 3, 0) * width, width)
    copies = []
    for c in range(chunks):
        part = pl.ds(c * step, step)
        copies.append(pltpu.make_async_copy(w_hbm.at[part, pl.ds(column, width)], w_buf.at[part, :], sem.at[c]))
        copies[c].start()
    total = None
    for c in range(chunks):
        copies[c].wait()
        term = dot(x_ref[:, c * step:(c + 1) * step], w_buf[c * step:(c + 1) * step, :])
        total = term if total is None else total + term
    out[...] = total.astype(bf16)


def first_block(z, x, weight, width):
    rows, features = x.shape
    chunks = 4
    smem, vmem, hbm = (pl.BlockSpec(memory_space=m) for m in (pltpu.SMEM, pltpu.VMEM, pltpu.HBM))
    return pl.pallas_call(
        first_body,
        out_shape=jax.ShapeDtypeStruct((rows, width), bf16),
        in_specs=[smem, vmem, hbm],
        out_specs=vmem,
        scratch_shapes=[pltpu.VMEM((features, width), bf16), pltpu.SemaphoreType.DMA((chunks,))],
        compiler_params=params(),
        cost_estimate=cost(2 * rows * features * width, 2 * features * (rows + width)),
        name="first_block",
    )(z.reshape(1), x, in_hbm(weight))


def rest_body(z_ref, place_ref, x_ref, w_hbm, *refs):
    second, third, own, unsort, w_buf, sem = refs
    z = z_ref[0]
    width = own.shape[1]
    blocks = (jnp.where(z < 2, 2, 1), z ^ 1, z)
    copies = []
    for k, block in enumerate(blocks):
        column = pl.multiple_of(block * width, width)
        copies.append(pltpu.make_async_copy(w_hbm.at[:, pl.ds(column, width)], w_buf.at[k], sem.at[k]))
        copies[k].start()
    unsort_matrix(place_ref, unsort)
    x = x_ref[...]
    for k, out in enumerate((second, third, own)):
        copies[k].wait()
        out[...] = dot(x, w_buf[k]).astype(bf16)


def unsort_matrix(place_ref, unsort):
    rows, total = unsort.shape
    place = jnp.broadcast_to(place_ref[0:1, :].astype(f32), (LANES, rows)).T
    lane = iota((rows, LANES), 1).astype(f32)
    for k in range(total // LANES):
        unsort[:, k * LANES:(k + 1) * LANES] = (place == lane + float(k * LANES)).astype(f32).astype(bf16)


def rest(z, place, x, weight, width, total):
    rows, features = x.shape
    smem, vmem, hbm = (pl.BlockSpec(memory_space=m) for m in (pltpu.SMEM, pltpu.VMEM, pltpu.HBM))
    shapes = [jax.ShapeDtypeStruct((rows, width), bf16)] * 3 + [jax.ShapeDtypeStruct((rows, total), bf16)]
    return pl.pallas_call(
        rest_body,
        out_shape=shapes,
        in_specs=[smem, vmem, vmem, hbm],
        out_specs=[vmem] * len(shapes),
        scratch_shapes=[pltpu.VMEM((3, features, width), bf16), pltpu.SemaphoreType.DMA((3,))],
        compiler_params=params(),
        cost_estimate=cost(6 * rows * features * width, 2 * features * (rows + 4 * width)),
        name="rest",
    )(z.reshape(1), place, x, in_hbm(weight))


def unsort_only(place, total):
    return pl.pallas_call(
        unsort_matrix,
        out_shape=jax.ShapeDtypeStruct((place.shape[1], total), bf16),
        compiler_params=params(),
        name="unsort",
    )(place)


def slot_mask(tag, group):
    lane = iota(tag.shape, 1)
    return tag == jnp.where(lane < ADAPTER_RANK, 2 * group + 1, 2 * group + 2).astype(f32)


def shrink_body(kept, down_ref, *refs):
    parts, out = refs[1 if kept else 0:-1], refs[-1]
    features, width = down_ref.shape
    capacity = parts[0].shape[0]
    half = capacity // 2
    first = iota((half, LANES), 1) < ADAPTER_RANK
    if kept:
        out[:kept, :] = refs[0][...]
    for k, part in enumerate(parts):
        full = dot(part[:, :features], down_ref[...])
        tag = part[:, features:].astype(f32)
        total = jnp.zeros((capacity, LANES), f32)
        for group in range(width // LANES):
            total += jnp.where(slot_mask(tag, group), full[:, group * LANES:(group + 1) * LANES], 0.0)
        total += pltpu.roll(total, ADAPTER_RANK, 1)
        spot = slice(kept + k * half, kept + (k + 1) * half)
        out[spot, :] = jnp.where(first, total[:half], total[half:]).astype(bf16)


def shrink_partial(down, parts, done=()):
    features, width = down.shape
    capacity = parts[0].shape[0]
    total = len(parts) * capacity
    kept = sum(d.shape[0] for d in done)
    return pl.pallas_call(
        functools.partial(shrink_body, kept),
        out_shape=jax.ShapeDtypeStruct((kept + total // 2, LANES), bf16),
        compiler_params=params(),
        cost_estimate=cost(2 * total * features * width, 2 * features * (total + width)),
        name="shrink_partial",
    )(down, *done, *parts)


def expand_body(count, one_ref, two_ref, up_ref, *refs):
    tags, outs = refs[:count], refs[count:]
    capacity = outs[0].shape[0]
    half = capacity // 2
    up = up_ref[...]
    first = iota((half, LANES), 1) < ADAPTER_RANK
    for k in range(count):
        part = pl.ds(k * half, half)
        shrink = (one_ref[part, :].astype(f32) + two_ref[part, :].astype(f32)).astype(bf16).astype(f32)
        turned = pltpu.roll(shrink, ADAPTER_RANK, 1)
        rows = jnp.concatenate([jnp.where(first, shrink, turned), jnp.where(first, turned, shrink)], axis=0)
        tag = tags[k][...].astype(f32)
        spread = [
            jnp.where(slot_mask(tag, group), rows, 0.0).astype(bf16) for group in range(up.shape[0] // LANES)
        ]
        outs[k][...] = dot(jnp.concatenate(spread, axis=1), up).astype(bf16)


def expand(one, two, up, parts):
    capacity, width = parts[0].shape
    count = len(parts)
    tag_block = pl.BlockSpec((capacity, LANES), lambda i: (0, width // LANES - 1))
    whole = lambda a: pl.BlockSpec(a.shape, lambda i: (0, 0))
    columns = up.shape[1]
    return pl.pallas_call(
        functools.partial(expand_body, count),
        grid=(1,),
        out_shape=[jax.ShapeDtypeStruct((capacity, columns), bf16)] * count,
        in_specs=[whole(one), whole(two), whole(up)] + [tag_block] * count,
        out_specs=[pl.BlockSpec((capacity, columns), lambda i: (0, 0))] * count,
        compiler_params=params(),
        cost_estimate=cost(2 * count * capacity * up.size, 2 * (up.size + count * capacity * columns)),
        name="expand",
    )(one, two, up, *parts)


def finish_body(count, unsort_ref, *refs):
    deltas, sums, out = refs[:count], refs[count:-1], refs[-1]
    base = sums[0][...].astype(f32)
    for term in sums[1:]:
        base += term[...].astype(f32)
    out[...] = (base + dot(unsort_ref[...], jnp.concatenate([d[...] for d in deltas], axis=0))).astype(bf16)


def finish(unsort, deltas, sums):
    rows, columns = sums[0].shape
    return pl.pallas_call(
        functools.partial(finish_body, len(deltas)),
        out_shape=jax.ShapeDtypeStruct((rows, columns), bf16),
        compiler_params=params(),
        cost_estimate=cost(2 * rows * unsort.shape[1] * columns, 12 * rows * columns),
        name="finish",
    )(unsort, *deltas, *sums)


def both(a, b):
    return (a.astype(f32) + b.astype(f32)).astype(bf16)


def after(value, *others):
    return lax.optimization_barrier((value,) + others)[0]


def swap(value, axis, bit):
    return lax.ppermute(value, axis, [(i, i ^ bit) for i in range(lax.axis_size(axis))])


EDGE = [(0, 1), (3, 2)]
MIDDLE = [(1, 2), (2, 1)]


def tp_sums(mine, *before):
    sums, bit = [mine], 1
    while True:
        other = swap(sums[-1], "tp", bit)
        bit *= 2
        if bit >= lax.axis_size("tp"):
            return sums, other
        sums.append(both(after(sums[-1], *before), other))


def shards(x, ids, table, weight, down, up):
    holders = lax.axis_size("ad")
    capacity = x.shape[0] // 4
    slots = up.shape[0] // ADAPTER_RANK
    width = up.shape[1]
    total = holders * capacity
    me, z = lax.axis_index("ad"), lax.axis_index("tp")
    place, *send = sort_rows(me, ids, table, x, holders, slots, capacity)
    parts = [send[0]] + [swap(send[j], "ad", j) for j in range(1, holders)]
    if lax.axis_size("tp") == 4:
        x = after(x, place)
        first = first_block(z, x, weight, width)
        edge0 = lax.ppermute(first, "tp", EDGE)
        second, third, own, unsort = rest(z, after(place, first), x, weight, width, total)
        edge1 = lax.ppermute(second, "tp", EDGE)
        early = shrink_partial(down, parts[:-1])
        inner0 = both(after(first, early), edge0)
        middle0 = lax.ppermute(inner0, "tp", MIDDLE)
        mine = shrink_partial(down, [after(parts[-1], inner0)], [early])
        inner1, inner2 = both(second, edge1), both(third, middle0)
        steps, other = tp_sums(mine, inner1, inner2)
        middle1 = lax.ppermute(after(inner1, steps[-1]), "tp", MIDDLE)
        last = swap(after(inner2, other), "tp", 1)
        sums = [own, middle1, last]
    else:
        unsort = unsort_only(place, total)
        full = dot(x, weight).astype(bf16)
        sums = [lax.psum_scatter(full, "tp", scatter_dimension=1, tiled=True)]
        steps, other = tp_sums(shrink_partial(down, parts))
    deltas = expand(steps[-1], other, up, parts)
    back = [deltas[0]] + [swap(deltas[j], "ad", j) for j in range(1, holders)]
    return finish(unsort, back, sums)


def solution(mesh):
    in_specs = (
        P(("rep", "ad"), "tp"),
        P(("rep", "ad")),
        P("rep"),
        P("tp", None),
        P(("rep", "tp"), "ad"),
        P(("rep", "ad"), "tp"),
    )
    out_specs = P(("rep", "ad"), "tp")
    return jax.shard_map(shards, mesh=mesh, in_specs=in_specs, out_specs=out_specs, check_vma=False)
```

```python
import functools

import jax
import jax.numpy as jnp
from jax import lax
from jax.experimental import pallas as pl
from jax.experimental.pallas import tpu as pltpu
from jax.sharding import PartitionSpec as P

ADAPTER_RANK = 64
LANES = 128
VMEM_BYTES = 32 * 1024 * 1024

bf16 = jnp.bfloat16
f32 = jnp.float32
i32 = jnp.int32


def params():
    return pltpu.CompilerParams(vmem_limit_bytes=VMEM_BYTES)


def cost(flops, nbytes):
    return pl.CostEstimate(flops=flops, bytes_accessed=nbytes, transcendentals=0)


def dot(a, b, contract=((1,), (0,))):
    return lax.dot_general(a, b, (contract, ((), ())), preferred_element_type=f32)


def in_hbm(a):
    return pltpu.with_memory_space_constraint(a, pltpu.HBM)


def iota(shape, dim):
    return lax.broadcasted_iota(i32, shape, dim)


def places(slots, capacity, holders, me, ids, table, earlier):
    rows = ids.shape[1]
    low = (iota((LANES, rows), 0) == (ids & (LANES - 1))).astype(f32).astype(bf16)
    high = iota((table.shape[0], rows), 0) == lax.shift_right_logical(ids, 7)
    found = dot(table.astype(f32).astype(bf16), low)
    slot = jnp.sum(jnp.where(high, found, 0.0), axis=0, keepdims=True).astype(i32)
    holder = lax.div(slot, slots)
    tag = (slot - holder * slots + 1).astype(f32)
    partner = holder ^ me
    mine = iota((max(8, holders), rows), 0) == partner
    before = dot(mine.astype(f32).astype(bf16), earlier)
    rank = jnp.sum(jnp.where(mine, before, 0.0), axis=0, keepdims=True).astype(i32)
    return partner * capacity + rank, tag


def sort_body(slots, capacity, holders, me_ref, z_ref, ids_hbm, table_hbm, x_hbm, w_hbm, place_ref, *refs):
    outs, (x_buf, w_buf, ids_buf, table_buf, small_sem, x_sem, w_sem) = refs[:holders], refs[holders:]
    rows, features = x_buf.shape
    width = w_buf.shape[1]
    chunks = x_sem.shape[0]
    step = features // chunks
    small = [
        pltpu.make_async_copy(ids_hbm, ids_buf, small_sem.at[0]),
        pltpu.make_async_copy(table_hbm, table_buf, small_sem.at[1]),
    ]
    copies = []
    for c in range(chunks):
        part = pl.ds(c * step, step)
        copies.append(pltpu.make_async_copy(x_hbm.at[:, part], x_buf.at[:, part], x_sem.at[c]))
    column = pl.multiple_of(jnp.where(z_ref[0] < 2, 3, 0) * width, width)
    w_copy = pltpu.make_async_copy(w_hbm.at[:, pl.ds(column, width)], w_buf, w_sem)
    for copy in small + copies + [w_copy]:
        copy.start()
    earlier = (iota((rows, rows), 0) < iota((rows, rows), 1)).astype(f32).astype(bf16)
    for copy in small:
        copy.wait()
    place, tag = places(slots, capacity, holders, me_ref[0], ids_buf[...], table_buf[...], earlier)
    place_ref[...] = jnp.broadcast_to(place, place_ref.shape)
    pick = (iota((holders * capacity, rows), 0) == place).astype(f32).astype(bf16)
    tags = dot(pick, jnp.broadcast_to(tag, (LANES, rows)).astype(bf16), ((1,), (1,))).astype(bf16)
    for j, out in enumerate(outs):
        out[:, features:] = tags[j * capacity:(j + 1) * capacity]
    for c in range(chunks):
        copies[c].wait()
        moved = dot(pick, x_buf[:, c * step:(c + 1) * step]).astype(bf16)
        for j, out in enumerate(outs):
            out[:, c * step:(c + 1) * step] = moved[j * capacity:(j + 1) * capacity]
    w_copy.wait()


def sort_rows(me, z, ids, table, x, weight, holders, slots, capacity, width):
    rows, features = x.shape
    ids, table = ids.reshape(1, rows), table.reshape(-1, LANES)
    chunks = max(1, features // 512)
    smem, vmem, hbm = (pl.BlockSpec(memory_space=m) for m in (pltpu.SMEM, pltpu.VMEM, pltpu.HBM))
    shapes = [jax.ShapeDtypeStruct((8, rows), i32)]
    shapes += [jax.ShapeDtypeStruct((capacity, features + LANES), bf16)] * holders
    shapes += [jax.ShapeDtypeStruct((rows, features), bf16), jax.ShapeDtypeStruct((features, width), bf16)]
    return pl.pallas_call(
        functools.partial(sort_body, slots, capacity, holders),
        out_shape=shapes,
        in_specs=[smem, smem, hbm, hbm, hbm, hbm],
        out_specs=[vmem] * len(shapes),
        scratch_shapes=[
            pltpu.VMEM(ids.shape, i32),
            pltpu.VMEM(table.shape, i32),
            pltpu.SemaphoreType.DMA((2,)),
            pltpu.SemaphoreType.DMA((chunks,)),
            pltpu.SemaphoreType.DMA(()),
        ],
        compiler_params=params(),
        cost_estimate=cost(2 * holders * capacity * rows * features, 4 * rows * features),
        name="sort_rows",
    )(me.reshape(1), z.reshape(1), in_hbm(ids), in_hbm(table), in_hbm(x), in_hbm(weight))


def first_body(x_ref, w_ref, out):
    out[...] = dot(x_ref[...], w_ref[...]).astype(bf16)


def first_block(x, w):
    (rows, features), width = x.shape, w.shape[1]
    return pl.pallas_call(
        first_body,
        out_shape=jax.ShapeDtypeStruct((rows, width), bf16),
        compiler_params=params(),
        cost_estimate=cost(2 * rows * features * width, 2 * features * (rows + width)),
        name="first_block",
    )(x, w)


def rest_body(z_ref, place_ref, x_ref, w_hbm, *refs):
    second, third, own, unsort, w_buf, sem = refs
    z = z_ref[0]
    width = own.shape[1]
    blocks = (jnp.where(z < 2, 2, 1), z ^ 1, z)
    copies = []
    for k, block in enumerate(blocks):
        column = pl.multiple_of(block * width, width)
        copies.append(pltpu.make_async_copy(w_hbm.at[:, pl.ds(column, width)], w_buf.at[k], sem.at[k]))
        copies[k].start()
    unsort_matrix(place_ref, unsort)
    x = x_ref[...]
    for k, out in enumerate((second, third, own)):
        copies[k].wait()
        out[...] = dot(x, w_buf[k]).astype(bf16)


def unsort_matrix(place_ref, unsort):
    rows, total = unsort.shape
    place = jnp.broadcast_to(place_ref[0:1, :].astype(f32), (LANES, rows)).T
    lane = iota((rows, LANES), 1).astype(f32)
    for k in range(total // LANES):
        unsort[:, k * LANES:(k + 1) * LANES] = (place == lane + float(k * LANES)).astype(f32).astype(bf16)


def rest(z, place, x, weight, width, total):
    rows, features = x.shape
    smem, vmem, hbm = (pl.BlockSpec(memory_space=m) for m in (pltpu.SMEM, pltpu.VMEM, pltpu.HBM))
    shapes = [jax.ShapeDtypeStruct((rows, width), bf16)] * 3 + [jax.ShapeDtypeStruct((rows, total), bf16)]
    return pl.pallas_call(
        rest_body,
        out_shape=shapes,
        in_specs=[smem, vmem, vmem, hbm],
        out_specs=[vmem] * len(shapes),
        scratch_shapes=[pltpu.VMEM((3, features, width), bf16), pltpu.SemaphoreType.DMA((3,))],
        compiler_params=params(),
        cost_estimate=cost(6 * rows * features * width, 2 * features * (rows + 4 * width)),
        name="rest",
    )(z.reshape(1), place, x, in_hbm(weight))


def unsort_only(place, total):
    return pl.pallas_call(
        unsort_matrix,
        out_shape=jax.ShapeDtypeStruct((place.shape[1], total), bf16),
        compiler_params=params(),
        name="unsort",
    )(place)


def slot_mask(tag, group):
    lane = iota(tag.shape, 1)
    return tag == jnp.where(lane < ADAPTER_RANK, 2 * group + 1, 2 * group + 2).astype(f32)


def shrink_body(kept, down_ref, *refs):
    parts, out = refs[1 if kept else 0:-1], refs[-1]
    features, width = down_ref.shape
    capacity = parts[0].shape[0]
    half = capacity // 2
    first = iota((half, LANES), 1) < ADAPTER_RANK
    if kept:
        out[:kept, :] = refs[0][...]
    for k, part in enumerate(parts):
        full = dot(part[:, :features], down_ref[...])
        tag = part[:, features:].astype(f32)
        total = jnp.zeros((capacity, LANES), f32)
        for group in range(width // LANES):
            total += jnp.where(slot_mask(tag, group), full[:, group * LANES:(group + 1) * LANES], 0.0)
        total += pltpu.roll(total, ADAPTER_RANK, 1)
        spot = slice(kept + k * half, kept + (k + 1) * half)
        out[spot, :] = jnp.where(first, total[:half], total[half:]).astype(bf16)


def shrink_partial(down, parts, done=()):
    features, width = down.shape
    capacity = parts[0].shape[0]
    total = len(parts) * capacity
    kept = sum(d.shape[0] for d in done)
    return pl.pallas_call(
        functools.partial(shrink_body, kept),
        out_shape=jax.ShapeDtypeStruct((kept + total // 2, LANES), bf16),
        compiler_params=params(),
        cost_estimate=cost(2 * total * features * width, 2 * features * (total + width)),
        name="shrink_partial",
    )(down, *done, *parts)


def expand_body(count, one_ref, two_ref, up_ref, *refs):
    tags, outs = refs[:count], refs[count:]
    capacity = outs[0].shape[0]
    half = capacity // 2
    up = up_ref[...]
    first = iota((half, LANES), 1) < ADAPTER_RANK
    for k in range(count):
        part = pl.ds(k * half, half)
        shrink = (one_ref[part, :].astype(f32) + two_ref[part, :].astype(f32)).astype(bf16).astype(f32)
        turned = pltpu.roll(shrink, ADAPTER_RANK, 1)
        rows = jnp.concatenate([jnp.where(first, shrink, turned), jnp.where(first, turned, shrink)], axis=0)
        tag = tags[k][...].astype(f32)
        spread = [
            jnp.where(slot_mask(tag, group), rows, 0.0).astype(bf16) for group in range(up.shape[0] // LANES)
        ]
        outs[k][...] = dot(jnp.concatenate(spread, axis=1), up).astype(bf16)


def expand(one, two, up, parts):
    capacity, width = parts[0].shape
    count = len(parts)
    tag_block = pl.BlockSpec((capacity, LANES), lambda i: (0, width // LANES - 1))
    whole = lambda a: pl.BlockSpec(a.shape, lambda i: (0, 0))
    columns = up.shape[1]
    return pl.pallas_call(
        functools.partial(expand_body, count),
        grid=(1,),
        out_shape=[jax.ShapeDtypeStruct((capacity, columns), bf16)] * count,
        in_specs=[whole(one), whole(two), whole(up)] + [tag_block] * count,
        out_specs=[pl.BlockSpec((capacity, columns), lambda i: (0, 0))] * count,
        compiler_params=params(),
        cost_estimate=cost(80 * count * capacity * up.size, 80 * (up.size + count * capacity * columns)),
        name="expand",
    )(one, two, up, *parts)


def finish_body(count, unsort_ref, *refs):
    deltas, sums, out = refs[:count], refs[count:-1], refs[-1]
    base = sums[0][...].astype(f32)
    for term in sums[1:]:
        base += term[...].astype(f32)
    out[...] = (base + dot(unsort_ref[...], jnp.concatenate([d[...] for d in deltas], axis=0))).astype(bf16)


def finish(unsort, deltas, sums):
    rows, columns = sums[0].shape
    return pl.pallas_call(
        functools.partial(finish_body, len(deltas)),
        out_shape=jax.ShapeDtypeStruct((rows, columns), bf16),
        compiler_params=params(),
        cost_estimate=cost(2 * rows * unsort.shape[1] * columns, 12 * rows * columns),
        name="finish",
    )(unsort, *deltas, *sums)


def both(a, b):
    return (a.astype(f32) + b.astype(f32)).astype(bf16)


def after(value, *others):
    return lax.optimization_barrier((value,) + others)[0]


def swap(value, axis, bit):
    return lax.ppermute(value, axis, [(i, i ^ bit) for i in range(lax.axis_size(axis))])


EDGE = [(0, 1), (3, 2)]
MIDDLE = [(1, 2), (2, 1)]


def tp_sums(mine, *before):
    sums, bit = [mine], 1
    while True:
        other = swap(sums[-1], "tp", bit)
        bit *= 2
        if bit >= lax.axis_size("tp"):
            return sums, other
        sums.append(both(after(sums[-1], *before), other))


def shards(x, ids, table, weight, down, up):
    holders = lax.axis_size("ad")
    capacity = x.shape[0] // 4
    slots = up.shape[0] // ADAPTER_RANK
    width = up.shape[1]
    total = holders * capacity
    me, z = lax.axis_index("ad"), lax.axis_index("tp")
    place, *send, x, w = sort_rows(me, z, ids, table, x, weight, holders, slots, capacity, width)
    parts = [send[0]] + [swap(send[j], "ad", j) for j in range(1, holders)]
    if lax.axis_size("tp") == 4:
        first = first_block(x, w)
        edge0 = lax.ppermute(first, "tp", EDGE)
        second, third, own, unsort = rest(z, after(place, first), x, weight, width, total)
        edge1 = lax.ppermute(second, "tp", EDGE)
        early = shrink_partial(down, parts[:-1])
        inner0 = both(after(first, early), edge0)
        middle0 = lax.ppermute(inner0, "tp", MIDDLE)
        mine = shrink_partial(down, [after(parts[-1], inner0)], [early])
        inner1 = both(second, edge1)
        steps, other = tp_sums(mine, inner1)
        middle1 = lax.ppermute(after(inner1, steps[-1]), "tp", MIDDLE)
        last = swap(both(after(third, steps[-1]), middle0), "tp", 1)
        sums = [own, middle1, last]
    else:
        unsort = unsort_only(place, total)
        full = dot(x, weight).astype(bf16)
        sums = [lax.psum_scatter(full, "tp", scatter_dimension=1, tiled=True)]
        steps, other = tp_sums(shrink_partial(down, parts))
    deltas = expand(steps[-1], other, up, parts)
    back = [deltas[0]] + [swap(deltas[j], "ad", j) for j in range(1, holders)]
    return finish(unsort, back, sums)


def solution(mesh):
    in_specs = (
        P(("rep", "ad"), "tp"),
        P(("rep", "ad")),
        P("rep"),
        P("tp", None),
        P(("rep", "tp"), "ad"),
        P(("rep", "ad"), "tp"),
    )
    out_specs = P(("rep", "ad"), "tp")
    return jax.shard_map(shards, mesh=mesh, in_specs=in_specs, out_specs=out_specs, check_vma=False)
```

```python
import functools

import jax
import jax.numpy as jnp
from jax import lax
from jax.experimental import pallas as pl
from jax.experimental.pallas import tpu as pltpu
from jax.sharding import PartitionSpec as P

ADAPTER_RANK = 64
LANES = 128
VMEM_BYTES = 32 * 1024 * 1024

bf16 = jnp.bfloat16
f32 = jnp.float32
i32 = jnp.int32


def params():
    return pltpu.CompilerParams(vmem_limit_bytes=VMEM_BYTES)


def cost(flops, nbytes):
    return pl.CostEstimate(flops=flops, bytes_accessed=nbytes, transcendentals=0)


def dot(a, b, contract=((1,), (0,))):
    return lax.dot_general(a, b, (contract, ((), ())), preferred_element_type=f32)


def in_hbm(a):
    return pltpu.with_memory_space_constraint(a, pltpu.HBM)


def iota(shape, dim):
    return lax.broadcasted_iota(i32, shape, dim)


def places(slots, capacity, holders, me, ids, table, earlier):
    rows = ids.shape[1]
    low = (iota((LANES, rows), 0) == (ids & (LANES - 1))).astype(f32).astype(bf16)
    high = iota((table.shape[0], rows), 0) == lax.shift_right_logical(ids, 7)
    found = dot(table.astype(f32).astype(bf16), low)
    slot = jnp.sum(jnp.where(high, found, 0.0), axis=0, keepdims=True).astype(i32)
    holder = lax.div(slot, slots)
    tag = (slot - holder * slots + 1).astype(f32)
    partner = holder ^ me
    mine = iota((max(8, holders), rows), 0) == partner
    before = dot(mine.astype(f32).astype(bf16), earlier)
    rank = jnp.sum(jnp.where(mine, before, 0.0), axis=0, keepdims=True).astype(i32)
    return partner * capacity + rank, tag


def sort_body(slots, capacity, holders, me_ref, z_ref, ids_hbm, table_hbm, x_hbm, w_hbm, place_ref, *refs):
    outs, (x_buf, w_buf, ids_buf, table_buf, small_sem, x_sem, w_sem) = refs[:holders], refs[holders:]
    rows, features = x_buf.shape
    width = w_buf.shape[1]
    chunks = x_sem.shape[0]
    step = features // chunks
    small = [
        pltpu.make_async_copy(ids_hbm, ids_buf, small_sem.at[0]),
        pltpu.make_async_copy(table_hbm, table_buf, small_sem.at[1]),
    ]
    copies = []
    for c in range(chunks):
        part = pl.ds(c * step, step)
        copies.append(pltpu.make_async_copy(x_hbm.at[:, part], x_buf.at[:, part], x_sem.at[c]))
    column = pl.multiple_of(jnp.where(z_ref[0] < 2, 3, 0) * width, width)
    w_copy = pltpu.make_async_copy(w_hbm.at[:, pl.ds(column, width)], w_buf, w_sem)
    for copy in small + copies + [w_copy]:
        copy.start()
    earlier = (iota((rows, rows), 0) < iota((rows, rows), 1)).astype(f32).astype(bf16)
    for copy in small:
        copy.wait()
    place, tag = places(slots, capacity, holders, me_ref[0], ids_buf[...], table_buf[...], earlier)
    place_ref[...] = jnp.broadcast_to(place, place_ref.shape)
    pick = (iota((holders * capacity, rows), 0) == place).astype(f32).astype(bf16)
    tags = dot(pick, jnp.broadcast_to(tag, (LANES, rows)).astype(bf16), ((1,), (1,))).astype(bf16)
    for j, out in enumerate(outs):
        out[:, features:] = tags[j * capacity:(j + 1) * capacity]
    for c in range(chunks):
        copies[c].wait()
        moved = dot(pick, x_buf[:, c * step:(c + 1) * step]).astype(bf16)
        for j, out in enumerate(outs):
            out[:, c * step:(c + 1) * step] = moved[j * capacity:(j + 1) * capacity]
    w_copy.wait()


def sort_rows(me, z, ids, table, x, weight, holders, slots, capacity, width):
    rows, features = x.shape
    ids, table = ids.reshape(1, rows), table.reshape(-1, LANES)
    chunks = max(1, features // 512)
    smem, vmem, hbm = (pl.BlockSpec(memory_space=m) for m in (pltpu.SMEM, pltpu.VMEM, pltpu.HBM))
    shapes = [jax.ShapeDtypeStruct((8, rows), i32)]
    shapes += [jax.ShapeDtypeStruct((capacity, features + LANES), bf16)] * holders
    shapes += [jax.ShapeDtypeStruct((rows, features), bf16), jax.ShapeDtypeStruct((features, width), bf16)]
    return pl.pallas_call(
        functools.partial(sort_body, slots, capacity, holders),
        out_shape=shapes,
        in_specs=[smem, smem, hbm, hbm, hbm, hbm],
        out_specs=[vmem] * len(shapes),
        scratch_shapes=[
            pltpu.VMEM(ids.shape, i32),
            pltpu.VMEM(table.shape, i32),
            pltpu.SemaphoreType.DMA((2,)),
            pltpu.SemaphoreType.DMA((chunks,)),
            pltpu.SemaphoreType.DMA(()),
        ],
        compiler_params=params(),
        cost_estimate=cost(2 * holders * capacity * rows * features, 4 * rows * features),
        name="sort_rows",
    )(me.reshape(1), z.reshape(1), in_hbm(ids), in_hbm(table), in_hbm(x), in_hbm(weight))


def first_body(x_ref, w_ref, out):
    out[...] = dot(x_ref[...], w_ref[...]).astype(bf16)


def first_block(x, w):
    (rows, features), width = x.shape, w.shape[1]
    return pl.pallas_call(
        first_body,
        out_shape=jax.ShapeDtypeStruct((rows, width), bf16),
        compiler_params=params(),
        cost_estimate=cost(2 * rows * features * width, 2 * features * (rows + width)),
        name="first_block",
    )(x, w)


def rest_body(z_ref, place_ref, x_ref, w_hbm, *refs):
    second, third, own, unsort, w_buf, sem = refs
    z = z_ref[0]
    width = own.shape[1]
    blocks = (jnp.where(z < 2, 2, 1), z ^ 1, z)
    copies = []
    for k, block in enumerate(blocks):
        column = pl.multiple_of(block * width, width)
        copies.append(pltpu.make_async_copy(w_hbm.at[:, pl.ds(column, width)], w_buf.at[k], sem.at[k]))
        copies[k].start()
    unsort_matrix(place_ref, unsort)
    x = x_ref[...]
    for k, out in enumerate((second, third, own)):
        copies[k].wait()
        out[...] = dot(x, w_buf[k]).astype(bf16)


def unsort_matrix(place_ref, unsort):
    rows, total = unsort.shape
    place = jnp.broadcast_to(place_ref[0:1, :].astype(f32), (LANES, rows)).T
    lane = iota((rows, LANES), 1).astype(f32)
    for k in range(total // LANES):
        unsort[:, k * LANES:(k + 1) * LANES] = (place == lane + float(k * LANES)).astype(f32).astype(bf16)


def rest(z, place, x, weight, width, total):
    rows, features = x.shape
    smem, vmem, hbm = (pl.BlockSpec(memory_space=m) for m in (pltpu.SMEM, pltpu.VMEM, pltpu.HBM))
    shapes = [jax.ShapeDtypeStruct((rows, width), bf16)] * 3 + [jax.ShapeDtypeStruct((rows, total), bf16)]
    return pl.pallas_call(
        rest_body,
        out_shape=shapes,
        in_specs=[smem, vmem, vmem, hbm],
        out_specs=[vmem] * len(shapes),
        scratch_shapes=[pltpu.VMEM((3, features, width), bf16), pltpu.SemaphoreType.DMA((3,))],
        compiler_params=params(),
        cost_estimate=cost(6 * rows * features * width, 2 * features * (rows + 4 * width)),
        name="rest",
    )(z.reshape(1), place, x, in_hbm(weight))


def unsort_only(place, total):
    return pl.pallas_call(
        unsort_matrix,
        out_shape=jax.ShapeDtypeStruct((place.shape[1], total), bf16),
        compiler_params=params(),
        name="unsort",
    )(place)


def slot_mask(tag, group):
    lane = iota(tag.shape, 1)
    return tag == jnp.where(lane < ADAPTER_RANK, 2 * group + 1, 2 * group + 2).astype(f32)


def shrink_body(kept, down_ref, *refs):
    parts, out = refs[1 if kept else 0:-1], refs[-1]
    features, width = down_ref.shape
    capacity = parts[0].shape[0]
    half = capacity // 2
    first = iota((half, LANES), 1) < ADAPTER_RANK
    if kept:
        out[:kept, :] = refs[0][...]
    for k, part in enumerate(parts):
        full = dot(part[:, :features], down_ref[...])
        tag = part[:, features:].astype(f32)
        total = jnp.zeros((capacity, LANES), f32)
        for group in range(width // LANES):
            total += jnp.where(slot_mask(tag, group), full[:, group * LANES:(group + 1) * LANES], 0.0)
        total += pltpu.roll(total, ADAPTER_RANK, 1)
        spot = slice(kept + k * half, kept + (k + 1) * half)
        out[spot, :] = jnp.where(first, total[:half], total[half:]).astype(bf16)


def shrink_partial(down, parts, done=()):
    features, width = down.shape
    capacity = parts[0].shape[0]
    total = len(parts) * capacity
    kept = sum(d.shape[0] for d in done)
    return pl.pallas_call(
        functools.partial(shrink_body, kept),
        out_shape=jax.ShapeDtypeStruct((kept + total // 2, LANES), bf16),
        compiler_params=params(),
        cost_estimate=cost(2 * total * features * width, 2 * features * (total + width)),
        name="shrink_partial",
    )(down, *done, *parts)


def expand_body(count, one_ref, two_ref, up_ref, *refs):
    tags, outs = refs[:count], refs[count:]
    capacity = outs[0].shape[0]
    half = capacity // 2
    up = up_ref[...]
    first = iota((half, LANES), 1) < ADAPTER_RANK
    for k in range(count):
        part = pl.ds(k * half, half)
        shrink = (one_ref[part, :].astype(f32) + two_ref[part, :].astype(f32)).astype(bf16).astype(f32)
        turned = pltpu.roll(shrink, ADAPTER_RANK, 1)
        rows = jnp.concatenate([jnp.where(first, shrink, turned), jnp.where(first, turned, shrink)], axis=0)
        tag = tags[k][...].astype(f32)
        spread = [
            jnp.where(slot_mask(tag, group), rows, 0.0).astype(bf16) for group in range(up.shape[0] // LANES)
        ]
        outs[k][...] = dot(jnp.concatenate(spread, axis=1), up).astype(bf16)


def expand(one, two, up, parts):
    capacity, width = parts[0].shape
    count = len(parts)
    tag_block = pl.BlockSpec((capacity, LANES), lambda i: (0, width // LANES - 1))
    whole = lambda a: pl.BlockSpec(a.shape, lambda i: (0, 0))
    columns = up.shape[1]
    return pl.pallas_call(
        functools.partial(expand_body, count),
        grid=(1,),
        out_shape=[jax.ShapeDtypeStruct((capacity, columns), bf16)] * count,
        in_specs=[whole(one), whole(two), whole(up)] + [tag_block] * count,
        out_specs=[pl.BlockSpec((capacity, columns), lambda i: (0, 0))] * count,
        compiler_params=params(),
        cost_estimate=cost(80 * count * capacity * up.size, 80 * (up.size + count * capacity * columns)),
        name="expand",
    )(one, two, up, *parts)


def finish_body(count, unsort_ref, *refs):
    deltas, sums, out = refs[:count], refs[count:-1], refs[-1]
    base = sums[0][...].astype(f32)
    for term in sums[1:]:
        base += term[...].astype(f32)
    out[...] = (base + dot(unsort_ref[...], jnp.concatenate([d[...] for d in deltas], axis=0))).astype(bf16)


def finish(unsort, deltas, sums):
    rows, columns = sums[0].shape
    return pl.pallas_call(
        functools.partial(finish_body, len(deltas)),
        out_shape=jax.ShapeDtypeStruct((rows, columns), bf16),
        compiler_params=params(),
        cost_estimate=cost(2 * rows * unsort.shape[1] * columns, 12 * rows * columns),
        name="finish",
    )(unsort, *deltas, *sums)


def both(a, b):
    return (a.astype(f32) + b.astype(f32)).astype(bf16)


def after(value, *others):
    return lax.optimization_barrier((value,) + others)[0]


def swap(value, axis, bit):
    return lax.ppermute(value, axis, [(i, i ^ bit) for i in range(lax.axis_size(axis))])


EDGE = [(0, 1), (3, 2)]
MIDDLE = [(1, 2), (2, 1)]
ACROSS = [(1, 3), (2, 0)]


def tp_sums(mine, *before):
    sums, bit = [mine], 1
    while True:
        other = swap(sums[-1], "tp", bit)
        bit *= 2
        if bit >= lax.axis_size("tp"):
            return sums, other
        sums.append(both(after(sums[-1], *before), other))


def shards(x, ids, table, weight, down, up):
    holders = lax.axis_size("ad")
    capacity = x.shape[0] // 4
    slots = up.shape[0] // ADAPTER_RANK
    width = up.shape[1]
    total = holders * capacity
    me, z = lax.axis_index("ad"), lax.axis_index("tp")
    place, *send, x, w = sort_rows(me, z, ids, table, x, weight, holders, slots, capacity, width)
    parts = [send[0]] + [swap(send[j], "ad", j) for j in range(1, holders)]
    if lax.axis_size("tp") == 4:
        first = first_block(x, w)
        edge0 = lax.ppermute(first, "tp", EDGE)
        second, third, own, unsort = rest(z, after(place, first), x, weight, width, total)
        edge1 = lax.ppermute(second, "tp", EDGE)
        early = shrink_partial(down, parts[:-1])
        inner0 = both(after(first, early), edge0)
        across = lax.ppermute(inner0, "tp", ACROSS)
        mine = shrink_partial(down, [after(parts[-1], inner0)], [early])
        inner1 = both(second, edge1)
        steps, other = tp_sums(mine, inner1)
        middle1 = lax.ppermute(after(inner1, steps[-1], across), "tp", MIDDLE)
        last = swap(after(third, steps[-1]), "tp", 1)
        sums = [own, across, middle1, last]
    else:
        unsort = unsort_only(place, total)
        full = dot(x, weight).astype(bf16)
        sums = [lax.psum_scatter(full, "tp", scatter_dimension=1, tiled=True)]
        steps, other = tp_sums(shrink_partial(down, parts))
    deltas = expand(steps[-1], other, up, parts)
    back = [deltas[0]] + [swap(deltas[j], "ad", j) for j in range(1, holders)]
    return finish(unsort, back, sums)


def solution(mesh):
    in_specs = (
        P(("rep", "ad"), "tp"),
        P(("rep", "ad")),
        P("rep"),
        P("tp", None),
        P(("rep", "tp"), "ad"),
        P(("rep", "ad"), "tp"),
    )
    out_specs = P(("rep", "ad"), "tp")
    return jax.shard_map(shards, mesh=mesh, in_specs=in_specs, out_specs=out_specs, check_vma=False)
```

```python
import functools

import jax
import jax.numpy as jnp
from jax import lax
from jax.experimental import pallas as pl
from jax.experimental.pallas import tpu as pltpu
from jax.sharding import PartitionSpec as P

ADAPTER_RANK = 64
LANES = 128
VMEM_BYTES = 32 * 1024 * 1024

bf16 = jnp.bfloat16
f32 = jnp.float32
i32 = jnp.int32


def params():
    return pltpu.CompilerParams(vmem_limit_bytes=VMEM_BYTES)


def cost(flops, nbytes):
    return pl.CostEstimate(flops=flops, bytes_accessed=nbytes, transcendentals=0)


def dot(a, b, contract=((1,), (0,))):
    return lax.dot_general(a, b, (contract, ((), ())), preferred_element_type=f32)


def in_hbm(a):
    return pltpu.with_memory_space_constraint(a, pltpu.HBM)


def iota(shape, dim):
    return lax.broadcasted_iota(i32, shape, dim)


def places(slots, capacity, holders, me, ids, table, earlier):
    rows = ids.shape[1]
    low = (iota((LANES, rows), 0) == (ids & (LANES - 1))).astype(f32).astype(bf16)
    high = iota((table.shape[0], rows), 0) == lax.shift_right_logical(ids, 7)
    found = dot(table.astype(f32).astype(bf16), low)
    slot = jnp.sum(jnp.where(high, found, 0.0), axis=0, keepdims=True).astype(i32)
    holder = lax.div(slot, slots)
    tag = (slot - holder * slots + 1).astype(f32)
    partner = holder ^ me
    mine = iota((max(8, holders), rows), 0) == partner
    before = dot(mine.astype(f32).astype(bf16), earlier)
    rank = jnp.sum(jnp.where(mine, before, 0.0), axis=0, keepdims=True).astype(i32)
    return partner * capacity + rank, tag


def sort_body(slots, capacity, holders, me_ref, z_ref, ids_hbm, table_hbm, x_hbm, w_hbm, place_ref, *refs):
    outs, (x_buf, w_buf, ids_buf, table_buf, small_sem, x_sem, w_sem) = refs[:holders], refs[holders:]
    rows, features = x_buf.shape
    width = w_buf.shape[1]
    chunks = x_sem.shape[0]
    step = features // chunks
    small = [
        pltpu.make_async_copy(ids_hbm, ids_buf, small_sem.at[0]),
        pltpu.make_async_copy(table_hbm, table_buf, small_sem.at[1]),
    ]
    copies = []
    for c in range(chunks):
        part = pl.ds(c * step, step)
        copies.append(pltpu.make_async_copy(x_hbm.at[:, part], x_buf.at[:, part], x_sem.at[c]))
    column = pl.multiple_of(jnp.where(z_ref[0] < 2, 3, 0) * width, width)
    w_copy = pltpu.make_async_copy(w_hbm.at[:, pl.ds(column, width)], w_buf, w_sem)
    for copy in small + copies + [w_copy]:
        copy.start()
    earlier = (iota((rows, rows), 0) < iota((rows, rows), 1)).astype(f32).astype(bf16)
    for copy in small:
        copy.wait()
    place, tag = places(slots, capacity, holders, me_ref[0], ids_buf[...], table_buf[...], earlier)
    place_ref[...] = jnp.broadcast_to(place, place_ref.shape)
    pick = (iota((holders * capacity, rows), 0) == place).astype(f32).astype(bf16)
    tags = dot(pick, jnp.broadcast_to(tag, (LANES, rows)).astype(bf16), ((1,), (1,))).astype(bf16)
    for j, out in enumerate(outs):
        out[:, features:] = tags[j * capacity:(j + 1) * capacity]
    for c in range(chunks):
        copies[c].wait()
        moved = dot(pick, x_buf[:, c * step:(c + 1) * step]).astype(bf16)
        for j, out in enumerate(outs):
            out[:, c * step:(c + 1) * step] = moved[j * capacity:(j + 1) * capacity]
    w_copy.wait()


def sort_rows(me, z, ids, table, x, weight, holders, slots, capacity, width):
    rows, features = x.shape
    ids, table = ids.reshape(1, rows), table.reshape(-1, LANES)
    chunks = max(1, features // 512)
    smem, vmem, hbm = (pl.BlockSpec(memory_space=m) for m in (pltpu.SMEM, pltpu.VMEM, pltpu.HBM))
    shapes = [jax.ShapeDtypeStruct((8, rows), i32)]
    shapes += [jax.ShapeDtypeStruct((capacity, features + LANES), bf16)] * holders
    shapes += [jax.ShapeDtypeStruct((rows, features), bf16), jax.ShapeDtypeStruct((features, width), bf16)]
    return pl.pallas_call(
        functools.partial(sort_body, slots, capacity, holders),
        out_shape=shapes,
        in_specs=[smem, smem, hbm, hbm, hbm, hbm],
        out_specs=[vmem] * len(shapes),
        scratch_shapes=[
            pltpu.VMEM(ids.shape, i32),
            pltpu.VMEM(table.shape, i32),
            pltpu.SemaphoreType.DMA((2,)),
            pltpu.SemaphoreType.DMA((chunks,)),
            pltpu.SemaphoreType.DMA(()),
        ],
        compiler_params=params(),
        cost_estimate=cost(2 * holders * capacity * rows * features, 4 * rows * features),
        name="sort_rows",
    )(me.reshape(1), z.reshape(1), in_hbm(ids), in_hbm(table), in_hbm(x), in_hbm(weight))


def first_body(x_ref, w_ref, *outs):
    half = outs[0].shape[0]
    for k, out in enumerate(outs):
        out[...] = dot(x_ref[k * half:(k + 1) * half, :], w_ref[...]).astype(bf16)


def first_block(x, w):
    (rows, features), width = x.shape, w.shape[1]
    return pl.pallas_call(
        first_body,
        out_shape=[jax.ShapeDtypeStruct((rows // 2, width), bf16)] * 2,
        compiler_params=params(),
        cost_estimate=cost(2 * rows * features * width, 2 * features * (rows + width)),
        name="first_block",
    )(x, w)


def rest_body(z_ref, place_ref, x_ref, w_hbm, *refs):
    second, third, own, unsort, w_buf, sem = refs
    z = z_ref[0]
    width = own.shape[1]
    blocks = (jnp.where(z < 2, 2, 1), z ^ 1, z)
    copies = []
    for k, block in enumerate(blocks):
        column = pl.multiple_of(block * width, width)
        copies.append(pltpu.make_async_copy(w_hbm.at[:, pl.ds(column, width)], w_buf.at[k], sem.at[k]))
        copies[k].start()
    unsort_matrix(place_ref, unsort)
    x = x_ref[...]
    for k, out in enumerate((second, third, own)):
        copies[k].wait()
        out[...] = dot(x, w_buf[k]).astype(bf16)


def unsort_matrix(place_ref, unsort):
    rows, total = unsort.shape
    place = jnp.broadcast_to(place_ref[0:1, :].astype(f32), (LANES, rows)).T
    lane = iota((rows, LANES), 1).astype(f32)
    for k in range(total // LANES):
        unsort[:, k * LANES:(k + 1) * LANES] = (place == lane + float(k * LANES)).astype(f32).astype(bf16)


def rest(z, place, x, weight, width, total):
    rows, features = x.shape
    smem, vmem, hbm = (pl.BlockSpec(memory_space=m) for m in (pltpu.SMEM, pltpu.VMEM, pltpu.HBM))
    shapes = [jax.ShapeDtypeStruct((rows, width), bf16)] * 3 + [jax.ShapeDtypeStruct((rows, total), bf16)]
    return pl.pallas_call(
        rest_body,
        out_shape=shapes,
        in_specs=[smem, vmem, vmem, hbm],
        out_specs=[vmem] * len(shapes),
        scratch_shapes=[pltpu.VMEM((3, features, width), bf16), pltpu.SemaphoreType.DMA((3,))],
        compiler_params=params(),
        cost_estimate=cost(6 * rows * features * width, 2 * features * (rows + 4 * width)),
        name="rest",
    )(z.reshape(1), place, x, in_hbm(weight))


def unsort_only(place, total):
    return pl.pallas_call(
        unsort_matrix,
        out_shape=jax.ShapeDtypeStruct((place.shape[1], total), bf16),
        compiler_params=params(),
        name="unsort",
    )(place)


def slot_mask(tag, group):
    lane = iota(tag.shape, 1)
    return tag == jnp.where(lane < ADAPTER_RANK, 2 * group + 1, 2 * group + 2).astype(f32)


def shrink_body(kept, down_ref, *refs):
    parts, out = refs[1 if kept else 0:-1], refs[-1]
    features, width = down_ref.shape
    capacity = parts[0].shape[0]
    half = capacity // 2
    first = iota((half, LANES), 1) < ADAPTER_RANK
    if kept:
        out[:kept, :] = refs[0][...]
    for k, part in enumerate(parts):
        full = dot(part[:, :features], down_ref[...])
        tag = part[:, features:].astype(f32)
        total = jnp.zeros((capacity, LANES), f32)
        for group in range(width // LANES):
            total += jnp.where(slot_mask(tag, group), full[:, group * LANES:(group + 1) * LANES], 0.0)
        total += pltpu.roll(total, ADAPTER_RANK, 1)
        spot = slice(kept + k * half, kept + (k + 1) * half)
        out[spot, :] = jnp.where(first, total[:half], total[half:]).astype(bf16)


def shrink_partial(down, parts, done=()):
    features, width = down.shape
    capacity = parts[0].shape[0]
    total = len(parts) * capacity
    kept = sum(d.shape[0] for d in done)
    return pl.pallas_call(
        functools.partial(shrink_body, kept),
        out_shape=jax.ShapeDtypeStruct((kept + total // 2, LANES), bf16),
        compiler_params=params(),
        cost_estimate=cost(2 * total * features * width, 2 * features * (total + width)),
        name="shrink_partial",
    )(down, *done, *parts)


def expand_body(count, one_ref, two_ref, up_ref, *refs):
    tags, outs = refs[:count], refs[count:]
    capacity = outs[0].shape[0]
    half = capacity // 2
    up = up_ref[...]
    first = iota((half, LANES), 1) < ADAPTER_RANK
    for k in range(count):
        part = pl.ds(k * half, half)
        shrink = (one_ref[part, :].astype(f32) + two_ref[part, :].astype(f32)).astype(bf16).astype(f32)
        turned = pltpu.roll(shrink, ADAPTER_RANK, 1)
        rows = jnp.concatenate([jnp.where(first, shrink, turned), jnp.where(first, turned, shrink)], axis=0)
        tag = tags[k][...].astype(f32)
        spread = [
            jnp.where(slot_mask(tag, group), rows, 0.0).astype(bf16) for group in range(up.shape[0] // LANES)
        ]
        outs[k][...] = dot(jnp.concatenate(spread, axis=1), up).astype(bf16)


def expand(one, two, up, parts):
    capacity, width = parts[0].shape
    count = len(parts)
    tag_block = pl.BlockSpec((capacity, LANES), lambda i: (0, width // LANES - 1))
    whole = lambda a: pl.BlockSpec(a.shape, lambda i: (0, 0))
    columns = up.shape[1]
    return pl.pallas_call(
        functools.partial(expand_body, count),
        grid=(1,),
        out_shape=[jax.ShapeDtypeStruct((capacity, columns), bf16)] * count,
        in_specs=[whole(one), whole(two), whole(up)] + [tag_block] * count,
        out_specs=[pl.BlockSpec((capacity, columns), lambda i: (0, 0))] * count,
        compiler_params=params(),
        cost_estimate=cost(80 * count * capacity * up.size, 80 * (up.size + count * capacity * columns)),
        name="expand",
    )(one, two, up, *parts)


def finish_body(count, unsort_ref, *refs):
    deltas, sums, out = refs[:count], refs[count:-1], refs[-1]
    rows = out.shape[0]
    base = None
    at = 0
    while at < len(sums):
        if sums[at].shape[0] == rows:
            term, at = sums[at][...].astype(f32), at + 1
        else:
            term, at = jnp.concatenate([sums[at][...], sums[at + 1][...]], axis=0).astype(f32), at + 2
        base = term if base is None else base + term
    out[...] = (base + dot(unsort_ref[...], jnp.concatenate([d[...] for d in deltas], axis=0))).astype(bf16)


def finish(unsort, deltas, sums):
    rows, columns = sums[0].shape
    return pl.pallas_call(
        functools.partial(finish_body, len(deltas)),
        out_shape=jax.ShapeDtypeStruct((rows, columns), bf16),
        compiler_params=params(),
        cost_estimate=cost(2 * rows * unsort.shape[1] * columns, 12 * rows * columns),
        name="finish",
    )(unsort, *deltas, *sums)


def both(a, b):
    return (a.astype(f32) + b.astype(f32)).astype(bf16)


def after(value, *others):
    return lax.optimization_barrier((value,) + others)[0]


def swap(value, axis, bit):
    return lax.ppermute(value, axis, [(i, i ^ bit) for i in range(lax.axis_size(axis))])


EDGE = [(0, 1), (3, 2)]
MIDDLE = [(1, 2), (2, 1)]
ACROSS = [(1, 3), (2, 0)]


def tp_sums(mine, *before):
    sums, bit = [mine], 1
    while True:
        other = swap(sums[-1], "tp", bit)
        bit *= 2
        if bit >= lax.axis_size("tp"):
            return sums, other
        sums.append(both(after(sums[-1], *before), other))


def shards(x, ids, table, weight, down, up):
    holders = lax.axis_size("ad")
    capacity = x.shape[0] // 4
    slots = up.shape[0] // ADAPTER_RANK
    width = up.shape[1]
    total = holders * capacity
    me, z = lax.axis_index("ad"), lax.axis_index("tp")
    place, *send, x, w = sort_rows(me, z, ids, table, x, weight, holders, slots, capacity, width)
    parts = [send[0]] + [swap(send[j], "ad", j) for j in range(1, holders)]
    if lax.axis_size("tp") == 4:
        first = first_block(x, w)
        edge0 = [lax.ppermute(f, "tp", EDGE) for f in first]
        second, third, own, unsort = rest(z, after(place, *first), x, weight, width, total)
        edge1 = lax.ppermute(second, "tp", EDGE)
        inner0 = [both(first[0], edge0[0])]
        parts[1] = after(parts[1], *inner0)
        early = shrink_partial(down, parts[:-1])
        inner0.append(both(after(first[1], early), edge0[1]))
        across = [lax.ppermute(i, "tp", ACROSS) for i in inner0]
        mine = shrink_partial(down, [after(parts[-1], *inner0)], [early])
        inner1 = both(second, edge1)
        steps, other = tp_sums(mine, inner1, *across)
        middle1 = lax.ppermute(after(inner1, steps[-1]), "tp", MIDDLE)
        last = swap(after(third, steps[-1]), "tp", 1)
        sums = [own, *across, middle1, last]
    else:
        unsort = unsort_only(place, total)
        full = dot(x, weight).astype(bf16)
        sums = [lax.psum_scatter(full, "tp", scatter_dimension=1, tiled=True)]
        steps, other = tp_sums(shrink_partial(down, parts))
    deltas = expand(steps[-1], other, up, parts)
    back = [deltas[0]] + [swap(deltas[j], "ad", j) for j in range(1, holders)]
    return finish(unsort, back, sums)


def solution(mesh):
    in_specs = (
        P(("rep", "ad"), "tp"),
        P(("rep", "ad")),
        P("rep"),
        P("tp", None),
        P(("rep", "tp"), "ad"),
        P(("rep", "ad"), "tp"),
    )
    out_specs = P(("rep", "ad"), "tp")
    return jax.shard_map(shards, mesh=mesh, in_specs=in_specs, out_specs=out_specs, check_vma=False)
```

```python
import functools

import jax
import jax.numpy as jnp
from jax import lax
from jax.experimental import pallas as pl
from jax.experimental.pallas import tpu as pltpu
from jax.sharding import PartitionSpec as P

ADAPTER_RANK = 64
LANES = 128
VMEM_BYTES = 32 * 1024 * 1024

bf16 = jnp.bfloat16
f32 = jnp.float32
i32 = jnp.int32


def params():
    return pltpu.CompilerParams(vmem_limit_bytes=VMEM_BYTES)


def cost(flops, nbytes):
    return pl.CostEstimate(flops=flops, bytes_accessed=nbytes, transcendentals=0)


def dot(a, b, contract=((1,), (0,))):
    return lax.dot_general(a, b, (contract, ((), ())), preferred_element_type=f32)


def in_hbm(a):
    return pltpu.with_memory_space_constraint(a, pltpu.HBM)


def iota(shape, dim):
    return lax.broadcasted_iota(i32, shape, dim)


def places(slots, capacity, holders, me, ids, table):
    rows = ids.shape[1]
    low = (iota((LANES, rows), 0) == (ids & (LANES - 1))).astype(f32).astype(bf16)
    high = iota((table.shape[0], rows), 0) == lax.shift_right_logical(ids, 7)
    found = dot(table.astype(f32).astype(bf16), low)
    slot = jnp.sum(jnp.where(high, found, 0.0), axis=0, keepdims=True).astype(i32)
    holder = split_slot(slot, slots)
    tag = (slot - holder * slots + 1).astype(f32)
    partner = holder ^ me
    mine = iota((max(8, holders), rows), 0) == partner
    ones = mine.astype(f32)
    groups = [ones[:, k:k + LANES] for k in range(0, rows, LANES)]
    earlier = (iota((LANES, LANES), 0) < iota((LANES, LANES), 1)).astype(f32).astype(bf16)
    before = dot(jnp.concatenate(groups, axis=0).astype(bf16), earlier)
    count = ones.shape[0]
    ranks, passed = [], jnp.zeros((count, 1), f32)
    for k, group in enumerate(groups):
        ranks.append(jnp.sum(group * (before[k * count:(k + 1) * count] + passed), axis=0, keepdims=True))
        passed += jnp.sum(group, axis=1, keepdims=True)
    return partner * capacity + jnp.concatenate(ranks, axis=1).astype(i32), tag


def split_slot(slot, slots):
    if slots & (slots - 1):
        return lax.div(slot, slots)
    return lax.shift_right_logical(slot, slots.bit_length() - 1)


def sort_body(slots, capacity, holders, me_ref, z_ref, ids_hbm, table_hbm, x_hbm, w_hbm, place_ref, *refs):
    outs, (x_buf, w_buf, ids_buf, table_buf, small_sem, x_sem, w_sem) = refs[:holders], refs[holders:]
    rows, features = x_buf.shape
    width = w_buf.shape[1]
    chunks = x_sem.shape[0]
    step = features // chunks
    small = [
        pltpu.make_async_copy(ids_hbm, ids_buf, small_sem.at[0]),
        pltpu.make_async_copy(table_hbm, table_buf, small_sem.at[1]),
    ]
    copies = []
    for c in range(chunks):
        part = pl.ds(c * step, step)
        copies.append(pltpu.make_async_copy(x_hbm.at[:, part], x_buf.at[:, part], x_sem.at[c]))
    column = pl.multiple_of(jnp.where(z_ref[0] < 2, 3, 0) * width, width)
    w_copy = pltpu.make_async_copy(w_hbm.at[:, pl.ds(column, width)], w_buf, w_sem)
    for copy in small + copies + [w_copy]:
        copy.start()
    for copy in small:
        copy.wait()
    place, tag = places(slots, capacity, holders, me_ref[0], ids_buf[...], table_buf[...])
    place_ref[...] = jnp.broadcast_to(place, place_ref.shape)
    pick = (iota((holders * capacity, rows), 0) == place).astype(f32).astype(bf16)
    tags = dot(pick, jnp.broadcast_to(tag, (LANES, rows)).astype(bf16), ((1,), (1,))).astype(bf16)
    for j, out in enumerate(outs):
        out[:, features:] = tags[j * capacity:(j + 1) * capacity]
    for c in range(chunks):
        copies[c].wait()
        moved = dot(pick, x_buf[:, c * step:(c + 1) * step]).astype(bf16)
        for j, out in enumerate(outs):
            out[:, c * step:(c + 1) * step] = moved[j * capacity:(j + 1) * capacity]
    w_copy.wait()


def sort_rows(me, z, ids, table, x, weight, holders, slots, capacity, width):
    rows, features = x.shape
    ids, table = ids.reshape(1, rows), table.reshape(-1, LANES)
    chunks = max(1, features // 512)
    smem, vmem, hbm = (pl.BlockSpec(memory_space=m) for m in (pltpu.SMEM, pltpu.VMEM, pltpu.HBM))
    shapes = [jax.ShapeDtypeStruct((8, rows), i32)]
    shapes += [jax.ShapeDtypeStruct((capacity, features + LANES), bf16)] * holders
    shapes += [jax.ShapeDtypeStruct((rows, features), bf16), jax.ShapeDtypeStruct((features, width), bf16)]
    return pl.pallas_call(
        functools.partial(sort_body, slots, capacity, holders),
        out_shape=shapes,
        in_specs=[smem, smem, hbm, hbm, hbm, hbm],
        out_specs=[vmem] * len(shapes),
        scratch_shapes=[
            pltpu.VMEM(ids.shape, i32),
            pltpu.VMEM(table.shape, i32),
            pltpu.SemaphoreType.DMA((2,)),
            pltpu.SemaphoreType.DMA((chunks,)),
            pltpu.SemaphoreType.DMA(()),
        ],
        compiler_params=params(),
        cost_estimate=cost(2 * holders * capacity * rows * features, 4 * rows * features),
        name="sort_rows",
    )(me.reshape(1), z.reshape(1), in_hbm(ids), in_hbm(table), in_hbm(x), in_hbm(weight))


def first_body(x_ref, w_ref, *outs):
    half = outs[0].shape[0]
    for k, out in enumerate(outs):
        out[...] = dot(x_ref[k * half:(k + 1) * half, :], w_ref[...]).astype(bf16)


def first_block(x, w):
    (rows, features), width = x.shape, w.shape[1]
    return pl.pallas_call(
        first_body,
        out_shape=[jax.ShapeDtypeStruct((rows // 2, width), bf16)] * 2,
        compiler_params=params(),
        cost_estimate=cost(2 * rows * features * width, 2 * features * (rows + width)),
        name="first_block",
    )(x, w)


def rest_body(z_ref, place_ref, x_ref, w_hbm, *refs):
    second, upper, lower, own, unsort, w_buf, sem = refs
    z = z_ref[0]
    width = own.shape[1]
    blocks = (jnp.where(z < 2, 2, 1), z ^ 1, z)
    copies = []
    for k, block in enumerate(blocks):
        column = pl.multiple_of(block * width, width)
        copies.append(pltpu.make_async_copy(w_hbm.at[:, pl.ds(column, width)], w_buf.at[k], sem.at[k]))
        copies[k].start()
    unsort_matrix(place_ref, unsort)
    x = x_ref[...]
    half = upper.shape[0]
    for k, outs in enumerate(((second,), (upper, lower), (own,))):
        copies[k].wait()
        for i, out in enumerate(outs):
            out[...] = dot(x[i * half:] if len(outs) == 1 else x[i * half:(i + 1) * half], w_buf[k]).astype(bf16)


def unsort_matrix(place_ref, unsort):
    rows, total = unsort.shape
    place = jnp.broadcast_to(place_ref[0:1, :].astype(f32), (LANES, rows)).T
    lane = iota((rows, LANES), 1).astype(f32)
    for k in range(total // LANES):
        unsort[:, k * LANES:(k + 1) * LANES] = (place == lane + float(k * LANES)).astype(f32).astype(bf16)


def rest(z, place, x, weight, width, total):
    rows, features = x.shape
    smem, vmem, hbm = (pl.BlockSpec(memory_space=m) for m in (pltpu.SMEM, pltpu.VMEM, pltpu.HBM))
    shapes = [jax.ShapeDtypeStruct((r, width), bf16) for r in (rows, rows // 2, rows // 2, rows)]
    shapes.append(jax.ShapeDtypeStruct((rows, total), bf16))
    return pl.pallas_call(
        rest_body,
        out_shape=shapes,
        in_specs=[smem, vmem, vmem, hbm],
        out_specs=[vmem] * len(shapes),
        scratch_shapes=[pltpu.VMEM((3, features, width), bf16), pltpu.SemaphoreType.DMA((3,))],
        compiler_params=params(),
        cost_estimate=cost(6 * rows * features * width, 2 * features * (rows + 4 * width)),
        name="rest",
    )(z.reshape(1), place, x, in_hbm(weight))


def unsort_only(place, total):
    return pl.pallas_call(
        unsort_matrix,
        out_shape=jax.ShapeDtypeStruct((place.shape[1], total), bf16),
        compiler_params=params(),
        name="unsort",
    )(place)


def slot_mask(tag, group):
    lane = iota(tag.shape, 1)
    return tag == jnp.where(lane < ADAPTER_RANK, 2 * group + 1, 2 * group + 2).astype(f32)


def shrink_body(kept, down_ref, *refs):
    parts, out = refs[1 if kept else 0:-1], refs[-1]
    features, width = down_ref.shape
    capacity = parts[0].shape[0]
    half = capacity // 2
    first = iota((half, LANES), 1) < ADAPTER_RANK
    if kept:
        out[:kept, :] = refs[0][...]
    for k, part in enumerate(parts):
        full = dot(part[:, :features], down_ref[...])
        tag = part[:, features:].astype(f32)
        total = jnp.zeros((capacity, LANES), f32)
        for group in range(width // LANES):
            total += jnp.where(slot_mask(tag, group), full[:, group * LANES:(group + 1) * LANES], 0.0)
        total += pltpu.roll(total, ADAPTER_RANK, 1)
        spot = slice(kept + k * half, kept + (k + 1) * half)
        out[spot, :] = jnp.where(first, total[:half], total[half:]).astype(bf16)


def shrink_partial(down, parts, done=()):
    features, width = down.shape
    capacity = parts[0].shape[0]
    total = len(parts) * capacity
    kept = sum(d.shape[0] for d in done)
    return pl.pallas_call(
        functools.partial(shrink_body, kept),
        out_shape=jax.ShapeDtypeStruct((kept + total // 2, LANES), bf16),
        compiler_params=params(),
        cost_estimate=cost(2 * total * features * width, 2 * features * (total + width)),
        name="shrink_partial",
    )(down, *done, *parts)


def expand_body(count, one_ref, two_ref, up_ref, *refs):
    tags, outs = refs[:count], refs[count:]
    capacity = outs[0].shape[0]
    half = capacity // 2
    up = up_ref[...]
    first = iota((half, LANES), 1) < ADAPTER_RANK
    for k in range(count):
        part = pl.ds(k * half, half)
        shrink = (one_ref[part, :].astype(f32) + two_ref[part, :].astype(f32)).astype(bf16).astype(f32)
        turned = pltpu.roll(shrink, ADAPTER_RANK, 1)
        rows = jnp.concatenate([jnp.where(first, shrink, turned), jnp.where(first, turned, shrink)], axis=0)
        tag = tags[k][...].astype(f32)
        spread = [
            jnp.where(slot_mask(tag, group), rows, 0.0).astype(bf16) for group in range(up.shape[0] // LANES)
        ]
        outs[k][...] = dot(jnp.concatenate(spread, axis=1), up).astype(bf16)


def expand(one, two, up, parts):
    capacity, width = parts[0].shape
    count = len(parts)
    tag_block = pl.BlockSpec((capacity, LANES), lambda i: (0, width // LANES - 1))
    whole = lambda a: pl.BlockSpec(a.shape, lambda i: (0, 0))
    columns = up.shape[1]
    return pl.pallas_call(
        functools.partial(expand_body, count),
        grid=(1,),
        out_shape=[jax.ShapeDtypeStruct((capacity, columns), bf16)] * count,
        in_specs=[whole(one), whole(two), whole(up)] + [tag_block] * count,
        out_specs=[pl.BlockSpec((capacity, columns), lambda i: (0, 0))] * count,
        compiler_params=params(),
        cost_estimate=cost(80 * count * capacity * up.size, 80 * (up.size + count * capacity * columns)),
        name="expand",
    )(one, two, up, *parts)


def finish_body(count, halves, unsort_ref, *refs):
    deltas, sums, out = refs[:count], refs[count:-1], refs[-1]
    rows = out.shape[0]
    whole = sums[:len(sums) - len(halves)]
    parts = [[], []]
    for ref, half in zip(sums[len(whole):], halves):
        parts[half].append(ref)
    sorted_deltas = jnp.concatenate([d[...] for d in deltas], axis=0)
    for half in range(2):
        part = slice(half * rows // 2, (half + 1) * rows // 2)
        total = dot(unsort_ref[part, :], sorted_deltas)
        terms = [ref[part, :].astype(f32) for ref in whole] + [ref[...].astype(f32) for ref in parts[half]]
        base = terms[0]
        for term in terms[1:]:
            base += term
        out[part, :] = (base + total).astype(bf16)


def finish(unsort, deltas, sums, halves=()):
    rows, columns = sums[0].shape
    return pl.pallas_call(
        functools.partial(finish_body, len(deltas), [which for part, which in halves]),
        out_shape=jax.ShapeDtypeStruct((rows, columns), bf16),
        compiler_params=params(),
        cost_estimate=cost(2 * rows * unsort.shape[1] * columns, 12 * rows * columns),
        name="finish",
    )(unsort, *deltas, *sums, *[part for part, which in halves])


def both(a, b):
    return (a.astype(f32) + b.astype(f32)).astype(bf16)


def after(value, *others):
    return lax.optimization_barrier((value,) + others)[0]


def swap(value, axis, bit):
    return lax.ppermute(value, axis, [(i, i ^ bit) for i in range(lax.axis_size(axis))])


EDGE = [(0, 1), (3, 2)]
MIDDLE = [(1, 2), (2, 1)]
OUTER = [(1, 0), (2, 3)]


def tp_sums(mine, *before):
    sums, bit = [mine], 1
    while True:
        other = swap(sums[-1], "tp", bit)
        bit *= 2
        if bit >= lax.axis_size("tp"):
            return sums, other
        sums.append(both(after(sums[-1], *before), other))


def shards(x, ids, table, weight, down, up):
    holders = lax.axis_size("ad")
    capacity = x.shape[0] // 4
    slots = up.shape[0] // ADAPTER_RANK
    width = up.shape[1]
    total = holders * capacity
    me, z = lax.axis_index("ad"), lax.axis_index("tp")
    place, *send, x, w = sort_rows(me, z, ids, table, x, weight, holders, slots, capacity, width)
    parts = [send[0]] + [swap(send[j], "ad", j) for j in range(1, holders)]
    if lax.axis_size("tp") == 4:
        first = first_block(x, w)
        edge0 = [lax.ppermute(f, "tp", EDGE) for f in first]
        second, *third, own, unsort = rest(z, after(place, parts[1], *first), x, weight, width, total)
        edge1 = lax.ppermute(second, "tp", EDGE)
        inner0 = [both(after(first[0], second), edge0[0])]
        early = shrink_partial(down, parts[:2] + [after(parts[2], *inner0)])
        inner0.append(both(after(first[1], early), edge0[1]))
        middle0 = [lax.ppermute(i, "tp", MIDDLE) for i in inner0]
        inner2 = [both(after(third[0], inner0[1]), middle0[0]), both(third[1], middle0[1])]
        outer = lax.ppermute(inner2[0], "tp", OUTER)
        mine = shrink_partial(down, [after(parts[-1], inner2[0])], [early])
        edge2 = lax.ppermute(after(third[0], mine), "tp", EDGE)
        inner1 = both(second, edge1)
        steps, other = tp_sums(mine, inner1, inner2[1], outer)
        middle1 = lax.ppermute(after(inner1, steps[-1]), "tp", MIDDLE)
        last = swap(after(inner2[1], steps[-1]), "tp", 1)
        other = after(other, edge2)
        sums, halves = [own, middle1], [(edge2, 0), (outer, 0), (last, 1)]
    else:
        unsort = unsort_only(place, total)
        full = dot(x, weight).astype(bf16)
        sums = [lax.psum_scatter(full, "tp", scatter_dimension=1, tiled=True)]
        halves = []
        steps, other = tp_sums(shrink_partial(down, parts))
    deltas = expand(steps[-1], other, up, parts)
    back = [deltas[0]] + [swap(deltas[j], "ad", j) for j in range(1, holders)]
    return finish(unsort, back, sums, halves)


def solution(mesh):
    in_specs = (
        P(("rep", "ad"), "tp"),
        P(("rep", "ad")),
        P("rep"),
        P("tp", None),
        P(("rep", "tp"), "ad"),
        P(("rep", "ad"), "tp"),
    )
    out_specs = P(("rep", "ad"), "tp")
    return jax.shard_map(shards, mesh=mesh, in_specs=in_specs, out_specs=out_specs, check_vma=False)
```

```python
import functools

import jax
import jax.numpy as jnp
from jax import lax
from jax.experimental import pallas as pl
from jax.experimental.pallas import tpu as pltpu
from jax.sharding import PartitionSpec as P

ADAPTER_RANK = 64
LANES = 128
VMEM_BYTES = 32 * 1024 * 1024

bf16 = jnp.bfloat16
f32 = jnp.float32
i32 = jnp.int32


def params():
    return pltpu.CompilerParams(vmem_limit_bytes=VMEM_BYTES)


def cost(flops, nbytes):
    return pl.CostEstimate(flops=flops, bytes_accessed=nbytes, transcendentals=0)


def dot(a, b, contract=((1,), (0,))):
    return lax.dot_general(a, b, (contract, ((), ())), preferred_element_type=f32)


def in_hbm(a):
    return pltpu.with_memory_space_constraint(a, pltpu.HBM)


def iota(shape, dim):
    return lax.broadcasted_iota(i32, shape, dim)


def places(slots, capacity, holders, me, ids, table):
    rows = ids.shape[1]
    low = (iota((LANES, rows), 0) == (ids & (LANES - 1))).astype(f32).astype(bf16)
    high = iota((table.shape[0], rows), 0) == lax.shift_right_logical(ids, 7)
    found = dot(table.astype(f32).astype(bf16), low)
    slot = jnp.sum(jnp.where(high, found, 0.0), axis=0, keepdims=True).astype(i32)
    holder = split_slot(slot, slots)
    tag = (slot - holder * slots + 1).astype(f32)
    partner = holder ^ me
    mine = iota((max(8, holders), rows), 0) == partner
    ones = mine.astype(f32)
    groups = [ones[:, k:k + LANES] for k in range(0, rows, LANES)]
    earlier = (iota((LANES, LANES), 0) < iota((LANES, LANES), 1)).astype(f32).astype(bf16)
    before = dot(jnp.concatenate(groups, axis=0).astype(bf16), earlier)
    count = ones.shape[0]
    ranks, passed = [], jnp.zeros((count, 1), f32)
    for k, group in enumerate(groups):
        ranks.append(jnp.sum(group * (before[k * count:(k + 1) * count] + passed), axis=0, keepdims=True))
        passed += jnp.sum(group, axis=1, keepdims=True)
    return partner * capacity + jnp.concatenate(ranks, axis=1).astype(i32), tag


def split_slot(slot, slots):
    if slots & (slots - 1):
        return lax.div(slot, slots)
    return lax.shift_right_logical(slot, slots.bit_length() - 1)


def sort_body(slots, capacity, holders, me_ref, z_ref, ids_hbm, table_hbm, x_hbm, w_hbm, place_ref, *refs):
    outs, (x_buf, w_buf, ids_buf, table_buf, small_sem, x_sem, w_sem) = refs[:holders], refs[holders:]
    rows, features = x_buf.shape
    width = w_buf.shape[1]
    chunks = x_sem.shape[0]
    step = features // chunks
    small = [
        pltpu.make_async_copy(ids_hbm, ids_buf, small_sem.at[0]),
        pltpu.make_async_copy(table_hbm, table_buf, small_sem.at[1]),
    ]
    copies = []
    for c in range(chunks):
        part = pl.ds(c * step, step)
        copies.append(pltpu.make_async_copy(x_hbm.at[:, part], x_buf.at[:, part], x_sem.at[c]))
    column = pl.multiple_of(jnp.where(z_ref[0] < 2, 3, 0) * width, width)
    w_copy = pltpu.make_async_copy(w_hbm.at[:, pl.ds(column, width)], w_buf, w_sem)
    for copy in small + copies + [w_copy]:
        copy.start()
    for copy in small:
        copy.wait()
    place, tag = places(slots, capacity, holders, me_ref[0], ids_buf[...], table_buf[...])
    place_ref[...] = jnp.broadcast_to(place, place_ref.shape)
    pick = (iota((holders * capacity, rows), 0) == place).astype(f32).astype(bf16)
    tags = dot(pick, jnp.broadcast_to(tag, (LANES, rows)).astype(bf16), ((1,), (1,))).astype(bf16)
    for j, out in enumerate(outs):
        out[:, features:] = tags[j * capacity:(j + 1) * capacity]
    for c in range(chunks):
        copies[c].wait()
        moved = dot(pick, x_buf[:, c * step:(c + 1) * step]).astype(bf16)
        for j, out in enumerate(outs):
            out[:, c * step:(c + 1) * step] = moved[j * capacity:(j + 1) * capacity]
    w_copy.wait()


def sort_rows(me, z, ids, table, x, weight, holders, slots, capacity, width):
    rows, features = x.shape
    ids, table = ids.reshape(1, rows), table.reshape(-1, LANES)
    chunks = max(1, features // 512)
    smem, vmem, hbm = (pl.BlockSpec(memory_space=m) for m in (pltpu.SMEM, pltpu.VMEM, pltpu.HBM))
    shapes = [jax.ShapeDtypeStruct((8, rows), i32)]
    shapes += [jax.ShapeDtypeStruct((capacity, features + LANES), bf16)] * holders
    shapes += [jax.ShapeDtypeStruct((rows, features), bf16), jax.ShapeDtypeStruct((features, width), bf16)]
    return pl.pallas_call(
        functools.partial(sort_body, slots, capacity, holders),
        out_shape=shapes,
        in_specs=[smem, smem, hbm, hbm, hbm, hbm],
        out_specs=[vmem] * len(shapes),
        scratch_shapes=[
            pltpu.VMEM(ids.shape, i32),
            pltpu.VMEM(table.shape, i32),
            pltpu.SemaphoreType.DMA((2,)),
            pltpu.SemaphoreType.DMA((chunks,)),
            pltpu.SemaphoreType.DMA(()),
        ],
        compiler_params=params(),
        cost_estimate=cost(2 * holders * capacity * rows * features, 4 * rows * features),
        name="sort_rows",
    )(me.reshape(1), z.reshape(1), in_hbm(ids), in_hbm(table), in_hbm(x), in_hbm(weight))


def first_body(x_ref, w_ref, *outs):
    half = outs[0].shape[0]
    for k, out in enumerate(outs):
        out[...] = dot(x_ref[k * half:(k + 1) * half, :], w_ref[...]).astype(bf16)


def first_block(x, w):
    (rows, features), width = x.shape, w.shape[1]
    return pl.pallas_call(
        first_body,
        out_shape=[jax.ShapeDtypeStruct((rows // 2, width), bf16)] * 2,
        compiler_params=params(),
        cost_estimate=cost(2 * rows * features * width, 2 * features * (rows + width)),
        name="first_block",
    )(x, w)


def rest_body(z_ref, place_ref, x_ref, w_hbm, *refs):
    *second, upper, lower, own, unsort, w_buf, sem = refs
    z = z_ref[0]
    width = own.shape[1]
    blocks = (jnp.where(z < 2, 2, 1), z ^ 1, z)
    copies = []
    for k, block in enumerate(blocks):
        column = pl.multiple_of(block * width, width)
        copies.append(pltpu.make_async_copy(w_hbm.at[:, pl.ds(column, width)], w_buf.at[k], sem.at[k]))
        copies[k].start()
    unsort_matrix(place_ref, unsort)
    for k, outs in enumerate((second, (upper, lower), (own,))):
        copies[k].wait()
        at = 0
        for out in outs:
            out[...] = dot(x_ref[at:at + out.shape[0], :], w_buf[k]).astype(bf16)
            at += out.shape[0]


def unsort_matrix(place_ref, unsort):
    rows, total = unsort.shape
    place = jnp.broadcast_to(place_ref[0:1, :].astype(f32), (LANES, rows)).T
    lane = iota((rows, LANES), 1).astype(f32)
    for k in range(total // LANES):
        unsort[:, k * LANES:(k + 1) * LANES] = (place == lane + float(k * LANES)).astype(f32).astype(bf16)


def rest(z, place, x, weight, width, total):
    rows, features = x.shape
    smem, vmem, hbm = (pl.BlockSpec(memory_space=m) for m in (pltpu.SMEM, pltpu.VMEM, pltpu.HBM))
    shapes = [jax.ShapeDtypeStruct((r, width), bf16) for r in (rows // 2, rows // 2, rows // 4, rows - rows // 4, rows)]
    shapes.append(jax.ShapeDtypeStruct((rows, total), bf16))
    return pl.pallas_call(
        rest_body,
        out_shape=shapes,
        in_specs=[smem, vmem, vmem, hbm],
        out_specs=[vmem] * len(shapes),
        scratch_shapes=[pltpu.VMEM((3, features, width), bf16), pltpu.SemaphoreType.DMA((3,))],
        compiler_params=params(),
        cost_estimate=cost(6 * rows * features * width, 2 * features * (rows + 4 * width)),
        name="rest",
    )(z.reshape(1), place, x, in_hbm(weight))


def unsort_only(place, total):
    return pl.pallas_call(
        unsort_matrix,
        out_shape=jax.ShapeDtypeStruct((place.shape[1], total), bf16),
        compiler_params=params(),
        name="unsort",
    )(place)


def slot_mask(tag, group):
    lane = iota(tag.shape, 1)
    return tag == jnp.where(lane < ADAPTER_RANK, 2 * group + 1, 2 * group + 2).astype(f32)


def shrink_body(kept, down_ref, *refs):
    parts, out = refs[1 if kept else 0:-1], refs[-1]
    features, width = down_ref.shape
    capacity = parts[0].shape[0]
    half = capacity // 2
    first = iota((half, LANES), 1) < ADAPTER_RANK
    if kept:
        out[:kept, :] = refs[0][...]
    for k, part in enumerate(parts):
        full = dot(part[:, :features], down_ref[...])
        tag = part[:, features:].astype(f32)
        total = jnp.zeros((capacity, LANES), f32)
        for group in range(width // LANES):
            total += jnp.where(slot_mask(tag, group), full[:, group * LANES:(group + 1) * LANES], 0.0)
        total += pltpu.roll(total, ADAPTER_RANK, 1)
        spot = slice(kept + k * half, kept + (k + 1) * half)
        out[spot, :] = jnp.where(first, total[:half], total[half:]).astype(bf16)


def shrink_partial(down, parts, done=()):
    features, width = down.shape
    capacity = parts[0].shape[0]
    total = len(parts) * capacity
    kept = sum(d.shape[0] for d in done)
    return pl.pallas_call(
        functools.partial(shrink_body, kept),
        out_shape=jax.ShapeDtypeStruct((kept + total // 2, LANES), bf16),
        compiler_params=params(),
        cost_estimate=cost(2 * total * features * width, 2 * features * (total + width)),
        name="shrink_partial",
    )(down, *done, *parts)


def expand_body(count, one_ref, two_ref, up_ref, *refs):
    tags, outs = refs[:count], refs[count:]
    capacity = outs[0].shape[0]
    half = capacity // 2
    up = up_ref[...]
    first = iota((half, LANES), 1) < ADAPTER_RANK
    for k in range(count):
        part = pl.ds(k * half, half)
        shrink = (one_ref[part, :].astype(f32) + two_ref[part, :].astype(f32)).astype(bf16).astype(f32)
        turned = pltpu.roll(shrink, ADAPTER_RANK, 1)
        rows = jnp.concatenate([jnp.where(first, shrink, turned), jnp.where(first, turned, shrink)], axis=0)
        tag = tags[k][...].astype(f32)
        spread = [
            jnp.where(slot_mask(tag, group), rows, 0.0).astype(bf16) for group in range(up.shape[0] // LANES)
        ]
        outs[k][...] = dot(jnp.concatenate(spread, axis=1), up).astype(bf16)


def expand(one, two, up, parts):
    capacity, width = parts[0].shape
    count = len(parts)
    tag_block = pl.BlockSpec((capacity, LANES), lambda i: (0, width // LANES - 1))
    whole = lambda a: pl.BlockSpec(a.shape, lambda i: (0, 0))
    columns = up.shape[1]
    return pl.pallas_call(
        functools.partial(expand_body, count),
        grid=(1,),
        out_shape=[jax.ShapeDtypeStruct((capacity, columns), bf16)] * count,
        in_specs=[whole(one), whole(two), whole(up)] + [tag_block] * count,
        out_specs=[pl.BlockSpec((capacity, columns), lambda i: (0, 0))] * count,
        compiler_params=params(),
        cost_estimate=cost(80 * count * capacity * up.size, 80 * (up.size + count * capacity * columns)),
        name="expand",
    )(one, two, up, *parts)


def finish_body(count, pieces, unsort_ref, *refs):
    deltas, rest, out = refs[:count], refs[count:-1], refs[-1]
    rows = out.shape[0]
    step = rows // 4
    sorted_deltas = jnp.concatenate([d[...] for d in deltas], axis=0)
    for start in range(0, rows, step):
        total = dot(unsort_ref[start:start + step, :], sorted_deltas)
        base, at = None, 0
        for number in pieces:
            first = start
            for ref in rest[at:at + number]:
                if 0 <= first < ref.shape[0]:
                    term = ref[first:first + step, :].astype(f32)
                    base = term if base is None else base + term
                first -= ref.shape[0]
            at += number
        out[start:start + step, :] = (base + total).astype(bf16)


def finish(unsort, deltas, terms):
    rows, total = unsort.shape
    columns = deltas[0].shape[1]
    return pl.pallas_call(
        functools.partial(finish_body, len(deltas), [len(t) for t in terms]),
        out_shape=jax.ShapeDtypeStruct((rows, columns), bf16),
        compiler_params=params(),
        cost_estimate=cost(2 * rows * total * columns, 12 * rows * columns),
        name="finish",
    )(unsort, *deltas, *[piece for t in terms for piece in t])


def both(a, b):
    return (a.astype(f32) + b.astype(f32)).astype(bf16)


def after(value, *others):
    return lax.optimization_barrier((value,) + others)[0]


def swap(value, axis, bit):
    return lax.ppermute(value, axis, [(i, i ^ bit) for i in range(lax.axis_size(axis))])


EDGE = [(0, 1), (3, 2)]
MIDDLE = [(1, 2), (2, 1)]
OUTER = [(1, 0), (2, 3)]


def tp_sums(mine, *before):
    sums, bit = [mine], 1
    while True:
        other = swap(sums[-1], "tp", bit)
        bit *= 2
        if bit >= lax.axis_size("tp"):
            return sums, other
        sums.append(both(after(sums[-1], *before), other))


def shards(x, ids, table, weight, down, up):
    holders = lax.axis_size("ad")
    capacity = x.shape[0] // 4
    slots = up.shape[0] // ADAPTER_RANK
    width = up.shape[1]
    total = holders * capacity
    me, z = lax.axis_index("ad"), lax.axis_index("tp")
    place, *send, x, w = sort_rows(me, z, ids, table, x, weight, holders, slots, capacity, width)
    parts = [send[0]] + [swap(send[j], "ad", j) for j in range(1, holders)]
    if lax.axis_size("tp") == 4:
        first = first_block(x, w)
        edge0 = [lax.ppermute(f, "tp", EDGE) for f in first]
        *blocks, own, unsort = rest(z, after(place, parts[1], *first), x, weight, width, total)
        second, third = blocks[:2], blocks[2:]
        edge1 = [lax.ppermute(s, "tp", EDGE) for s in second]
        inner0 = [both(after(first[0], own), edge0[0])]
        early = shrink_partial(down, parts[:2] + [after(parts[2], *inner0)])
        inner0.append(both(after(first[1], early), edge0[1]))
        middle0 = [lax.ppermute(i, "tp", MIDDLE) for i in inner0]
        quarter = third[0].shape[0]
        inner2 = [both(after(third[0], inner0[1]), middle0[0][:quarter])]
        outer = lax.ppermute(inner2[0], "tp", OUTER)
        inner1 = [both(after(second[0], inner2[0]), edge1[0])]
        middle1 = [lax.ppermute(inner1[0], "tp", MIDDLE)]
        mine = shrink_partial(down, [after(parts[-1], *inner1)], [early])
        edge2 = lax.ppermute(after(third[0], mine), "tp", EDGE)
        inner1.append(both(second[1], edge1[1]))
        inner2.append(both(third[1], jnp.concatenate([middle0[0][quarter:], middle0[1]], axis=0)))
        steps, other = tp_sums(mine, inner1[1], inner2[1], outer)
        last = swap(after(inner2[1], steps[-1]), "tp", 1)
        middle1.append(lax.ppermute(after(inner1[1], steps[-1], middle1[0]), "tp", MIDDLE))
        other = after(other, edge2)
        sums = [[own], middle1, [edge2, last], [outer]]
    else:
        unsort = unsort_only(place, total)
        full = dot(x, weight).astype(bf16)
        sums = [[lax.psum_scatter(full, "tp", scatter_dimension=1, tiled=True)]]
        steps, other = tp_sums(shrink_partial(down, parts))
    deltas = expand(steps[-1], other, up, parts)
    back = [deltas[0]] + [swap(deltas[j], "ad", j) for j in range(1, holders)]
    return finish(unsort, back, sums)


def solution(mesh):
    in_specs = (
        P(("rep", "ad"), "tp"),
        P(("rep", "ad")),
        P("rep"),
        P("tp", None),
        P(("rep", "tp"), "ad"),
        P(("rep", "ad"), "tp"),
    )
    out_specs = P(("rep", "ad"), "tp")
    return jax.shard_map(shards, mesh=mesh, in_specs=in_specs, out_specs=out_specs, check_vma=False)
```

```python
import functools

import jax
import jax.numpy as jnp
from jax import lax
from jax.experimental import pallas as pl
from jax.experimental.pallas import tpu as pltpu
from jax.sharding import PartitionSpec as P

ADAPTER_RANK = 64
LANES = 128
NEAR = 2
VMEM_BYTES = 32 * 1024 * 1024

bf16 = jnp.bfloat16
f32 = jnp.float32
i32 = jnp.int32


def params():
    return pltpu.CompilerParams(vmem_limit_bytes=VMEM_BYTES)


def cost(flops, nbytes):
    return pl.CostEstimate(flops=flops, bytes_accessed=nbytes, transcendentals=0)


def dot(a, b, contract=((1,), (0,))):
    return lax.dot_general(a, b, (contract, ((), ())), preferred_element_type=f32)


def in_hbm(a):
    return pltpu.with_memory_space_constraint(a, pltpu.HBM)


def iota(shape, dim):
    return lax.broadcasted_iota(i32, shape, dim)


def places(slots, capacity, holders, me, ids, table):
    rows = ids.shape[1]
    low = (iota((LANES, rows), 0) == (ids & (LANES - 1))).astype(f32).astype(bf16)
    high = iota((table.shape[0], rows), 0) == lax.shift_right_logical(ids, 7)
    found = dot(table.astype(f32).astype(bf16), low)
    slot = jnp.sum(jnp.where(high, found, 0.0), axis=0, keepdims=True).astype(i32)
    holder = split_slot(slot, slots)
    tag = (slot - holder * slots + 1).astype(f32)
    partner = holder ^ me
    mine = iota((max(8, holders), rows), 0) == partner
    ones = mine.astype(f32)
    groups = [ones[:, k:k + LANES] for k in range(0, rows, LANES)]
    earlier = (iota((LANES, LANES), 0) < iota((LANES, LANES), 1)).astype(f32).astype(bf16)
    before = dot(jnp.concatenate(groups, axis=0).astype(bf16), earlier)
    count = ones.shape[0]
    ranks, passed = [], jnp.zeros((count, 1), f32)
    for k, group in enumerate(groups):
        ranks.append(jnp.sum(group * (before[k * count:(k + 1) * count] + passed), axis=0, keepdims=True))
        passed += jnp.sum(group, axis=1, keepdims=True)
    return partner * capacity + jnp.concatenate(ranks, axis=1).astype(i32), tag


def split_slot(slot, slots):
    if slots & (slots - 1):
        return lax.div(slot, slots)
    return lax.shift_right_logical(slot, slots.bit_length() - 1)


def pick_rows(start, place, tag, x, outs):
    rows, features = x.shape
    capacity = outs[0].shape[0]
    pick = iota((len(outs) * capacity, rows), 0) + start * capacity == place
    pick = pick.astype(f32).astype(bf16)
    tags = dot(pick, jnp.broadcast_to(tag, (LANES, rows)).astype(bf16), ((1,), (1,))).astype(bf16)
    step = min(512, features)
    for c in range(0, features, step):
        moved = dot(pick, x[:, c:c + step]).astype(bf16)
        for j, out in enumerate(outs):
            out[:, c:c + step] = moved[j * capacity:(j + 1) * capacity]
    for j, out in enumerate(outs):
        out[:, features:] = tags[j * capacity:(j + 1) * capacity]


def far_body(slots, capacity, holders, me_ref, z_ref, ids_hbm, table_hbm, x_hbm, w_hbm, places_ref, *refs):
    outs, (x_buf, w_buf, ids_buf, table_buf, small_sem, x_sem, w_sem) = refs[:holders - NEAR], refs[holders - NEAR:]
    width = w_buf.shape[1]
    small = [
        pltpu.make_async_copy(ids_hbm, ids_buf, small_sem.at[0]),
        pltpu.make_async_copy(table_hbm, table_buf, small_sem.at[1]),
    ]
    x_copy = pltpu.make_async_copy(x_hbm, x_buf, x_sem)
    column = pl.multiple_of(jnp.where(z_ref[0] < 2, 3, 0) * width, width)
    w_copy = pltpu.make_async_copy(w_hbm.at[:, pl.ds(column, width)], w_buf, w_sem)
    for copy in small + [x_copy, w_copy]:
        copy.start()
    for copy in small:
        copy.wait()
    place, tag = places(slots, capacity, holders, me_ref[0], ids_buf[...], table_buf[...])
    row = iota(places_ref.shape, 0)
    places_ref[...] = jnp.where(row == 0, place, jnp.where(row == 1, tag.astype(i32), 0))
    x_copy.wait()
    pick_rows(NEAR, place, tag, x_buf, outs)
    w_copy.wait()


def far_rows(me, z, ids, table, x, weight, holders, slots, capacity, width):
    rows, features = x.shape
    ids, table = ids.reshape(1, rows), table.reshape(-1, LANES)
    smem, vmem, hbm = (pl.BlockSpec(memory_space=m) for m in (pltpu.SMEM, pltpu.VMEM, pltpu.HBM))
    shapes = [jax.ShapeDtypeStruct((8, rows), i32)]
    shapes += [jax.ShapeDtypeStruct((capacity, features + LANES), bf16)] * (holders - NEAR)
    shapes += [jax.ShapeDtypeStruct((rows, features), bf16), jax.ShapeDtypeStruct((features, width), bf16)]
    return pl.pallas_call(
        functools.partial(far_body, slots, capacity, holders),
        out_shape=shapes,
        in_specs=[smem, smem, hbm, hbm, hbm, hbm],
        out_specs=[vmem] * len(shapes),
        scratch_shapes=[
            pltpu.VMEM(ids.shape, i32),
            pltpu.VMEM(table.shape, i32),
            pltpu.SemaphoreType.DMA((2,)),
            pltpu.SemaphoreType.DMA(()),
            pltpu.SemaphoreType.DMA(()),
        ],
        compiler_params=params(),
        cost_estimate=cost(2 * holders * capacity * rows * features, 4 * rows * features),
        name="far_rows",
    )(me.reshape(1), z.reshape(1), in_hbm(ids), in_hbm(table), in_hbm(x), in_hbm(weight))


def near_body(places_ref, x_ref, *outs):
    pick_rows(0, places_ref[0:1, :], places_ref[1:2, :].astype(f32), x_ref, outs)


def near_rows(spots, x, capacity):
    rows, features = x.shape
    return pl.pallas_call(
        near_body,
        out_shape=[jax.ShapeDtypeStruct((capacity, features + LANES), bf16)] * NEAR,
        compiler_params=params(),
        cost_estimate=cost(2 * NEAR * capacity * rows * features, 4 * rows * features),
        name="near_rows",
    )(spots, x)


def first_body(x_ref, w_ref, out):
    out[...] = dot(x_ref[...], w_ref[...]).astype(bf16)


def first_block(x, w):
    (rows, features), width = x.shape, w.shape[1]
    return pl.pallas_call(
        first_body,
        out_shape=jax.ShapeDtypeStruct((rows, width), bf16),
        compiler_params=params(),
        cost_estimate=cost(2 * rows * features * width, 2 * features * (rows + width)),
        name="first_block",
    )(x, w)


def rest_body(z_ref, spots_ref, x_ref, w_hbm, *refs):
    near, (second, third, own, unsort, w_buf, sem) = refs[:NEAR], refs[NEAR:]
    z = z_ref[0]
    width = own.shape[1]
    copies = []
    for k, block in enumerate((jnp.where(z < 2, 2, 1), z ^ 1, z)):
        column = pl.multiple_of(block * width, width)
        copies.append(pltpu.make_async_copy(w_hbm.at[:, pl.ds(column, width)], w_buf.at[k], sem.at[k]))
        copies[k].start()
    near_body(spots_ref, x_ref, *near)
    unsort_matrix(spots_ref, unsort)
    for k, out in enumerate((second, third, own)):
        copies[k].wait()
        out[...] = dot(x_ref[...], w_buf[k]).astype(bf16)


def unsort_matrix(place_ref, unsort):
    rows, total = unsort.shape
    place = jnp.broadcast_to(place_ref[0:1, :].astype(f32), (LANES, rows)).T
    lane = iota((rows, LANES), 1).astype(f32)
    for k in range(total // LANES):
        unsort[:, k * LANES:(k + 1) * LANES] = (place == lane + float(k * LANES)).astype(f32).astype(bf16)


def rest(z, spots, x, weight, width, total, capacity):
    rows, features = x.shape
    smem, vmem, hbm = (pl.BlockSpec(memory_space=m) for m in (pltpu.SMEM, pltpu.VMEM, pltpu.HBM))
    shapes = [jax.ShapeDtypeStruct((capacity, features + LANES), bf16)] * NEAR
    shapes += [jax.ShapeDtypeStruct((rows, width), bf16)] * 3 + [jax.ShapeDtypeStruct((rows, total), bf16)]
    return pl.pallas_call(
        rest_body,
        out_shape=shapes,
        in_specs=[smem, vmem, vmem, hbm],
        out_specs=[vmem] * len(shapes),
        scratch_shapes=[pltpu.VMEM((3, features, width), bf16), pltpu.SemaphoreType.DMA((3,))],
        compiler_params=params(),
        cost_estimate=cost(6 * rows * features * width, 2 * features * (rows + 4 * width)),
        name="rest",
    )(z.reshape(1), spots, x, in_hbm(weight))


def unsort_only(place, total):
    return pl.pallas_call(
        unsort_matrix,
        out_shape=jax.ShapeDtypeStruct((place.shape[1], total), bf16),
        compiler_params=params(),
        name="unsort",
    )(place)


def slot_mask(tag, group):
    lane = iota(tag.shape, 1)
    return tag == jnp.where(lane < ADAPTER_RANK, 2 * group + 1, 2 * group + 2).astype(f32)


def shrink_body(kept, down_ref, *refs):
    parts, out = refs[1 if kept else 0:-1], refs[-1]
    features, width = down_ref.shape
    capacity = parts[0].shape[0]
    half = capacity // 2
    first = iota((half, LANES), 1) < ADAPTER_RANK
    if kept:
        out[:kept, :] = refs[0][...]
    for k, part in enumerate(parts):
        full = dot(part[:, :features], down_ref[...])
        tag = part[:, features:].astype(f32)
        total = jnp.zeros((capacity, LANES), f32)
        for group in range(width // LANES):
            total += jnp.where(slot_mask(tag, group), full[:, group * LANES:(group + 1) * LANES], 0.0)
        total += pltpu.roll(total, ADAPTER_RANK, 1)
        spot = slice(kept + k * half, kept + (k + 1) * half)
        out[spot, :] = jnp.where(first, total[:half], total[half:]).astype(bf16)


def shrink_partial(down, parts, done=()):
    features, width = down.shape
    capacity = parts[0].shape[0]
    total = len(parts) * capacity
    kept = sum(d.shape[0] for d in done)
    return pl.pallas_call(
        functools.partial(shrink_body, kept),
        out_shape=jax.ShapeDtypeStruct((kept + total // 2, LANES), bf16),
        compiler_params=params(),
        cost_estimate=cost(2 * total * features * width, 2 * features * (total + width)),
        name="shrink_partial",
    )(down, *done, *parts)


def expand_body(count, one_ref, two_ref, up_ref, *refs):
    tags, outs = refs[:count], refs[count:]
    capacity = outs[0].shape[0]
    half = capacity // 2
    up = up_ref[...]
    first = iota((half, LANES), 1) < ADAPTER_RANK
    for k in range(count):
        part = pl.ds(k * half, half)
        shrink = (one_ref[part, :].astype(f32) + two_ref[part, :].astype(f32)).astype(bf16).astype(f32)
        turned = pltpu.roll(shrink, ADAPTER_RANK, 1)
        rows = jnp.concatenate([jnp.where(first, shrink, turned), jnp.where(first, turned, shrink)], axis=0)
        tag = tags[k][...].astype(f32)
        spread = [
            jnp.where(slot_mask(tag, group), rows, 0.0).astype(bf16) for group in range(up.shape[0] // LANES)
        ]
        outs[k][...] = dot(jnp.concatenate(spread, axis=1), up).astype(bf16)


def expand(one, two, up, parts):
    capacity, width = parts[0].shape
    count = len(parts)
    tag_block = pl.BlockSpec((capacity, LANES), lambda i: (0, width // LANES - 1))
    whole = lambda a: pl.BlockSpec(a.shape, lambda i: (0, 0))
    columns = up.shape[1]
    return pl.pallas_call(
        functools.partial(expand_body, count),
        grid=(1,),
        out_shape=[jax.ShapeDtypeStruct((capacity, columns), bf16)] * count,
        in_specs=[whole(one), whole(two), whole(up)] + [tag_block] * count,
        out_specs=[pl.BlockSpec((capacity, columns), lambda i: (0, 0))] * count,
        compiler_params=params(),
        cost_estimate=cost(80 * count * capacity * up.size, 80 * (up.size + count * capacity * columns)),
        name="expand",
    )(one, two, up, *parts)


def finish_body(count, unsort_ref, *refs):
    deltas, sums, out = refs[:count], refs[count:-1], refs[-1]
    base = sums[0][...].astype(f32)
    for term in sums[1:]:
        base += term[...].astype(f32)
    out[...] = (base + dot(unsort_ref[...], jnp.concatenate([d[...] for d in deltas], axis=0))).astype(bf16)


def finish(unsort, deltas, sums):
    rows, columns = sums[0].shape
    return pl.pallas_call(
        functools.partial(finish_body, len(deltas)),
        out_shape=jax.ShapeDtypeStruct((rows, columns), bf16),
        compiler_params=params(),
        cost_estimate=cost(2 * rows * unsort.shape[1] * columns, 12 * rows * columns),
        name="finish",
    )(unsort, *deltas, *sums)


def both(a, b):
    return (a.astype(f32) + b.astype(f32)).astype(bf16)


def after(value, *others):
    return lax.optimization_barrier((value,) + others)[0]


def swap(value, axis, bit):
    return lax.ppermute(value, axis, [(i, i ^ bit) for i in range(lax.axis_size(axis))])


EDGE = [(0, 1), (3, 2)]
MIDDLE = [(1, 2), (2, 1)]


def tp_sums(mine, *before):
    sums, bit = [mine], 1
    while True:
        other = swap(sums[-1], "tp", bit)
        bit *= 2
        if bit >= lax.axis_size("tp"):
            return sums, other
        sums.append(both(after(sums[-1], *before), other))


def shards(x, ids, table, weight, down, up):
    holders = lax.axis_size("ad")
    capacity = x.shape[0] // 4
    slots = up.shape[0] // ADAPTER_RANK
    width = up.shape[1]
    total = holders * capacity
    me, z = lax.axis_index("ad"), lax.axis_index("tp")
    spots, *far, x, w = far_rows(me, z, ids, table, x, weight, holders, slots, capacity, width)
    far = [swap(rows, "ad", j + NEAR) for j, rows in enumerate(far)]
    if lax.axis_size("tp") == 4 and holders == 4:
        first = first_block(x, w)
        edge0 = lax.ppermute(first, "tp", EDGE)
        *near, second, third, own, unsort = rest(z, after(spots, first), x, weight, width, total, capacity)
        near = [near[0], swap(near[1], "ad", 1)]
        edge1 = lax.ppermute(second, "tp", EDGE)
        early = shrink_partial(down, [near[0], far[0]])
        inner0 = both(after(first, early), edge0)
        middle0 = lax.ppermute(inner0, "tp", MIDDLE)
        early = shrink_partial(down, [after(near[1], inner0)], [early])
        mine = shrink_partial(down, [after(far[1], early)], [early])
        parts, order = [near[0], far[0], near[1], far[1]], (0, 2, 1, 3)
        inner1, inner2 = both(after(second, mine), edge1), both(third, middle0)
        steps, other = tp_sums(mine, inner1, inner2)
        last = swap(after(inner2, steps[-1]), "tp", 1)
        middle1 = lax.ppermute(after(inner1, steps[-1]), "tp", MIDDLE)
        sums = [own, middle1, last]
    else:
        near = near_rows(spots, x, capacity)
        near = [near[0], swap(near[1], "ad", 1)]
        parts, order = near + far, range(holders)
        unsort = unsort_only(spots, total)
        full = dot(x, weight).astype(bf16)
        sums = [lax.psum_scatter(full, "tp", scatter_dimension=1, tiled=True)]
        steps, other = tp_sums(shrink_partial(down, parts))
    deltas = expand(steps[-1], other, up, parts)
    back = [None] * holders
    for j, delta in zip(order, deltas):
        back[j] = swap(delta, "ad", j) if j else delta
    return finish(unsort, back, sums)


def solution(mesh):
    in_specs = (
        P(("rep", "ad"), "tp"),
        P(("rep", "ad")),
        P("rep"),
        P("tp", None),
        P(("rep", "tp"), "ad"),
        P(("rep", "ad"), "tp"),
    )
    out_specs = P(("rep", "ad"), "tp")
    return jax.shard_map(shards, mesh=mesh, in_specs=in_specs, out_specs=out_specs, check_vma=False)
```

```python
import functools

import jax
import jax.numpy as jnp
from jax import lax
from jax.experimental import pallas as pl
from jax.experimental.pallas import tpu as pltpu
from jax.sharding import PartitionSpec as P

ADAPTER_RANK = 64
LANES = 128
NEAR = 2
VMEM_BYTES = 32 * 1024 * 1024

bf16 = jnp.bfloat16
f32 = jnp.float32
i32 = jnp.int32


def params():
    return pltpu.CompilerParams(vmem_limit_bytes=VMEM_BYTES)


def cost(flops, nbytes):
    return pl.CostEstimate(flops=flops, bytes_accessed=nbytes, transcendentals=0)


def dot(a, b, contract=((1,), (0,))):
    return lax.dot_general(a, b, (contract, ((), ())), preferred_element_type=f32)


def in_hbm(a):
    return pltpu.with_memory_space_constraint(a, pltpu.HBM)


def iota(shape, dim):
    return lax.broadcasted_iota(i32, shape, dim)


def places(slots, capacity, holders, me, ids, table):
    rows = ids.shape[1]
    low = (iota((LANES, rows), 0) == (ids & (LANES - 1))).astype(f32).astype(bf16)
    high = iota((table.shape[0], rows), 0) == lax.shift_right_logical(ids, 7)
    found = dot(table.astype(f32).astype(bf16), low)
    slot = jnp.sum(jnp.where(high, found, 0.0), axis=0, keepdims=True).astype(i32)
    holder = split_slot(slot, slots)
    tag = (slot - holder * slots + 1).astype(f32)
    partner = holder ^ me
    mine = iota((max(8, holders), rows), 0) == partner
    ones = mine.astype(f32)
    groups = [ones[:, k:k + LANES] for k in range(0, rows, LANES)]
    earlier = (iota((LANES, LANES), 0) < iota((LANES, LANES), 1)).astype(f32).astype(bf16)
    before = dot(jnp.concatenate(groups, axis=0).astype(bf16), earlier)
    count = ones.shape[0]
    ranks, passed = [], jnp.zeros((count, 1), f32)
    for k, group in enumerate(groups):
        ranks.append(jnp.sum(group * (before[k * count:(k + 1) * count] + passed), axis=0, keepdims=True))
        passed += jnp.sum(group, axis=1, keepdims=True)
    return partner * capacity + jnp.concatenate(ranks, axis=1).astype(i32), tag


def split_slot(slot, slots):
    if slots & (slots - 1):
        return lax.div(slot, slots)
    return lax.shift_right_logical(slot, slots.bit_length() - 1)


def pick_rows(start, place, tag, x, outs):
    rows, features = x.shape
    capacity = outs[0].shape[0]
    pick = iota((len(outs) * capacity, rows), 0) + start * capacity == place
    pick = pick.astype(f32).astype(bf16)
    tags = dot(pick, jnp.broadcast_to(tag, (LANES, rows)).astype(bf16), ((1,), (1,))).astype(bf16)
    step = min(512, features)
    for c in range(0, features, step):
        moved = dot(pick, x[:, c:c + step]).astype(bf16)
        for j, out in enumerate(outs):
            out[:, c:c + step] = moved[j * capacity:(j + 1) * capacity]
    for j, out in enumerate(outs):
        out[:, features:] = tags[j * capacity:(j + 1) * capacity]


def far_body(slots, capacity, holders, me_ref, z_ref, ids_hbm, table_hbm, x_hbm, w_hbm, places_ref, *refs):
    outs, (x_buf, w_buf, ids_buf, table_buf, small_sem, x_sem, w_sem) = refs[:holders - NEAR], refs[holders - NEAR:]
    width = w_buf.shape[1]
    small = [
        pltpu.make_async_copy(ids_hbm, ids_buf, small_sem.at[0]),
        pltpu.make_async_copy(table_hbm, table_buf, small_sem.at[1]),
    ]
    x_copy = pltpu.make_async_copy(x_hbm, x_buf, x_sem)
    column = pl.multiple_of(jnp.where(z_ref[0] < 2, 3, 0) * width, width)
    w_copy = pltpu.make_async_copy(w_hbm.at[:, pl.ds(column, width)], w_buf, w_sem)
    for copy in small + [x_copy, w_copy]:
        copy.start()
    for copy in small:
        copy.wait()
    place, tag = places(slots, capacity, holders, me_ref[0], ids_buf[...], table_buf[...])
    row = iota(places_ref.shape, 0)
    places_ref[...] = jnp.where(row == 0, place, jnp.where(row == 1, tag.astype(i32), 0))
    x_copy.wait()
    pick_rows(NEAR, place, tag, x_buf, outs)
    w_copy.wait()


def far_rows(me, z, ids, table, x, weight, holders, slots, capacity, width):
    rows, features = x.shape
    ids, table = ids.reshape(1, rows), table.reshape(-1, LANES)
    smem, vmem, hbm = (pl.BlockSpec(memory_space=m) for m in (pltpu.SMEM, pltpu.VMEM, pltpu.HBM))
    shapes = [jax.ShapeDtypeStruct((8, rows), i32)]
    shapes += [jax.ShapeDtypeStruct((capacity, features + LANES), bf16)] * (holders - NEAR)
    shapes += [jax.ShapeDtypeStruct((rows, features), bf16), jax.ShapeDtypeStruct((features, width), bf16)]
    return pl.pallas_call(
        functools.partial(far_body, slots, capacity, holders),
        out_shape=shapes,
        in_specs=[smem, smem, hbm, hbm, hbm, hbm],
        out_specs=[vmem] * len(shapes),
        scratch_shapes=[
            pltpu.VMEM(ids.shape, i32),
            pltpu.VMEM(table.shape, i32),
            pltpu.SemaphoreType.DMA((2,)),
            pltpu.SemaphoreType.DMA(()),
            pltpu.SemaphoreType.DMA(()),
        ],
        compiler_params=params(),
        cost_estimate=cost(2 * holders * capacity * rows * features, 4 * rows * features),
        name="far_rows",
    )(me.reshape(1), z.reshape(1), in_hbm(ids), in_hbm(table), in_hbm(x), in_hbm(weight))


def near_body(places_ref, x_ref, *outs):
    pick_rows(0, places_ref[0:1, :], places_ref[1:2, :].astype(f32), x_ref, outs)


def near_rows(spots, x, capacity):
    rows, features = x.shape
    return pl.pallas_call(
        near_body,
        out_shape=[jax.ShapeDtypeStruct((capacity, features + LANES), bf16)] * NEAR,
        compiler_params=params(),
        cost_estimate=cost(2 * NEAR * capacity * rows * features, 4 * rows * features),
        name="near_rows",
    )(spots, x)


def first_body(x_ref, w_ref, out):
    out[...] = dot(x_ref[...], w_ref[...]).astype(bf16)


def first_block(x, w):
    (rows, features), width = x.shape, w.shape[1]
    return pl.pallas_call(
        first_body,
        out_shape=jax.ShapeDtypeStruct((rows, width), bf16),
        compiler_params=params(),
        cost_estimate=cost(2 * rows * features * width, 2 * features * (rows + width)),
        name="first_block",
    )(x, w)


def rest_body(z_ref, spots_ref, x_ref, w_hbm, *refs):
    near, (second, third, own, unsort, w_buf, sem) = refs[:NEAR], refs[NEAR:]
    z = z_ref[0]
    width = own.shape[1]
    copies = []
    for k, block in enumerate((jnp.where(z < 2, 2, 1), z ^ 1, z)):
        column = pl.multiple_of(block * width, width)
        copies.append(pltpu.make_async_copy(w_hbm.at[:, pl.ds(column, width)], w_buf.at[k], sem.at[k]))
        copies[k].start()
    near_body(spots_ref, x_ref, *near)
    unsort_matrix(spots_ref, unsort)
    for k, out in enumerate((second, third, own)):
        copies[k].wait()
        out[...] = dot(x_ref[...], w_buf[k]).astype(bf16)


def unsort_matrix(place_ref, unsort):
    rows, total = unsort.shape
    place = jnp.broadcast_to(place_ref[0:1, :].astype(f32), (LANES, rows)).T
    lane = iota((rows, LANES), 1).astype(f32)
    for k in range(total // LANES):
        unsort[:, k * LANES:(k + 1) * LANES] = (place == lane + float(k * LANES)).astype(f32).astype(bf16)


def rest(z, spots, x, weight, width, total, capacity):
    rows, features = x.shape
    smem, vmem, hbm = (pl.BlockSpec(memory_space=m) for m in (pltpu.SMEM, pltpu.VMEM, pltpu.HBM))
    shapes = [jax.ShapeDtypeStruct((capacity, features + LANES), bf16)] * NEAR
    shapes += [jax.ShapeDtypeStruct((rows, width), bf16)] * 3 + [jax.ShapeDtypeStruct((rows, total), bf16)]
    return pl.pallas_call(
        rest_body,
        out_shape=shapes,
        in_specs=[smem, vmem, vmem, hbm],
        out_specs=[vmem] * len(shapes),
        scratch_shapes=[pltpu.VMEM((3, features, width), bf16), pltpu.SemaphoreType.DMA((3,))],
        compiler_params=params(),
        cost_estimate=cost(6 * rows * features * width, 2 * features * (rows + 4 * width)),
        name="rest",
    )(z.reshape(1), spots, x, in_hbm(weight))


def unsort_only(place, total):
    return pl.pallas_call(
        unsort_matrix,
        out_shape=jax.ShapeDtypeStruct((place.shape[1], total), bf16),
        compiler_params=params(),
        name="unsort",
    )(place)


def slot_mask(tag, group):
    lane = iota(tag.shape, 1)
    return tag == jnp.where(lane < ADAPTER_RANK, 2 * group + 1, 2 * group + 2).astype(f32)


def shrink_body(kept, down_ref, *refs):
    parts, out = refs[1 if kept else 0:-1], refs[-1]
    features, width = down_ref.shape
    capacity = parts[0].shape[0]
    half = capacity // 2
    first = iota((half, LANES), 1) < ADAPTER_RANK
    if kept:
        out[:kept, :] = refs[0][...]
    for k, part in enumerate(parts):
        full = dot(part[:, :features], down_ref[...])
        tag = part[:, features:].astype(f32)
        total = jnp.zeros((capacity, LANES), f32)
        for group in range(width // LANES):
            total += jnp.where(slot_mask(tag, group), full[:, group * LANES:(group + 1) * LANES], 0.0)
        total += pltpu.roll(total, ADAPTER_RANK, 1)
        spot = slice(kept + k * half, kept + (k + 1) * half)
        out[spot, :] = jnp.where(first, total[:half], total[half:]).astype(bf16)


def shrink_partial(down, parts, done=()):
    features, width = down.shape
    capacity = parts[0].shape[0]
    total = len(parts) * capacity
    kept = sum(d.shape[0] for d in done)
    return pl.pallas_call(
        functools.partial(shrink_body, kept),
        out_shape=jax.ShapeDtypeStruct((kept + total // 2, LANES), bf16),
        compiler_params=params(),
        cost_estimate=cost(2 * total * features * width, 2 * features * (total + width)),
        name="shrink_partial",
    )(down, *done, *parts)


def expand_body(terms, up_ref, *refs):
    shares, refs = refs[:terms], refs[terms:]
    count = len(refs) // 2
    tags, outs = refs[:count], refs[count:]
    capacity = outs[0].shape[0]
    half = capacity // 2
    up = up_ref[...]
    first = iota((half, LANES), 1) < ADAPTER_RANK
    for k in range(count):
        part = pl.ds(k * half, half)
        shrink = shares[0][part, :].astype(f32)
        for share in shares[1:]:
            shrink += share[part, :].astype(f32)
        shrink = shrink.astype(bf16).astype(f32)
        turned = pltpu.roll(shrink, ADAPTER_RANK, 1)
        rows = jnp.concatenate([jnp.where(first, shrink, turned), jnp.where(first, turned, shrink)], axis=0)
        tag = tags[k][...].astype(f32)
        spread = [
            jnp.where(slot_mask(tag, group), rows, 0.0).astype(bf16) for group in range(up.shape[0] // LANES)
        ]
        outs[k][...] = dot(jnp.concatenate(spread, axis=1), up).astype(bf16)


def expand(shares, up, parts):
    capacity, width = parts[0].shape
    count = len(parts)
    tag_block = pl.BlockSpec((capacity, LANES), lambda i: (0, width // LANES - 1))
    whole = lambda a: pl.BlockSpec(a.shape, lambda i: (0, 0))
    columns = up.shape[1]
    return pl.pallas_call(
        functools.partial(expand_body, len(shares)),
        grid=(1,),
        out_shape=[jax.ShapeDtypeStruct((capacity, columns), bf16)] * count,
        in_specs=[whole(up)] + [whole(s) for s in shares] + [tag_block] * count,
        out_specs=[pl.BlockSpec((capacity, columns), lambda i: (0, 0))] * count,
        compiler_params=params(),
        cost_estimate=cost(80 * count * capacity * up.size, 80 * (up.size + count * capacity * columns)),
        name="expand",
    )(up, *shares, *parts)


def deltas_body(unsort_ref, own_ref, *refs):
    deltas, out = refs[:-1], refs[-1]
    placed = dot(unsort_ref[...], jnp.concatenate([d[...] for d in deltas], axis=0))
    out[...] = own_ref[...].astype(f32) + placed


def with_deltas(unsort, deltas, own):
    rows, columns = own.shape
    return pl.pallas_call(
        deltas_body,
        out_shape=jax.ShapeDtypeStruct((rows, columns), f32),
        compiler_params=params(),
        cost_estimate=cost(2 * rows * unsort.shape[1] * columns, 12 * rows * columns),
        name="with_deltas",
    )(unsort, own, *deltas)


def both(a, b):
    return (a.astype(f32) + b.astype(f32)).astype(bf16)


def after(value, *others):
    return lax.optimization_barrier((value,) + others)[0]


def swap(value, axis, bit):
    return lax.ppermute(value, axis, [(i, i ^ bit) for i in range(lax.axis_size(axis))])


EDGE = [(0, 1), (3, 2)]
MIDDLE = [(1, 2), (2, 1)]


def tp_sums(mine):
    sums, bit = [mine], 1
    while True:
        other = swap(sums[-1], "tp", bit)
        bit *= 2
        if bit >= lax.axis_size("tp"):
            return [sums[-1], other]
        sums.append(both(sums[-1], other))


def shards(x, ids, table, weight, down, up):
    holders = lax.axis_size("ad")
    capacity = x.shape[0] // 4
    slots = up.shape[0] // ADAPTER_RANK
    width = up.shape[1]
    total = holders * capacity
    me, z = lax.axis_index("ad"), lax.axis_index("tp")
    spots, *far, x, w = far_rows(me, z, ids, table, x, weight, holders, slots, capacity, width)
    far = [swap(rows, "ad", j + NEAR) for j, rows in enumerate(far)]
    if lax.axis_size("tp") == 4 and holders == 4:
        first = first_block(x, w)
        edge0 = lax.ppermute(first, "tp", EDGE)
        *near, second, third, own, unsort = rest(z, after(spots, first), x, weight, width, total, capacity)
        near = [near[0], swap(near[1], "ad", 1)]
        edge1 = lax.ppermute(second, "tp", EDGE)
        early = shrink_partial(down, [near[0], far[0]])
        inner0 = both(after(first, early), edge0)
        middle0 = lax.ppermute(inner0, "tp", MIDDLE)
        early = shrink_partial(down, [after(near[1], inner0)], [early])
        mine = shrink_partial(down, [after(far[1], early)], [early])
        parts, order = [near[0], far[0], near[1], far[1]], (0, 2, 1, 3)
        shares = [mine] + [swap(mine, "tp", bit) for bit in (2, 3, 1)]
        middle1 = lax.ppermute(both(after(second, mine), edge1), "tp", MIDDLE)
        last = swap(both(after(third, mine), middle0), "tp", 1)
        sums = [middle1, last]
    else:
        near = near_rows(spots, x, capacity)
        near = [near[0], swap(near[1], "ad", 1)]
        parts, order = near + far, range(holders)
        unsort = unsort_only(spots, total)
        full = dot(x, weight).astype(bf16)
        own, sums = lax.psum_scatter(full, "tp", scatter_dimension=1, tiled=True), []
        shares = tp_sums(shrink_partial(down, parts))
    deltas = expand(shares, up, parts)
    back = [None] * holders
    for j, delta in zip(order, deltas):
        back[j] = swap(delta, "ad", j) if j else delta
    total = with_deltas(unsort, back, own)
    for term in sums:
        total += term.astype(f32)
    return total.astype(bf16)


def solution(mesh):
    in_specs = (
        P(("rep", "ad"), "tp"),
        P(("rep", "ad")),
        P("rep"),
        P("tp", None),
        P(("rep", "tp"), "ad"),
        P(("rep", "ad"), "tp"),
    )
    out_specs = P(("rep", "ad"), "tp")
    return jax.shard_map(shards, mesh=mesh, in_specs=in_specs, out_specs=out_specs, check_vma=False)
```

```python
import functools

import jax
import jax.numpy as jnp
from jax import lax
from jax.experimental import pallas as pl
from jax.experimental.pallas import tpu as pltpu
from jax.sharding import PartitionSpec as P

ADAPTER_RANK = 64
LANES = 128
NEAR = 2
VMEM_BYTES = 32 * 1024 * 1024

bf16 = jnp.bfloat16
f32 = jnp.float32
i32 = jnp.int32


def params():
    return pltpu.CompilerParams(vmem_limit_bytes=VMEM_BYTES)


def cost(flops, nbytes):
    return pl.CostEstimate(flops=flops, bytes_accessed=nbytes, transcendentals=0)


def dot(a, b, contract=((1,), (0,))):
    return lax.dot_general(a, b, (contract, ((), ())), preferred_element_type=f32)


def in_hbm(a):
    return pltpu.with_memory_space_constraint(a, pltpu.HBM)


def iota(shape, dim):
    return lax.broadcasted_iota(i32, shape, dim)


def places(slots, capacity, holders, me, ids, table):
    rows = ids.shape[1]
    low = (iota((LANES, rows), 0) == (ids & (LANES - 1))).astype(f32).astype(bf16)
    high = iota((table.shape[0], rows), 0) == lax.shift_right_logical(ids, 7)
    found = dot(table.astype(f32).astype(bf16), low)
    slot = jnp.sum(jnp.where(high, found, 0.0), axis=0, keepdims=True).astype(i32)
    holder = split_slot(slot, slots)
    tag = (slot - holder * slots + 1).astype(f32)
    partner = holder ^ me
    mine = iota((max(8, holders), rows), 0) == partner
    ones = mine.astype(f32)
    groups = [ones[:, k:k + LANES] for k in range(0, rows, LANES)]
    earlier = (iota((LANES, LANES), 0) < iota((LANES, LANES), 1)).astype(f32).astype(bf16)
    before = dot(jnp.concatenate(groups, axis=0).astype(bf16), earlier)
    count = ones.shape[0]
    ranks, passed = [], jnp.zeros((count, 1), f32)
    for k, group in enumerate(groups):
        ranks.append(jnp.sum(group * (before[k * count:(k + 1) * count] + passed), axis=0, keepdims=True))
        passed += jnp.sum(group, axis=1, keepdims=True)
    return partner * capacity + jnp.concatenate(ranks, axis=1).astype(i32), tag


def split_slot(slot, slots):
    if slots & (slots - 1):
        return lax.div(slot, slots)
    return lax.shift_right_logical(slot, slots.bit_length() - 1)


def pick_rows(start, place, tag, x, outs):
    rows, features = x.shape
    capacity = outs[0].shape[0]
    pick = iota((len(outs) * capacity, rows), 0) + start * capacity == place
    pick = pick.astype(f32).astype(bf16)
    tags = dot(pick, jnp.broadcast_to(tag, (LANES, rows)).astype(bf16), ((1,), (1,))).astype(bf16)
    step = min(512, features)
    for c in range(0, features, step):
        moved = dot(pick, x[:, c:c + step]).astype(bf16)
        for j, out in enumerate(outs):
            out[:, c:c + step] = moved[j * capacity:(j + 1) * capacity]
    for j, out in enumerate(outs):
        out[:, features:] = tags[j * capacity:(j + 1) * capacity]


def far_body(slots, capacity, holders, me_ref, z_ref, ids_hbm, table_hbm, x_hbm, w_hbm, places_ref, *refs):
    outs, (x_buf, w_buf, ids_buf, table_buf, small_sem, x_sem, w_sem) = refs[:holders - NEAR], refs[holders - NEAR:]
    width = w_buf.shape[1]
    small = [
        pltpu.make_async_copy(ids_hbm, ids_buf, small_sem.at[0]),
        pltpu.make_async_copy(table_hbm, table_buf, small_sem.at[1]),
    ]
    x_copy = pltpu.make_async_copy(x_hbm, x_buf, x_sem)
    column = pl.multiple_of(jnp.where(z_ref[0] < 2, 3, 0) * width, width)
    w_copy = pltpu.make_async_copy(w_hbm.at[:, pl.ds(column, width)], w_buf, w_sem)
    for copy in small + [x_copy, w_copy]:
        copy.start()
    for copy in small:
        copy.wait()
    place, tag = places(slots, capacity, holders, me_ref[0], ids_buf[...], table_buf[...])
    row = iota(places_ref.shape, 0)
    places_ref[...] = jnp.where(row == 0, place, jnp.where(row == 1, tag.astype(i32), 0))
    x_copy.wait()
    pick_rows(NEAR, place, tag, x_buf, outs)
    w_copy.wait()


def far_rows(me, z, ids, table, x, weight, holders, slots, capacity, width):
    rows, features = x.shape
    ids, table = ids.reshape(1, rows), table.reshape(-1, LANES)
    smem, vmem, hbm = (pl.BlockSpec(memory_space=m) for m in (pltpu.SMEM, pltpu.VMEM, pltpu.HBM))
    shapes = [jax.ShapeDtypeStruct((8, rows), i32)]
    shapes += [jax.ShapeDtypeStruct((capacity, features + LANES), bf16)] * (holders - NEAR)
    shapes += [jax.ShapeDtypeStruct((rows, features), bf16), jax.ShapeDtypeStruct((features, width), bf16)]
    return pl.pallas_call(
        functools.partial(far_body, slots, capacity, holders),
        out_shape=shapes,
        in_specs=[smem, smem, hbm, hbm, hbm, hbm],
        out_specs=[vmem] * len(shapes),
        scratch_shapes=[
            pltpu.VMEM(ids.shape, i32),
            pltpu.VMEM(table.shape, i32),
            pltpu.SemaphoreType.DMA((2,)),
            pltpu.SemaphoreType.DMA(()),
            pltpu.SemaphoreType.DMA(()),
        ],
        compiler_params=params(),
        cost_estimate=cost(2 * holders * capacity * rows * features, 4 * rows * features),
        name="far_rows",
    )(me.reshape(1), z.reshape(1), in_hbm(ids), in_hbm(table), in_hbm(x), in_hbm(weight))


def near_body(places_ref, x_ref, *outs):
    pick_rows(0, places_ref[0:1, :], places_ref[1:2, :].astype(f32), x_ref, outs)


def near_rows(spots, x, capacity):
    rows, features = x.shape
    return pl.pallas_call(
        near_body,
        out_shape=[jax.ShapeDtypeStruct((capacity, features + LANES), bf16)] * NEAR,
        compiler_params=params(),
        cost_estimate=cost(2 * NEAR * capacity * rows * features, 4 * rows * features),
        name="near_rows",
    )(spots, x)


def first_body(x_ref, w_ref, out):
    out[...] = dot(x_ref[...], w_ref[...]).astype(bf16)


def first_block(x, w):
    (rows, features), width = x.shape, w.shape[1]
    return pl.pallas_call(
        first_body,
        out_shape=jax.ShapeDtypeStruct((rows, width), bf16),
        compiler_params=params(),
        cost_estimate=cost(2 * rows * features * width, 2 * features * (rows + width)),
        name="first_block",
    )(x, w)


def rest_body(z_ref, spots_ref, x_ref, w_hbm, *refs):
    near, (second, third, own, unsort, w_buf, sem) = refs[:NEAR], refs[NEAR:]
    z = z_ref[0]
    width = own.shape[1]
    copies = []
    for k, block in enumerate((jnp.where(z < 2, 2, 1), z ^ 1, z)):
        column = pl.multiple_of(block * width, width)
        copies.append(pltpu.make_async_copy(w_hbm.at[:, pl.ds(column, width)], w_buf.at[k], sem.at[k]))
        copies[k].start()
    near_body(spots_ref, x_ref, *near)
    unsort_matrix(spots_ref, unsort)
    for k, out in enumerate((second, third, own)):
        copies[k].wait()
        out[...] = dot(x_ref[...], w_buf[k]).astype(bf16)


def unsort_matrix(place_ref, unsort):
    rows, total = unsort.shape
    place = jnp.broadcast_to(place_ref[0:1, :].astype(f32), (LANES, rows)).T
    lane = iota((rows, LANES), 1).astype(f32)
    for k in range(total // LANES):
        unsort[:, k * LANES:(k + 1) * LANES] = (place == lane + float(k * LANES)).astype(f32).astype(bf16)


def rest(z, spots, x, weight, width, total, capacity):
    rows, features = x.shape
    smem, vmem, hbm = (pl.BlockSpec(memory_space=m) for m in (pltpu.SMEM, pltpu.VMEM, pltpu.HBM))
    shapes = [jax.ShapeDtypeStruct((capacity, features + LANES), bf16)] * NEAR
    shapes += [jax.ShapeDtypeStruct((rows, width), bf16)] * 3 + [jax.ShapeDtypeStruct((rows, total), bf16)]
    return pl.pallas_call(
        rest_body,
        out_shape=shapes,
        in_specs=[smem, vmem, vmem, hbm],
        out_specs=[vmem] * len(shapes),
        scratch_shapes=[pltpu.VMEM((3, features, width), bf16), pltpu.SemaphoreType.DMA((3,))],
        compiler_params=params(),
        cost_estimate=cost(6 * rows * features * width, 2 * features * (rows + 4 * width)),
        name="rest",
    )(z.reshape(1), spots, x, in_hbm(weight))


def unsort_only(place, total):
    return pl.pallas_call(
        unsort_matrix,
        out_shape=jax.ShapeDtypeStruct((place.shape[1], total), bf16),
        compiler_params=params(),
        name="unsort",
    )(place)


def slot_mask(tag, group):
    lane = iota(tag.shape, 1)
    return tag == jnp.where(lane < ADAPTER_RANK, 2 * group + 1, 2 * group + 2).astype(f32)


def shrink_body(kept, down_ref, *refs):
    parts, out = refs[1 if kept else 0:-1], refs[-1]
    features, width = down_ref.shape
    capacity = parts[0].shape[0]
    half = capacity // 2
    first = iota((half, LANES), 1) < ADAPTER_RANK
    if kept:
        out[:kept, :] = refs[0][...]
    for k, part in enumerate(parts):
        full = dot(part[:, :features], down_ref[...])
        tag = part[:, features:].astype(f32)
        total = jnp.zeros((capacity, LANES), f32)
        for group in range(width // LANES):
            total += jnp.where(slot_mask(tag, group), full[:, group * LANES:(group + 1) * LANES], 0.0)
        total += pltpu.roll(total, ADAPTER_RANK, 1)
        spot = slice(kept + k * half, kept + (k + 1) * half)
        out[spot, :] = jnp.where(first, total[:half], total[half:]).astype(bf16)


def shrink_partial(down, parts, done=()):
    features, width = down.shape
    capacity = parts[0].shape[0]
    total = len(parts) * capacity
    kept = sum(d.shape[0] for d in done)
    return pl.pallas_call(
        functools.partial(shrink_body, kept),
        out_shape=jax.ShapeDtypeStruct((kept + total // 2, LANES), bf16),
        compiler_params=params(),
        cost_estimate=cost(2 * total * features * width, 2 * features * (total + width)),
        name="shrink_partial",
    )(down, *done, *parts)


def expand_body(count, one_ref, two_ref, up_ref, *refs):
    tags, outs = refs[:count], refs[count:]
    capacity = outs[0].shape[0]
    half = capacity // 2
    up = up_ref[...]
    first = iota((half, LANES), 1) < ADAPTER_RANK
    for k in range(count):
        part = pl.ds(k * half, half)
        shrink = (one_ref[part, :].astype(f32) + two_ref[part, :].astype(f32)).astype(bf16).astype(f32)
        turned = pltpu.roll(shrink, ADAPTER_RANK, 1)
        rows = jnp.concatenate([jnp.where(first, shrink, turned), jnp.where(first, turned, shrink)], axis=0)
        tag = tags[k][...].astype(f32)
        spread = [
            jnp.where(slot_mask(tag, group), rows, 0.0).astype(bf16) for group in range(up.shape[0] // LANES)
        ]
        outs[k][...] = dot(jnp.concatenate(spread, axis=1), up).astype(bf16)


def expand(one, two, up, parts):
    capacity, width = parts[0].shape
    count = len(parts)
    tag_block = pl.BlockSpec((capacity, LANES), lambda i: (0, width // LANES - 1))
    whole = lambda a: pl.BlockSpec(a.shape, lambda i: (0, 0))
    columns = up.shape[1]
    return pl.pallas_call(
        functools.partial(expand_body, count),
        grid=(1,),
        out_shape=[jax.ShapeDtypeStruct((capacity, columns), bf16)] * count,
        in_specs=[whole(one), whole(two), whole(up)] + [tag_block] * count,
        out_specs=[pl.BlockSpec((capacity, columns), lambda i: (0, 0))] * count,
        compiler_params=params(),
        cost_estimate=cost(80 * count * capacity * up.size, 80 * (up.size + count * capacity * columns)),
        name="expand",
    )(one, two, up, *parts)


def deltas_body(unsort_ref, own_ref, *refs):
    deltas, out = refs[:-1], refs[-1]
    placed = dot(unsort_ref[...], jnp.concatenate([d[...] for d in deltas], axis=0))
    out[...] = own_ref[...].astype(f32) + placed


def with_deltas(unsort, deltas, own):
    rows, columns = own.shape
    return pl.pallas_call(
        deltas_body,
        out_shape=jax.ShapeDtypeStruct((rows, columns), f32),
        compiler_params=params(),
        cost_estimate=cost(2 * rows * unsort.shape[1] * columns, 12 * rows * columns),
        name="with_deltas",
    )(unsort, own, *deltas)


def finish_body(start_ref, *refs):
    terms, (out_hbm, out_buf, sem) = refs[:-3], refs[-3:]
    pieces = sem.shape[0]
    step = out_buf.shape[0] // pieces
    copies = []
    for k in range(pieces):
        part = pl.ds(k * step, step)
        total = start_ref[part, :]
        for term in terms:
            total += term[part, :].astype(f32)
        out_buf[part, :] = total.astype(bf16)
        copies.append(pltpu.make_async_copy(out_buf.at[part, :], out_hbm.at[part, :], sem.at[k]))
        copies[k].start()
    for copy in copies:
        copy.wait()


def finish(start, terms):
    vmem, hbm = (pl.BlockSpec(memory_space=m) for m in (pltpu.VMEM, pltpu.HBM))
    return pl.pallas_call(
        finish_body,
        out_shape=jax.ShapeDtypeStruct(start.shape, bf16),
        in_specs=[vmem] * (1 + len(terms)),
        out_specs=hbm,
        scratch_shapes=[pltpu.VMEM(start.shape, bf16), pltpu.SemaphoreType.DMA((4,))],
        compiler_params=params(),
        cost_estimate=cost(start.size, 8 * start.size),
        name="finish",
    )(start, *terms)


def both(a, b):
    return (a.astype(f32) + b.astype(f32)).astype(bf16)


def after(value, *others):
    return lax.optimization_barrier((value,) + others)[0]


def swap(value, axis, bit):
    return lax.ppermute(value, axis, [(i, i ^ bit) for i in range(lax.axis_size(axis))])


EDGE = [(0, 1), (3, 2)]
MIDDLE = [(1, 2), (2, 1)]


def tp_sums(mine, *before):
    sums, bit = [mine], 1
    while True:
        other = swap(sums[-1], "tp", bit)
        bit *= 2
        if bit >= lax.axis_size("tp"):
            return sums, other
        sums.append(both(after(sums[-1], *before), other))


def shards(x, ids, table, weight, down, up):
    holders = lax.axis_size("ad")
    capacity = x.shape[0] // 4
    slots = up.shape[0] // ADAPTER_RANK
    width = up.shape[1]
    total = holders * capacity
    me, z = lax.axis_index("ad"), lax.axis_index("tp")
    spots, *far, x, w = far_rows(me, z, ids, table, x, weight, holders, slots, capacity, width)
    far = [swap(rows, "ad", j + NEAR) for j, rows in enumerate(far)]
    if lax.axis_size("tp") == 4 and holders == 4:
        first = first_block(x, w)
        edge0 = lax.ppermute(first, "tp", EDGE)
        *near, second, third, own, unsort = rest(z, after(spots, first), x, weight, width, total, capacity)
        near = [near[0], swap(near[1], "ad", 1)]
        edge1 = lax.ppermute(second, "tp", EDGE)
        early = shrink_partial(down, [near[0], far[0]])
        inner0 = both(after(first, early), edge0)
        middle0 = lax.ppermute(inner0, "tp", MIDDLE)
        early = shrink_partial(down, [after(near[1], inner0)], [early])
        mine = shrink_partial(down, [after(far[1], early)], [early])
        parts, order = [near[0], far[0], near[1], far[1]], (0, 2, 1, 3)
        inner1 = both(after(second, mine), edge1)
        steps, other = tp_sums(mine, inner1)
        inner2 = both(after(third, steps[-1]), middle0)
        last = swap(inner2, "tp", 1)
        middle1 = lax.ppermute(after(inner1, inner2), "tp", MIDDLE)
        sums = [middle1, last]
    else:
        near = near_rows(spots, x, capacity)
        near = [near[0], swap(near[1], "ad", 1)]
        parts, order = near + far, range(holders)
        unsort = unsort_only(spots, total)
        full = dot(x, weight).astype(bf16)
        own, sums = lax.psum_scatter(full, "tp", scatter_dimension=1, tiled=True), []
        steps, other = tp_sums(shrink_partial(down, parts))
    deltas = expand(steps[-1], other, up, parts)
    back = [None] * holders
    for j, delta in zip(order, deltas):
        back[j] = swap(delta, "ad", j) if j else delta
    return finish(with_deltas(unsort, back, own), sums)


def solution(mesh):
    in_specs = (
        P(("rep", "ad"), "tp"),
        P(("rep", "ad")),
        P("rep"),
        P("tp", None),
        P(("rep", "tp"), "ad"),
        P(("rep", "ad"), "tp"),
    )
    out_specs = P(("rep", "ad"), "tp")
    return jax.shard_map(shards, mesh=mesh, in_specs=in_specs, out_specs=out_specs, check_vma=False)
```

```python
import functools

import jax
import jax.numpy as jnp
from jax import lax
from jax.experimental import pallas as pl
from jax.experimental.pallas import tpu as pltpu
from jax.sharding import PartitionSpec as P

ADAPTER_RANK = 64
LANES = 128
NEAR = 2
VMEM_BYTES = 32 * 1024 * 1024

bf16 = jnp.bfloat16
f32 = jnp.float32
i32 = jnp.int32


def params():
    return pltpu.CompilerParams(vmem_limit_bytes=VMEM_BYTES)


def cost(flops, nbytes):
    return pl.CostEstimate(flops=flops, bytes_accessed=nbytes, transcendentals=0)


def dot(a, b, contract=((1,), (0,))):
    return lax.dot_general(a, b, (contract, ((), ())), preferred_element_type=f32)


def in_hbm(a):
    return pltpu.with_memory_space_constraint(a, pltpu.HBM)


def iota(shape, dim):
    return lax.broadcasted_iota(i32, shape, dim)


def places(slots, capacity, holders, me, ids, table):
    rows = ids.shape[1]
    low = (iota((LANES, rows), 0) == (ids & (LANES - 1))).astype(f32).astype(bf16)
    high = iota((table.shape[0], rows), 0) == lax.shift_right_logical(ids, 7)
    found = dot(table.astype(f32).astype(bf16), low)
    slot = jnp.sum(jnp.where(high, found, 0.0), axis=0, keepdims=True).astype(i32)
    holder = split_slot(slot, slots)
    tag = (slot - holder * slots + 1).astype(f32)
    partner = holder ^ me
    mine = iota((max(8, holders), rows), 0) == partner
    ones = mine.astype(f32)
    groups = [ones[:, k:k + LANES] for k in range(0, rows, LANES)]
    earlier = (iota((LANES, LANES), 0) < iota((LANES, LANES), 1)).astype(f32).astype(bf16)
    before = dot(jnp.concatenate(groups, axis=0).astype(bf16), earlier)
    count = ones.shape[0]
    ranks, passed = [], jnp.zeros((count, 1), f32)
    for k, group in enumerate(groups):
        ranks.append(jnp.sum(group * (before[k * count:(k + 1) * count] + passed), axis=0, keepdims=True))
        passed += jnp.sum(group, axis=1, keepdims=True)
    return partner * capacity + jnp.concatenate(ranks, axis=1).astype(i32), tag


def split_slot(slot, slots):
    if slots & (slots - 1):
        return lax.div(slot, slots)
    return lax.shift_right_logical(slot, slots.bit_length() - 1)


def pick_rows(start, place, tag, x, outs):
    rows, features = x.shape
    capacity = outs[0].shape[0]
    pick = iota((len(outs) * capacity, rows), 0) + start * capacity == place
    pick = pick.astype(f32).astype(bf16)
    tags = dot(pick, jnp.broadcast_to(tag, (LANES, rows)).astype(bf16), ((1,), (1,))).astype(bf16)
    step = min(512, features)
    for c in range(0, features, step):
        moved = dot(pick, x[:, c:c + step]).astype(bf16)
        for j, out in enumerate(outs):
            out[:, c:c + step] = moved[j * capacity:(j + 1) * capacity]
    for j, out in enumerate(outs):
        out[:, features:] = tags[j * capacity:(j + 1) * capacity]


def far_body(slots, capacity, holders, me_ref, z_ref, ids_hbm, table_hbm, x_hbm, w_hbm, places_ref, *refs):
    outs, (x_buf, w_buf, ids_buf, table_buf, small_sem, x_sem, w_sem) = refs[:holders - NEAR], refs[holders - NEAR:]
    width = w_buf.shape[1]
    small = [
        pltpu.make_async_copy(ids_hbm, ids_buf, small_sem.at[0]),
        pltpu.make_async_copy(table_hbm, table_buf, small_sem.at[1]),
    ]
    x_copy = pltpu.make_async_copy(x_hbm, x_buf, x_sem)
    column = pl.multiple_of(jnp.where(z_ref[0] < 2, 3, 0) * width, width)
    w_copy = pltpu.make_async_copy(w_hbm.at[:, pl.ds(column, width)], w_buf, w_sem)
    for copy in small + [x_copy, w_copy]:
        copy.start()
    for copy in small:
        copy.wait()
    place, tag = places(slots, capacity, holders, me_ref[0], ids_buf[...], table_buf[...])
    row = iota(places_ref.shape, 0)
    places_ref[...] = jnp.where(row == 0, place, jnp.where(row == 1, tag.astype(i32), 0))
    x_copy.wait()
    pick_rows(NEAR, place, tag, x_buf, outs)
    w_copy.wait()


def far_rows(me, z, ids, table, x, weight, holders, slots, capacity, width):
    rows, features = x.shape
    ids, table = ids.reshape(1, rows), table.reshape(-1, LANES)
    smem, vmem, hbm = (pl.BlockSpec(memory_space=m) for m in (pltpu.SMEM, pltpu.VMEM, pltpu.HBM))
    shapes = [jax.ShapeDtypeStruct((8, rows), i32)]
    shapes += [jax.ShapeDtypeStruct((capacity, features + LANES), bf16)] * (holders - NEAR)
    shapes += [jax.ShapeDtypeStruct((rows, features), bf16), jax.ShapeDtypeStruct((features, width), bf16)]
    return pl.pallas_call(
        functools.partial(far_body, slots, capacity, holders),
        out_shape=shapes,
        in_specs=[smem, smem, hbm, hbm, hbm, hbm],
        out_specs=[vmem] * len(shapes),
        scratch_shapes=[
            pltpu.VMEM(ids.shape, i32),
            pltpu.VMEM(table.shape, i32),
            pltpu.SemaphoreType.DMA((2,)),
            pltpu.SemaphoreType.DMA(()),
            pltpu.SemaphoreType.DMA(()),
        ],
        compiler_params=params(),
        cost_estimate=cost(2 * holders * capacity * rows * features, 4 * rows * features),
        name="far_rows",
    )(me.reshape(1), z.reshape(1), in_hbm(ids), in_hbm(table), in_hbm(x), in_hbm(weight))


def near_body(places_ref, x_ref, *outs):
    pick_rows(0, places_ref[0:1, :], places_ref[1:2, :].astype(f32), x_ref, outs)


def near_rows(spots, x, capacity):
    rows, features = x.shape
    return pl.pallas_call(
        near_body,
        out_shape=[jax.ShapeDtypeStruct((capacity, features + LANES), bf16)] * NEAR,
        compiler_params=params(),
        cost_estimate=cost(2 * NEAR * capacity * rows * features, 4 * rows * features),
        name="near_rows",
    )(spots, x)


def first_body(x_ref, w_ref, out):
    out[...] = dot(x_ref[...], w_ref[...]).astype(bf16)


def first_block(x, w):
    (rows, features), width = x.shape, w.shape[1]
    return pl.pallas_call(
        first_body,
        out_shape=jax.ShapeDtypeStruct((rows, width), bf16),
        compiler_params=params(),
        cost_estimate=cost(2 * rows * features * width, 2 * features * (rows + width)),
        name="first_block",
    )(x, w)


def rest_body(z_ref, spots_ref, x_ref, w_hbm, *refs):
    near, (second, third, own, unsort, w_buf, sem) = refs[:NEAR], refs[NEAR:]
    z = z_ref[0]
    width = own.shape[1]
    copies = []
    for k, block in enumerate((jnp.where(z < 2, 2, 1), z ^ 1, z)):
        column = pl.multiple_of(block * width, width)
        copies.append(pltpu.make_async_copy(w_hbm.at[:, pl.ds(column, width)], w_buf.at[k], sem.at[k]))
        copies[k].start()
    near_body(spots_ref, x_ref, *near)
    unsort_matrix(spots_ref, unsort)
    for k, out in enumerate((second, third, own)):
        copies[k].wait()
        out[...] = dot(x_ref[...], w_buf[k]).astype(bf16)


def unsort_matrix(place_ref, unsort):
    rows, total = unsort.shape
    place = jnp.broadcast_to(place_ref[0:1, :].astype(f32), (LANES, rows)).T
    lane = iota((rows, LANES), 1).astype(f32)
    for k in range(total // LANES):
        unsort[:, k * LANES:(k + 1) * LANES] = (place == lane + float(k * LANES)).astype(f32).astype(bf16)


def rest(z, spots, x, weight, width, total, capacity):
    rows, features = x.shape
    smem, vmem, hbm = (pl.BlockSpec(memory_space=m) for m in (pltpu.SMEM, pltpu.VMEM, pltpu.HBM))
    shapes = [jax.ShapeDtypeStruct((capacity, features + LANES), bf16)] * NEAR
    shapes += [jax.ShapeDtypeStruct((rows, width), bf16)] * 3 + [jax.ShapeDtypeStruct((rows, total), bf16)]
    return pl.pallas_call(
        rest_body,
        out_shape=shapes,
        in_specs=[smem, vmem, vmem, hbm],
        out_specs=[vmem] * len(shapes),
        scratch_shapes=[pltpu.VMEM((3, features, width), bf16), pltpu.SemaphoreType.DMA((3,))],
        compiler_params=params(),
        cost_estimate=cost(6 * rows * features * width, 2 * features * (rows + 4 * width)),
        name="rest",
    )(z.reshape(1), spots, x, in_hbm(weight))


def unsort_only(place, total):
    return pl.pallas_call(
        unsort_matrix,
        out_shape=jax.ShapeDtypeStruct((place.shape[1], total), bf16),
        compiler_params=params(),
        name="unsort",
    )(place)


def slot_mask(tag, group):
    lane = iota(tag.shape, 1)
    return tag == jnp.where(lane < ADAPTER_RANK, 2 * group + 1, 2 * group + 2).astype(f32)


def shrink_body(kept, down_ref, *refs):
    parts, out = refs[1 if kept else 0:-1], refs[-1]
    features, width = down_ref.shape
    capacity = parts[0].shape[0]
    half = capacity // 2
    first = iota((half, LANES), 1) < ADAPTER_RANK
    if kept:
        out[:kept, :] = refs[0][...]
    for k, part in enumerate(parts):
        full = dot(part[:, :features], down_ref[...])
        tag = part[:, features:].astype(f32)
        total = jnp.zeros((capacity, LANES), f32)
        for group in range(width // LANES):
            total += jnp.where(slot_mask(tag, group), full[:, group * LANES:(group + 1) * LANES], 0.0)
        total += pltpu.roll(total, ADAPTER_RANK, 1)
        spot = slice(kept + k * half, kept + (k + 1) * half)
        out[spot, :] = jnp.where(first, total[:half], total[half:]).astype(bf16)


def shrink_partial(down, parts, done=()):
    features, width = down.shape
    capacity = parts[0].shape[0]
    total = len(parts) * capacity
    kept = sum(d.shape[0] for d in done)
    return pl.pallas_call(
        functools.partial(shrink_body, kept),
        out_shape=jax.ShapeDtypeStruct((kept + total // 2, LANES), bf16),
        compiler_params=params(),
        cost_estimate=cost(2 * total * features * width, 2 * features * (total + width)),
        name="shrink_partial",
    )(down, *done, *parts)


def expand_body(count, one_ref, two_ref, up_ref, *refs):
    tags, outs = refs[:count], refs[count:]
    capacity = outs[0].shape[0]
    half = capacity // 2
    up = up_ref[...]
    first = iota((half, LANES), 1) < ADAPTER_RANK
    for k in range(count):
        part = pl.ds(k * half, half)
        shrink = (one_ref[part, :].astype(f32) + two_ref[part, :].astype(f32)).astype(bf16).astype(f32)
        turned = pltpu.roll(shrink, ADAPTER_RANK, 1)
        rows = jnp.concatenate([jnp.where(first, shrink, turned), jnp.where(first, turned, shrink)], axis=0)
        tag = tags[k][...].astype(f32)
        spread = [
            jnp.where(slot_mask(tag, group), rows, 0.0).astype(bf16) for group in range(up.shape[0] // LANES)
        ]
        outs[k][...] = dot(jnp.concatenate(spread, axis=1), up).astype(bf16)


def expand(one, two, up, parts):
    capacity, width = parts[0].shape
    count = len(parts)
    tag_block = pl.BlockSpec((capacity, LANES), lambda i: (0, width // LANES - 1))
    whole = lambda a: pl.BlockSpec(a.shape, lambda i: (0, 0))
    columns = up.shape[1]
    return pl.pallas_call(
        functools.partial(expand_body, count),
        grid=(1,),
        out_shape=[jax.ShapeDtypeStruct((capacity, columns), bf16)] * count,
        in_specs=[whole(one), whole(two), whole(up)] + [tag_block] * count,
        out_specs=[pl.BlockSpec((capacity, columns), lambda i: (0, 0))] * count,
        compiler_params=params(),
        cost_estimate=cost(30 * count * capacity * up.size, 30 * (up.size + count * capacity * columns)),
        name="expand",
    )(one, two, up, *parts)


def deltas_body(count, unsort_ref, *refs):
    deltas, bases, out = refs[:count], refs[count:-1], refs[-1]
    total = dot(unsort_ref[...], jnp.concatenate([d[...] for d in deltas], axis=0))
    for base in bases:
        total += base[...].astype(f32)
    out[...] = total


def with_deltas(unsort, deltas, bases):
    rows, columns = bases[0].shape
    return pl.pallas_call(
        functools.partial(deltas_body, len(deltas)),
        out_shape=jax.ShapeDtypeStruct((rows, columns), f32),
        compiler_params=params(),
        cost_estimate=cost(2 * rows * unsort.shape[1] * columns, 2 * 6 * rows * columns),
        name="with_deltas",
    )(unsort, *deltas, *bases)


def finish_body(start_ref, *refs):
    terms, (out_hbm, out_buf, sem) = refs[:-3], refs[-3:]
    pieces = sem.shape[0]
    step = out_buf.shape[0] // pieces
    copies = []
    for k in range(pieces):
        part = pl.ds(k * step, step)
        total = start_ref[part, :]
        for term in terms:
            total += term[part, :].astype(f32)
        out_buf[part, :] = total.astype(bf16)
        copies.append(pltpu.make_async_copy(out_buf.at[part, :], out_hbm.at[part, :], sem.at[k]))
        copies[k].start()
    for copy in copies:
        copy.wait()


def finish(start, terms):
    vmem, hbm = (pl.BlockSpec(memory_space=m) for m in (pltpu.VMEM, pltpu.HBM))
    return pl.pallas_call(
        finish_body,
        out_shape=jax.ShapeDtypeStruct(start.shape, bf16),
        in_specs=[vmem] * (1 + len(terms)),
        out_specs=hbm,
        scratch_shapes=[pltpu.VMEM(start.shape, bf16), pltpu.SemaphoreType.DMA((4,))],
        compiler_params=params(),
        cost_estimate=cost(start.size, 8 * start.size),
        name="finish",
    )(start, *terms)


def both(a, b):
    return (a.astype(f32) + b.astype(f32)).astype(bf16)


def after(value, *others):
    return lax.optimization_barrier((value,) + others)[0]


def swap(value, axis, bit):
    return lax.ppermute(value, axis, [(i, i ^ bit) for i in range(lax.axis_size(axis))])


EDGE = [(0, 1), (3, 2)]
MIDDLE = [(1, 2), (2, 1)]


def tp_sums(mine, *before):
    sums, bit = [mine], lax.axis_size("tp") // 2
    while True:
        other = swap(sums[-1], "tp", bit)
        bit //= 2
        if not bit:
            return sums, other
        sums.append(both(after(sums[-1], *before), other))


def shards(x, ids, table, weight, down, up):
    holders = lax.axis_size("ad")
    capacity = x.shape[0] // 4
    slots = up.shape[0] // ADAPTER_RANK
    width = up.shape[1]
    total = holders * capacity
    me, z = lax.axis_index("ad"), lax.axis_index("tp")
    spots, *far, x, w = far_rows(me, z, ids, table, x, weight, holders, slots, capacity, width)
    far = [swap(rows, "ad", j + NEAR) for j, rows in enumerate(far)]
    if lax.axis_size("tp") == 4 and holders == 4:
        first = first_block(x, w)
        edge0 = lax.ppermute(first, "tp", EDGE)
        *near, second, third, own, unsort = rest(z, after(spots, first), x, weight, width, total, capacity)
        near = [near[0], swap(near[1], "ad", 1)]
        edge1 = lax.ppermute(second, "tp", EDGE)
        early = shrink_partial(down, [near[0], far[0]])
        inner0 = both(after(first, early), edge0)
        middle0 = lax.ppermute(inner0, "tp", MIDDLE)
        early = shrink_partial(down, [after(near[1], inner0)], [early])
        mine = shrink_partial(down, [after(far[1], early)], [early])
        parts, order = [near[0], far[0], near[1], far[1]], (0, 2, 1, 3)
        inner1 = both(after(second, mine), edge1)
        steps, other = tp_sums(mine, inner1)
        middle1 = lax.ppermute(inner1, "tp", MIDDLE)
        inner2 = both(after(third, steps[-1]), middle0)
        last = swap(inner2, "tp", 1)
        bases, sums = [own, middle1], [last]
    else:
        near = near_rows(spots, x, capacity)
        near = [near[0], swap(near[1], "ad", 1)]
        parts, order = near + far, range(holders)
        unsort = unsort_only(spots, total)
        full = dot(x, weight).astype(bf16)
        bases, sums = [lax.psum_scatter(full, "tp", scatter_dimension=1, tiled=True)], []
        steps, other = tp_sums(shrink_partial(down, parts))
    deltas = expand(steps[-1], other, up, parts)
    back = [None] * holders
    for j, delta in zip(order, deltas):
        back[j] = swap(delta, "ad", j) if j else delta
    return finish(with_deltas(unsort, back, bases), sums)


def solution(mesh):
    in_specs = (
        P(("rep", "ad"), "tp"),
        P(("rep", "ad")),
        P("rep"),
        P("tp", None),
        P(("rep", "tp"), "ad"),
        P(("rep", "ad"), "tp"),
    )
    out_specs = P(("rep", "ad"), "tp")
    return jax.shard_map(shards, mesh=mesh, in_specs=in_specs, out_specs=out_specs, check_vma=False)
```

```python
import functools

import jax
import jax.numpy as jnp
from jax import lax
from jax.experimental import pallas as pl
from jax.experimental.pallas import tpu as pltpu
from jax.sharding import PartitionSpec as P

ADAPTER_RANK = 64
LANES = 128
NEAR = 2
TAG_ROWS = 16
VMEM_BYTES = 32 * 1024 * 1024

bf16 = jnp.bfloat16
f32 = jnp.float32
i32 = jnp.int32


def params():
    return pltpu.CompilerParams(vmem_limit_bytes=VMEM_BYTES)


def cost(flops, nbytes):
    return pl.CostEstimate(flops=flops, bytes_accessed=nbytes, transcendentals=0)


def dot(a, b, contract=((1,), (0,))):
    return lax.dot_general(a, b, (contract, ((), ())), preferred_element_type=f32)


def in_hbm(a):
    return pltpu.with_memory_space_constraint(a, pltpu.HBM)


def iota(shape, dim):
    return lax.broadcasted_iota(i32, shape, dim)


def places(slots, capacity, holders, me, ids, table):
    rows = ids.shape[1]
    low = (iota((LANES, rows), 0) == (ids & (LANES - 1))).astype(f32).astype(bf16)
    high = iota((table.shape[0], rows), 0) == lax.shift_right_logical(ids, 7)
    found = dot(table.astype(f32).astype(bf16), low)
    slot = jnp.sum(jnp.where(high, found, 0.0), axis=0, keepdims=True).astype(i32)
    holder = split_slot(slot, slots)
    tag = (slot - holder * slots + 1).astype(f32)
    partner = holder ^ me
    mine = iota((max(8, holders), rows), 0) == partner
    ones = mine.astype(f32)
    groups = [ones[:, k:k + LANES] for k in range(0, rows, LANES)]
    earlier = (iota((LANES, LANES), 0) < iota((LANES, LANES), 1)).astype(f32).astype(bf16)
    before = dot(jnp.concatenate(groups, axis=0).astype(bf16), earlier)
    count = ones.shape[0]
    ranks, passed = [], jnp.zeros((count, 1), f32)
    for k, group in enumerate(groups):
        ranks.append(jnp.sum(group * (before[k * count:(k + 1) * count] + passed), axis=0, keepdims=True))
        passed += jnp.sum(group, axis=1, keepdims=True)
    return partner * capacity + jnp.concatenate(ranks, axis=1).astype(i32), tag


def split_slot(slot, slots):
    if slots & (slots - 1):
        return lax.div(slot, slots)
    return lax.shift_right_logical(slot, slots.bit_length() - 1)


def pick_rows(start, place, tag, x, outs):
    rows, features = x.shape
    pick = iota((len(outs) * LANES, rows), 0) + start * LANES == place
    pick = pick.astype(f32).astype(bf16)
    tags = dot(jnp.broadcast_to(tag, (TAG_ROWS, rows)).astype(bf16), pick, ((1,), (1,))).astype(bf16)
    step = min(512, features)
    for c in range(0, features, step):
        moved = dot(pick, x[:, c:c + step]).astype(bf16)
        for j, out in enumerate(outs):
            for i in range(0, step, LANES):
                out[c + i:c + i + LANES, :] = moved[j * LANES:(j + 1) * LANES, i:i + LANES]
    for j, out in enumerate(outs):
        out[features:, :] = tags[:, j * LANES:(j + 1) * LANES]


def part_rows(part, features):
    return jnp.concatenate([part[c:c + LANES, :] for c in range(0, features, LANES)], axis=1)


def tag_lanes(tags):
    return jnp.broadcast_to(tags[0:1, :].astype(f32), (LANES, LANES)).T


def part_shape(features):
    return jax.ShapeDtypeStruct((features + TAG_ROWS, LANES), bf16)


def far_body(slots, capacity, holders, me_ref, z_ref, ids_hbm, table_hbm, x_hbm, w_hbm, places_ref, *refs):
    outs, (x_buf, w_buf, ids_buf, table_buf, small_sem, x_sem, w_sem) = refs[:holders - NEAR], refs[holders - NEAR:]
    width = w_buf.shape[1]
    small = [
        pltpu.make_async_copy(ids_hbm, ids_buf, small_sem.at[0]),
        pltpu.make_async_copy(table_hbm, table_buf, small_sem.at[1]),
    ]
    x_copy = pltpu.make_async_copy(x_hbm, x_buf, x_sem)
    column = pl.multiple_of(jnp.where(z_ref[0] < 2, 3, 0) * width, width)
    w_copy = pltpu.make_async_copy(w_hbm.at[:, pl.ds(column, width)], w_buf, w_sem)
    for copy in small + [x_copy, w_copy]:
        copy.start()
    for copy in small:
        copy.wait()
    place, tag = places(slots, capacity, holders, me_ref[0], ids_buf[...], table_buf[...])
    row = iota(places_ref.shape, 0)
    places_ref[...] = jnp.where(row == 0, place, jnp.where(row == 1, tag.astype(i32), 0))
    x_copy.wait()
    pick_rows(NEAR, place, tag, x_buf, outs)
    w_copy.wait()


def far_rows(me, z, ids, table, x, weight, holders, slots, capacity, width):
    rows, features = x.shape
    ids, table = ids.reshape(1, rows), table.reshape(-1, LANES)
    smem, vmem, hbm = (pl.BlockSpec(memory_space=m) for m in (pltpu.SMEM, pltpu.VMEM, pltpu.HBM))
    shapes = [jax.ShapeDtypeStruct((8, rows), i32)]
    shapes += [part_shape(features)] * (holders - NEAR)
    shapes += [jax.ShapeDtypeStruct((rows, features), bf16), jax.ShapeDtypeStruct((features, width), bf16)]
    return pl.pallas_call(
        functools.partial(far_body, slots, capacity, holders),
        out_shape=shapes,
        in_specs=[smem, smem, hbm, hbm, hbm, hbm],
        out_specs=[vmem] * len(shapes),
        scratch_shapes=[
            pltpu.VMEM(ids.shape, i32),
            pltpu.VMEM(table.shape, i32),
            pltpu.SemaphoreType.DMA((2,)),
            pltpu.SemaphoreType.DMA(()),
            pltpu.SemaphoreType.DMA(()),
        ],
        compiler_params=params(),
        cost_estimate=cost(2 * holders * capacity * rows * features, 4 * rows * features),
        name="far_rows",
    )(me.reshape(1), z.reshape(1), in_hbm(ids), in_hbm(table), in_hbm(x), in_hbm(weight))


def near_body(places_ref, x_ref, *outs):
    pick_rows(0, places_ref[0:1, :], places_ref[1:2, :].astype(f32), x_ref, outs)


def near_rows(spots, x, capacity):
    rows, features = x.shape
    return pl.pallas_call(
        near_body,
        out_shape=[part_shape(features)] * NEAR,
        compiler_params=params(),
        cost_estimate=cost(2 * NEAR * capacity * rows * features, 4 * rows * features),
        name="near_rows",
    )(spots, x)


def first_body(x_ref, w_ref, out):
    out[...] = dot(x_ref[...], w_ref[...]).astype(bf16)


def first_block(x, w):
    (rows, features), width = x.shape, w.shape[1]
    return pl.pallas_call(
        first_body,
        out_shape=jax.ShapeDtypeStruct((rows, width), bf16),
        compiler_params=params(),
        cost_estimate=cost(2 * rows * features * width, 2 * features * (rows + width)),
        name="first_block",
    )(x, w)


def rest_body(z_ref, spots_ref, x_ref, w_hbm, *refs):
    near, (second, third, own, unsort, w_buf, sem) = refs[:NEAR], refs[NEAR:]
    z = z_ref[0]
    width = own.shape[1]
    copies = []
    for k, block in enumerate((jnp.where(z < 2, 2, 1), z ^ 1, z)):
        column = pl.multiple_of(block * width, width)
        copies.append(pltpu.make_async_copy(w_hbm.at[:, pl.ds(column, width)], w_buf.at[k], sem.at[k]))
        copies[k].start()
    near_body(spots_ref, x_ref, *near)
    unsort_matrix(spots_ref, unsort)
    for k, out in enumerate((second, third, own)):
        copies[k].wait()
        out[...] = dot(x_ref[...], w_buf[k]).astype(bf16)


def unsort_matrix(place_ref, unsort):
    rows, total = unsort.shape
    place = jnp.broadcast_to(place_ref[0:1, :].astype(f32), (LANES, rows)).T
    lane = iota((rows, LANES), 1).astype(f32)
    for k in range(total // LANES):
        unsort[:, k * LANES:(k + 1) * LANES] = (place == lane + float(k * LANES)).astype(f32).astype(bf16)


def rest(z, spots, x, weight, width, total, capacity):
    rows, features = x.shape
    smem, vmem, hbm = (pl.BlockSpec(memory_space=m) for m in (pltpu.SMEM, pltpu.VMEM, pltpu.HBM))
    shapes = [part_shape(features)] * NEAR
    shapes += [jax.ShapeDtypeStruct((rows, width), bf16)] * 3 + [jax.ShapeDtypeStruct((rows, total), bf16)]
    return pl.pallas_call(
        rest_body,
        out_shape=shapes,
        in_specs=[smem, vmem, vmem, hbm],
        out_specs=[vmem] * len(shapes),
        scratch_shapes=[pltpu.VMEM((3, features, width), bf16), pltpu.SemaphoreType.DMA((3,))],
        compiler_params=params(),
        cost_estimate=cost(6 * rows * features * width, 2 * features * (rows + 4 * width)),
        name="rest",
    )(z.reshape(1), spots, x, in_hbm(weight))


def unsort_only(place, total):
    return pl.pallas_call(
        unsort_matrix,
        out_shape=jax.ShapeDtypeStruct((place.shape[1], total), bf16),
        compiler_params=params(),
        name="unsort",
    )(place)


def slot_mask(tag, group):
    lane = iota(tag.shape, 1)
    return tag == jnp.where(lane < ADAPTER_RANK, 2 * group + 1, 2 * group + 2).astype(f32)


def shrink_body(kept, down_ref, *refs):
    parts, out = refs[1 if kept else 0:-1], refs[-1]
    features, width = down_ref.shape
    half = LANES // 2
    first = iota((half, LANES), 1) < ADAPTER_RANK
    if kept:
        out[:kept, :] = refs[0][...]
    for k, part in enumerate(parts):
        tag = tag_lanes(part[features:, :])
        full = dot(part_rows(part, features), down_ref[...])
        total = jnp.zeros((LANES, LANES), f32)
        for group in range(width // LANES):
            total += jnp.where(slot_mask(tag, group), full[:, group * LANES:(group + 1) * LANES], 0.0)
        total += pltpu.roll(total, ADAPTER_RANK, 1)
        spot = slice(kept + k * half, kept + (k + 1) * half)
        out[spot, :] = jnp.where(first, total[:half], total[half:]).astype(bf16)


def shrink_partial(down, parts, done=()):
    features, width = down.shape
    total = len(parts) * LANES
    kept = sum(d.shape[0] for d in done)
    return pl.pallas_call(
        functools.partial(shrink_body, kept),
        out_shape=jax.ShapeDtypeStruct((kept + total // 2, LANES), bf16),
        compiler_params=params(),
        cost_estimate=cost(2 * total * features * width, 2 * features * (total + width)),
        name="shrink_partial",
    )(down, *done, *parts)


def expand_body(count, one_ref, two_ref, up_ref, *refs):
    tags, outs = refs[:count], refs[count:]
    capacity = outs[0].shape[0]
    half = capacity // 2
    up = up_ref[...]
    first = iota((half, LANES), 1) < ADAPTER_RANK
    for k in range(count):
        part = pl.ds(k * half, half)
        shrink = (one_ref[part, :].astype(f32) + two_ref[part, :].astype(f32)).astype(bf16).astype(f32)
        turned = pltpu.roll(shrink, ADAPTER_RANK, 1)
        rows = jnp.concatenate([jnp.where(first, shrink, turned), jnp.where(first, turned, shrink)], axis=0)
        tag = tag_lanes(tags[k][...])
        spread = [
            jnp.where(slot_mask(tag, group), rows, 0.0).astype(bf16) for group in range(up.shape[0] // LANES)
        ]
        outs[k][...] = dot(jnp.concatenate(spread, axis=1), up).astype(bf16)


def expand(one, two, up, parts):
    capacity, count = LANES, len(parts)
    last = parts[0].shape[0] // TAG_ROWS - 1
    tag_block = pl.BlockSpec((TAG_ROWS, LANES), lambda i: (last, 0))
    whole = lambda a: pl.BlockSpec(a.shape, lambda i: (0, 0))
    columns = up.shape[1]
    return pl.pallas_call(
        functools.partial(expand_body, count),
        grid=(1,),
        out_shape=[jax.ShapeDtypeStruct((capacity, columns), bf16)] * count,
        in_specs=[whole(one), whole(two), whole(up)] + [tag_block] * count,
        out_specs=[pl.BlockSpec((capacity, columns), lambda i: (0, 0))] * count,
        compiler_params=params(),
        cost_estimate=cost(80 * count * capacity * up.size, 80 * (up.size + count * capacity * columns)),
        name="expand",
    )(one, two, up, *parts)


def deltas_body(unsort_ref, own_ref, *refs):
    deltas, out = refs[:-1], refs[-1]
    placed = dot(unsort_ref[...], jnp.concatenate([d[...] for d in deltas], axis=0))
    out[...] = own_ref[...].astype(f32) + placed


def with_deltas(unsort, deltas, own):
    rows, columns = own.shape
    return pl.pallas_call(
        deltas_body,
        out_shape=jax.ShapeDtypeStruct((rows, columns), f32),
        compiler_params=params(),
        cost_estimate=cost(2 * rows * unsort.shape[1] * columns, 12 * rows * columns),
        name="with_deltas",
    )(unsort, own, *deltas)


def finish_body(start_ref, *refs):
    terms, (out_hbm, out_buf, sem) = refs[:-3], refs[-3:]
    pieces = sem.shape[0]
    step = out_buf.shape[0] // pieces
    copies = []
    for k in range(pieces):
        part = pl.ds(k * step, step)
        total = start_ref[part, :]
        for term in terms:
            total += term[part, :].astype(f32)
        out_buf[part, :] = total.astype(bf16)
        copies.append(pltpu.make_async_copy(out_buf.at[part, :], out_hbm.at[part, :], sem.at[k]))
        copies[k].start()
    for copy in copies:
        copy.wait()


def finish(start, terms):
    vmem, hbm = (pl.BlockSpec(memory_space=m) for m in (pltpu.VMEM, pltpu.HBM))
    return pl.pallas_call(
        finish_body,
        out_shape=jax.ShapeDtypeStruct(start.shape, bf16),
        in_specs=[vmem] * (1 + len(terms)),
        out_specs=hbm,
        scratch_shapes=[pltpu.VMEM(start.shape, bf16), pltpu.SemaphoreType.DMA((4,))],
        compiler_params=params(),
        cost_estimate=cost(start.size, 8 * start.size),
        name="finish",
    )(start, *terms)


def both(a, b):
    return (a.astype(f32) + b.astype(f32)).astype(bf16)


def after(value, *others):
    return lax.optimization_barrier((value,) + others)[0]


def swap(value, axis, bit):
    return lax.ppermute(value, axis, [(i, i ^ bit) for i in range(lax.axis_size(axis))])


EDGE = [(0, 1), (3, 2)]
MIDDLE = [(1, 2), (2, 1)]


def tp_sums(mine, *before):
    sums, bit = [mine], 1
    while True:
        other = swap(sums[-1], "tp", bit)
        bit *= 2
        if bit >= lax.axis_size("tp"):
            return sums, other
        sums.append(both(after(sums[-1], *before), other))


def shards(x, ids, table, weight, down, up):
    holders = lax.axis_size("ad")
    capacity = x.shape[0] // 4
    assert capacity == LANES
    slots = up.shape[0] // ADAPTER_RANK
    width = up.shape[1]
    total = holders * capacity
    me, z = lax.axis_index("ad"), lax.axis_index("tp")
    spots, *far, x, w = far_rows(me, z, ids, table, x, weight, holders, slots, capacity, width)
    far = [swap(rows, "ad", j + NEAR) for j, rows in enumerate(far)]
    if lax.axis_size("tp") == 4 and holders == 4:
        first = first_block(x, w)
        edge0 = lax.ppermute(first, "tp", EDGE)
        *near, second, third, own, unsort = rest(z, after(spots, first), x, weight, width, total, capacity)
        near = [near[0], swap(near[1], "ad", 1)]
        edge1 = lax.ppermute(second, "tp", EDGE)
        early = shrink_partial(down, [near[0], far[0]])
        inner0 = both(after(first, early), edge0)
        middle0 = lax.ppermute(inner0, "tp", MIDDLE)
        early = shrink_partial(down, [after(near[1], inner0)], [early])
        mine = shrink_partial(down, [after(far[1], early)], [early])
        parts, order = [near[0], far[0], near[1], far[1]], (0, 2, 1, 3)
        inner1 = both(after(second, mine), edge1)
        steps, other = tp_sums(mine, inner1)
        inner2 = both(after(third, steps[-1]), middle0)
        last = swap(inner2, "tp", 1)
        middle1 = lax.ppermute(after(inner1, inner2), "tp", MIDDLE)
        sums = [middle1, last]
    else:
        near = near_rows(spots, x, capacity)
        near = [near[0], swap(near[1], "ad", 1)]
        parts, order = near + far, range(holders)
        unsort = unsort_only(spots, total)
        full = dot(x, weight).astype(bf16)
        own, sums = lax.psum_scatter(full, "tp", scatter_dimension=1, tiled=True), []
        steps, other = tp_sums(shrink_partial(down, parts))
    deltas = expand(steps[-1], other, up, parts)
    back = [None] * holders
    for j, delta in zip(order, deltas):
        back[j] = swap(delta, "ad", j) if j else delta
    return finish(with_deltas(unsort, back, own), sums)


def solution(mesh):
    in_specs = (
        P(("rep", "ad"), "tp"),
        P(("rep", "ad")),
        P("rep"),
        P("tp", None),
        P(("rep", "tp"), "ad"),
        P(("rep", "ad"), "tp"),
    )
    out_specs = P(("rep", "ad"), "tp")
    return jax.shard_map(shards, mesh=mesh, in_specs=in_specs, out_specs=out_specs, check_vma=False)
```

```python
import functools

import jax
import jax.numpy as jnp
from jax import lax
from jax.experimental import pallas as pl
from jax.experimental.pallas import tpu as pltpu
from jax.sharding import PartitionSpec as P

ADAPTER_RANK = 64
LANES = 128
NEAR = 2
TAG_ROWS = 16
VMEM_BYTES = 32 * 1024 * 1024

bf16 = jnp.bfloat16
f32 = jnp.float32
i32 = jnp.int32


def params():
    return pltpu.CompilerParams(vmem_limit_bytes=VMEM_BYTES)


def cost(flops, nbytes):
    return pl.CostEstimate(flops=flops, bytes_accessed=nbytes, transcendentals=0)


def dot(a, b, contract=((1,), (0,))):
    return lax.dot_general(a, b, (contract, ((), ())), preferred_element_type=f32)


def in_hbm(a):
    return pltpu.with_memory_space_constraint(a, pltpu.HBM)


def iota(shape, dim):
    return lax.broadcasted_iota(i32, shape, dim)


def places(slots, capacity, holders, me, ids, table):
    rows = ids.shape[1]
    low = (iota((LANES, rows), 0) == (ids & (LANES - 1))).astype(f32).astype(bf16)
    high = iota((table.shape[0], rows), 0) == lax.shift_right_logical(ids, 7)
    found = dot(table.astype(f32).astype(bf16), low)
    slot = jnp.sum(jnp.where(high, found, 0.0), axis=0, keepdims=True).astype(i32)
    holder = split_slot(slot, slots)
    tag = (slot - holder * slots + 1).astype(f32)
    partner = holder ^ me
    mine = iota((max(8, holders), rows), 0) == partner
    ones = mine.astype(f32)
    groups = [ones[:, k:k + LANES] for k in range(0, rows, LANES)]
    earlier = (iota((LANES, LANES), 0) < iota((LANES, LANES), 1)).astype(f32).astype(bf16)
    before = dot(jnp.concatenate(groups, axis=0).astype(bf16), earlier)
    count = ones.shape[0]
    ranks, passed = [], jnp.zeros((count, 1), f32)
    for k, group in enumerate(groups):
        ranks.append(jnp.sum(group * (before[k * count:(k + 1) * count] + passed), axis=0, keepdims=True))
        passed += jnp.sum(group, axis=1, keepdims=True)
    return partner * capacity + jnp.concatenate(ranks, axis=1).astype(i32), tag


def split_slot(slot, slots):
    if slots & (slots - 1):
        return lax.div(slot, slots)
    return lax.shift_right_logical(slot, slots.bit_length() - 1)


def pick_rows(start, place, tag, x, outs):
    rows, features = x.shape
    pick = iota((len(outs) * LANES, rows), 0) + start * LANES == place
    pick = pick.astype(f32).astype(bf16)
    tags = dot(jnp.broadcast_to(tag, (TAG_ROWS, rows)).astype(bf16), pick, ((1,), (1,))).astype(bf16)
    step = min(512, features)
    for c in range(0, features, step):
        moved = dot(pick, x[:, c:c + step]).astype(bf16)
        for j, out in enumerate(outs):
            for i in range(0, step, LANES):
                out[c + i:c + i + LANES, :] = moved[j * LANES:(j + 1) * LANES, i:i + LANES]
    for j, out in enumerate(outs):
        out[features:, :] = tags[:, j * LANES:(j + 1) * LANES]


def part_rows(part, features):
    return jnp.concatenate([part[c:c + LANES, :] for c in range(0, features, LANES)], axis=1)


def tag_lanes(tags):
    return jnp.broadcast_to(tags[0:1, :].astype(f32), (LANES, LANES)).T


def part_shape(features):
    return jax.ShapeDtypeStruct((features + TAG_ROWS, LANES), bf16)


def far_body(slots, capacity, holders, me_ref, z_ref, ids_hbm, table_hbm, x_hbm, w_hbm, places_ref, *refs):
    outs, (x_buf, w_buf, ids_buf, table_buf, small_sem, x_sem, w_sem) = refs[:holders - NEAR], refs[holders - NEAR:]
    width = w_buf.shape[1]
    small = [
        pltpu.make_async_copy(ids_hbm, ids_buf, small_sem.at[0]),
        pltpu.make_async_copy(table_hbm, table_buf, small_sem.at[1]),
    ]
    x_copy = pltpu.make_async_copy(x_hbm, x_buf, x_sem)
    column = pl.multiple_of(jnp.where(z_ref[0] < 2, 3, 0) * width, width)
    w_copy = pltpu.make_async_copy(w_hbm.at[:, pl.ds(column, width)], w_buf, w_sem)
    for copy in small + [x_copy, w_copy]:
        copy.start()
    for copy in small:
        copy.wait()
    place, tag = places(slots, capacity, holders, me_ref[0], ids_buf[...], table_buf[...])
    row = iota(places_ref.shape, 0)
    places_ref[...] = jnp.where(row == 0, place, jnp.where(row == 1, tag.astype(i32), 0))
    x_copy.wait()
    pick_rows(NEAR, place, tag, x_buf, outs)
    w_copy.wait()


def far_rows(me, z, ids, table, x, weight, holders, slots, capacity, width):
    rows, features = x.shape
    ids, table = ids.reshape(1, rows), table.reshape(-1, LANES)
    smem, vmem, hbm = (pl.BlockSpec(memory_space=m) for m in (pltpu.SMEM, pltpu.VMEM, pltpu.HBM))
    shapes = [jax.ShapeDtypeStruct((8, rows), i32)]
    shapes += [part_shape(features)] * (holders - NEAR)
    shapes += [jax.ShapeDtypeStruct((rows, features), bf16), jax.ShapeDtypeStruct((features, width), bf16)]
    return pl.pallas_call(
        functools.partial(far_body, slots, capacity, holders),
        out_shape=shapes,
        in_specs=[smem, smem, hbm, hbm, hbm, hbm],
        out_specs=[vmem] * len(shapes),
        scratch_shapes=[
            pltpu.VMEM(ids.shape, i32),
            pltpu.VMEM(table.shape, i32),
            pltpu.SemaphoreType.DMA((2,)),
            pltpu.SemaphoreType.DMA(()),
            pltpu.SemaphoreType.DMA(()),
        ],
        compiler_params=params(),
        cost_estimate=cost(2 * holders * capacity * rows * features, 4 * rows * features),
        name="far_rows",
    )(me.reshape(1), z.reshape(1), in_hbm(ids), in_hbm(table), in_hbm(x), in_hbm(weight))


def near_body(places_ref, x_ref, *outs):
    pick_rows(0, places_ref[0:1, :], places_ref[1:2, :].astype(f32), x_ref, outs)


def near_rows(spots, x, capacity):
    rows, features = x.shape
    return pl.pallas_call(
        near_body,
        out_shape=[part_shape(features)] * NEAR,
        compiler_params=params(),
        cost_estimate=cost(2 * NEAR * capacity * rows * features, 4 * rows * features),
        name="near_rows",
    )(spots, x)


def first_body(x_ref, w_ref, out):
    out[...] = dot(x_ref[...], w_ref[...]).astype(bf16)


def first_block(x, w):
    (rows, features), width = x.shape, w.shape[1]
    return pl.pallas_call(
        first_body,
        out_shape=jax.ShapeDtypeStruct((rows, width), bf16),
        compiler_params=params(),
        cost_estimate=cost(2 * rows * features * width, 2 * features * (rows + width)),
        name="first_block",
    )(x, w)


def rest_body(z_ref, spots_ref, x_ref, w_hbm, *refs):
    near, (second, third, own, unsort, w_buf, sem) = refs[:NEAR], refs[NEAR:]
    z = z_ref[0]
    width = own.shape[1]
    copies = []
    for k, block in enumerate((jnp.where(z < 2, 2, 1), z ^ 1, z)):
        column = pl.multiple_of(block * width, width)
        copies.append(pltpu.make_async_copy(w_hbm.at[:, pl.ds(column, width)], w_buf.at[k], sem.at[k]))
        copies[k].start()
    near_body(spots_ref, x_ref, *near)
    unsort_matrix(spots_ref, unsort)
    for k, out in enumerate((second, third, own)):
        copies[k].wait()
        out[...] = dot(x_ref[...], w_buf[k]).astype(bf16)


def unsort_matrix(place_ref, unsort):
    rows, total = unsort.shape
    place = jnp.broadcast_to(place_ref[0:1, :].astype(f32), (LANES, rows)).T
    lane = iota((rows, LANES), 1).astype(f32)
    for k in range(total // LANES):
        unsort[:, k * LANES:(k + 1) * LANES] = (place == lane + float(k * LANES)).astype(f32).astype(bf16)


def rest(z, spots, x, weight, width, total, capacity):
    rows, features = x.shape
    smem, vmem, hbm = (pl.BlockSpec(memory_space=m) for m in (pltpu.SMEM, pltpu.VMEM, pltpu.HBM))
    shapes = [part_shape(features)] * NEAR
    shapes += [jax.ShapeDtypeStruct((rows, width), bf16)] * 3 + [jax.ShapeDtypeStruct((rows, total), bf16)]
    return pl.pallas_call(
        rest_body,
        out_shape=shapes,
        in_specs=[smem, vmem, vmem, hbm],
        out_specs=[vmem] * len(shapes),
        scratch_shapes=[pltpu.VMEM((3, features, width), bf16), pltpu.SemaphoreType.DMA((3,))],
        compiler_params=params(),
        cost_estimate=cost(6 * rows * features * width, 2 * features * (rows + 4 * width)),
        name="rest",
    )(z.reshape(1), spots, x, in_hbm(weight))


def unsort_only(place, total):
    return pl.pallas_call(
        unsort_matrix,
        out_shape=jax.ShapeDtypeStruct((place.shape[1], total), bf16),
        compiler_params=params(),
        name="unsort",
    )(place)


def slot_mask(tag, group):
    lane = iota(tag.shape, 1)
    return tag == jnp.where(lane < ADAPTER_RANK, 2 * group + 1, 2 * group + 2).astype(f32)


def shrink_body(kept, down_ref, *refs):
    parts, out = refs[1 if kept else 0:-1], refs[-1]
    features, width = down_ref.shape
    half = LANES // 2
    first = iota((half, LANES), 1) < ADAPTER_RANK
    if kept:
        out[:kept, :] = refs[0][...]
    for k, part in enumerate(parts):
        tag = tag_lanes(part[features:, :])
        full = dot(part_rows(part, features), down_ref[...])
        total = jnp.zeros((LANES, LANES), f32)
        for group in range(width // LANES):
            total += jnp.where(slot_mask(tag, group), full[:, group * LANES:(group + 1) * LANES], 0.0)
        total += pltpu.roll(total, ADAPTER_RANK, 1)
        spot = slice(kept + k * half, kept + (k + 1) * half)
        out[spot, :] = jnp.where(first, total[:half], total[half:]).astype(bf16)


def shrink_partial(down, parts, done=()):
    features, width = down.shape
    total = len(parts) * LANES
    kept = sum(d.shape[0] for d in done)
    return pl.pallas_call(
        functools.partial(shrink_body, kept),
        out_shape=jax.ShapeDtypeStruct((kept + total // 2, LANES), bf16),
        compiler_params=params(),
        cost_estimate=cost(2 * total * features * width, 2 * features * (total + width)),
        name="shrink_partial",
    )(down, *done, *parts)


def expand_body(count, one_ref, two_ref, up_ref, *refs):
    tags, outs = refs[:count], refs[count:]
    capacity = outs[0].shape[0]
    half = capacity // 2
    up = up_ref[...]
    first = iota((half, LANES), 1) < ADAPTER_RANK
    for k in range(count):
        part = pl.ds(k * half, half)
        shrink = (one_ref[part, :].astype(f32) + two_ref[part, :].astype(f32)).astype(bf16).astype(f32)
        turned = pltpu.roll(shrink, ADAPTER_RANK, 1)
        rows = jnp.concatenate([jnp.where(first, shrink, turned), jnp.where(first, turned, shrink)], axis=0)
        tag = tag_lanes(tags[k][...])
        spread = [
            jnp.where(slot_mask(tag, group), rows, 0.0).astype(bf16) for group in range(up.shape[0] // LANES)
        ]
        outs[k][...] = dot(jnp.concatenate(spread, axis=1), up).astype(bf16)


def expand(one, two, up, parts):
    capacity, count = LANES, len(parts)
    last = parts[0].shape[0] // TAG_ROWS - 1
    tag_block = pl.BlockSpec((TAG_ROWS, LANES), lambda i: (last, 0))
    whole = lambda a: pl.BlockSpec(a.shape, lambda i: (0, 0))
    columns = up.shape[1]
    return pl.pallas_call(
        functools.partial(expand_body, count),
        grid=(1,),
        out_shape=[jax.ShapeDtypeStruct((capacity, columns), bf16)] * count,
        in_specs=[whole(one), whole(two), whole(up)] + [tag_block] * count,
        out_specs=[pl.BlockSpec((capacity, columns), lambda i: (0, 0))] * count,
        compiler_params=params(),
        cost_estimate=cost(80 * count * capacity * up.size, 80 * (up.size + count * capacity * columns)),
        name="expand",
    )(one, two, up, *parts)


def deltas_body(unsort_ref, own_ref, *refs):
    deltas, out = refs[:-1], refs[-1]
    placed = dot(unsort_ref[...], jnp.concatenate([d[...] for d in deltas], axis=0))
    out[...] = own_ref[...].astype(f32) + placed


def with_deltas(unsort, deltas, own):
    rows, columns = own.shape
    return pl.pallas_call(
        deltas_body,
        out_shape=jax.ShapeDtypeStruct((rows, columns), f32),
        compiler_params=params(),
        cost_estimate=cost(2 * rows * unsort.shape[1] * columns, 12 * rows * columns),
        name="with_deltas",
    )(unsort, own, *deltas)


def finish_body(start_ref, *refs):
    terms, (out_hbm, out_buf, sem) = refs[:-3], refs[-3:]
    pieces = sem.shape[0]
    step = out_buf.shape[0] // pieces
    copies = []
    for k in range(pieces):
        part = pl.ds(k * step, step)
        total = start_ref[part, :]
        for term in terms:
            total += term[part, :].astype(f32)
        out_buf[part, :] = total.astype(bf16)
        copies.append(pltpu.make_async_copy(out_buf.at[part, :], out_hbm.at[part, :], sem.at[k]))
        copies[k].start()
    for copy in copies:
        copy.wait()


def finish(start, terms):
    vmem, hbm = (pl.BlockSpec(memory_space=m) for m in (pltpu.VMEM, pltpu.HBM))
    return pl.pallas_call(
        finish_body,
        out_shape=jax.ShapeDtypeStruct(start.shape, bf16),
        in_specs=[vmem] * (1 + len(terms)),
        out_specs=hbm,
        scratch_shapes=[pltpu.VMEM(start.shape, bf16), pltpu.SemaphoreType.DMA((4,))],
        compiler_params=params(),
        cost_estimate=cost(start.size, 8 * start.size),
        name="finish",
    )(start, *terms)


def both(a, b):
    return (a.astype(f32) + b.astype(f32)).astype(bf16)


def after(value, *others):
    return lax.optimization_barrier((value,) + others)[0]


def swap(value, axis, bit):
    return lax.ppermute(value, axis, [(i, i ^ bit) for i in range(lax.axis_size(axis))])


EDGE = [(0, 1), (3, 2)]
MIDDLE = [(1, 2), (2, 1)]


def tp_sums(mine, *before):
    sums, bit = [mine], 1
    while True:
        other = swap(sums[-1], "tp", bit)
        bit *= 2
        if bit >= lax.axis_size("tp"):
            return sums, other
        sums.append(both(after(sums[-1], *before), other))


def shards(x, ids, table, weight, down, up):
    holders = lax.axis_size("ad")
    capacity = x.shape[0] // 4
    assert capacity == LANES
    slots = up.shape[0] // ADAPTER_RANK
    width = up.shape[1]
    total = holders * capacity
    me, z = lax.axis_index("ad"), lax.axis_index("tp")
    spots, *far, x, w = far_rows(me, z, ids, table, x, weight, holders, slots, capacity, width)
    if lax.axis_size("tp") == 4 and holders == 4:
        first = first_block(x, w)
        edge0 = lax.ppermute(first, "tp", EDGE)
        far = [swap(after(rows, first), "ad", j + NEAR) for j, rows in enumerate(far)]
        *near, second, third, own, unsort = rest(z, after(spots, first), x, weight, width, total, capacity)
        near = [near[0], swap(near[1], "ad", 1)]
        edge1 = lax.ppermute(second, "tp", EDGE)
        inner0 = both(first, edge0)
        middle0 = lax.ppermute(inner0, "tp", MIDDLE)
        early = shrink_partial(down, [near[0], after(far[0], inner0)])
        early = shrink_partial(down, [after(near[1], inner0)], [early])
        mine = shrink_partial(down, [after(far[1], early)], [early])
        parts, order = [near[0], far[0], near[1], far[1]], (0, 2, 1, 3)
        inner1 = both(after(second, mine), edge1)
        steps, other = tp_sums(mine, inner1)
        inner2 = both(after(third, steps[-1]), middle0)
        last = swap(inner2, "tp", 1)
        middle1 = lax.ppermute(after(inner1, inner2), "tp", MIDDLE)
        sums = [middle1, last]
    else:
        far = [swap(rows, "ad", j + NEAR) for j, rows in enumerate(far)]
        near = near_rows(spots, x, capacity)
        near = [near[0], swap(near[1], "ad", 1)]
        parts, order = near + far, range(holders)
        unsort = unsort_only(spots, total)
        full = dot(x, weight).astype(bf16)
        own, sums = lax.psum_scatter(full, "tp", scatter_dimension=1, tiled=True), []
        steps, other = tp_sums(shrink_partial(down, parts))
    deltas = expand(steps[-1], other, up, parts)
    back = [None] * holders
    for j, delta in zip(order, deltas):
        back[j] = swap(delta, "ad", j) if j else delta
    return finish(with_deltas(unsort, back, own), sums)


def solution(mesh):
    in_specs = (
        P(("rep", "ad"), "tp"),
        P(("rep", "ad")),
        P("rep"),
        P("tp", None),
        P(("rep", "tp"), "ad"),
        P(("rep", "ad"), "tp"),
    )
    out_specs = P(("rep", "ad"), "tp")
    return jax.shard_map(shards, mesh=mesh, in_specs=in_specs, out_specs=out_specs, check_vma=False)
```

```python
import functools

import jax
import jax.numpy as jnp
from jax import lax
from jax.experimental import pallas as pl
from jax.experimental.pallas import tpu as pltpu
from jax.sharding import PartitionSpec as P

ADAPTER_RANK = 64
LANES = 128
NEAR = 2
TAG_ROWS = 16
VMEM_BYTES = 32 * 1024 * 1024

bf16 = jnp.bfloat16
f32 = jnp.float32
i32 = jnp.int32


def params():
    return pltpu.CompilerParams(vmem_limit_bytes=VMEM_BYTES)


def cost(flops, nbytes):
    return pl.CostEstimate(flops=flops, bytes_accessed=nbytes, transcendentals=0)


def dot(a, b, contract=((1,), (0,))):
    return lax.dot_general(a, b, (contract, ((), ())), preferred_element_type=f32)


def in_hbm(a):
    return pltpu.with_memory_space_constraint(a, pltpu.HBM)


def iota(shape, dim):
    return lax.broadcasted_iota(i32, shape, dim)


def places(slots, capacity, holders, me, ids, table):
    rows = ids.shape[1]
    low = (iota((LANES, rows), 0) == (ids & (LANES - 1))).astype(f32).astype(bf16)
    high = iota((table.shape[0], rows), 0) == lax.shift_right_logical(ids, 7)
    found = dot(table.astype(f32).astype(bf16), low)
    slot = jnp.sum(jnp.where(high, found, 0.0), axis=0, keepdims=True).astype(i32)
    holder = split_slot(slot, slots)
    tag = (slot - holder * slots + 1).astype(f32)
    partner = holder ^ me
    mine = iota((max(8, holders), rows), 0) == partner
    ones = mine.astype(f32)
    groups = [ones[:, k:k + LANES] for k in range(0, rows, LANES)]
    earlier = (iota((LANES, LANES), 0) < iota((LANES, LANES), 1)).astype(f32).astype(bf16)
    before = dot(jnp.concatenate(groups, axis=0).astype(bf16), earlier)
    count = ones.shape[0]
    ranks, passed = [], jnp.zeros((count, 1), f32)
    for k, group in enumerate(groups):
        ranks.append(jnp.sum(group * (before[k * count:(k + 1) * count] + passed), axis=0, keepdims=True))
        passed += jnp.sum(group, axis=1, keepdims=True)
    return partner * capacity + jnp.concatenate(ranks, axis=1).astype(i32), tag


def split_slot(slot, slots):
    if slots & (slots - 1):
        return lax.div(slot, slots)
    return lax.shift_right_logical(slot, slots.bit_length() - 1)


def pick_rows(start, place, tag, x, outs):
    rows, features = x.shape
    pick = iota((len(outs) * LANES, rows), 0) + start * LANES == place
    pick = pick.astype(f32).astype(bf16)
    tags = dot(jnp.broadcast_to(tag, (TAG_ROWS, rows)).astype(bf16), pick, ((1,), (1,))).astype(bf16)
    step = min(512, features)
    for c in range(0, features, step):
        moved = dot(pick, x[:, c:c + step]).astype(bf16)
        for j, out in enumerate(outs):
            for i in range(0, step, LANES):
                out[c + i:c + i + LANES, :] = moved[j * LANES:(j + 1) * LANES, i:i + LANES]
    for j, out in enumerate(outs):
        out[features:, :] = tags[:, j * LANES:(j + 1) * LANES]


def part_rows(part, features):
    return jnp.concatenate([part[c:c + LANES, :] for c in range(0, features, LANES)], axis=1)


def tag_lanes(tags):
    return jnp.broadcast_to(tags[0:1, :].astype(f32), (LANES, LANES)).T


def part_shape(features):
    return jax.ShapeDtypeStruct((features + TAG_ROWS, LANES), bf16)


def far_body(slots, capacity, holders, me_ref, z_ref, ids_hbm, table_hbm, x_hbm, w_hbm, places_ref, *refs):
    outs, (x_buf, w_buf, ids_buf, table_buf, small_sem, x_sem, w_sem) = refs[:holders - NEAR], refs[holders - NEAR:]
    width = w_buf.shape[1]
    small = [
        pltpu.make_async_copy(ids_hbm, ids_buf, small_sem.at[0]),
        pltpu.make_async_copy(table_hbm, table_buf, small_sem.at[1]),
    ]
    x_copy = pltpu.make_async_copy(x_hbm, x_buf, x_sem)
    column = pl.multiple_of(jnp.where(z_ref[0] < 2, 3, 0) * width, width)
    w_copy = pltpu.make_async_copy(w_hbm.at[:, pl.ds(column, width)], w_buf, w_sem)
    for copy in small + [x_copy, w_copy]:
        copy.start()
    for copy in small:
        copy.wait()
    place, tag = places(slots, capacity, holders, me_ref[0], ids_buf[...], table_buf[...])
    row = iota(places_ref.shape, 0)
    places_ref[...] = jnp.where(row == 0, place, jnp.where(row == 1, tag.astype(i32), 0))
    x_copy.wait()
    pick_rows(NEAR, place, tag, x_buf, outs)
    w_copy.wait()


def far_rows(me, z, ids, table, x, weight, holders, slots, capacity, width):
    rows, features = x.shape
    ids, table = ids.reshape(1, rows), table.reshape(-1, LANES)
    smem, vmem, hbm = (pl.BlockSpec(memory_space=m) for m in (pltpu.SMEM, pltpu.VMEM, pltpu.HBM))
    shapes = [jax.ShapeDtypeStruct((8, rows), i32)]
    shapes += [part_shape(features)] * (holders - NEAR)
    shapes += [jax.ShapeDtypeStruct((rows, features), bf16), jax.ShapeDtypeStruct((features, width), bf16)]
    return pl.pallas_call(
        functools.partial(far_body, slots, capacity, holders),
        out_shape=shapes,
        in_specs=[smem, smem, hbm, hbm, hbm, hbm],
        out_specs=[vmem] * len(shapes),
        scratch_shapes=[
            pltpu.VMEM(ids.shape, i32),
            pltpu.VMEM(table.shape, i32),
            pltpu.SemaphoreType.DMA((2,)),
            pltpu.SemaphoreType.DMA(()),
            pltpu.SemaphoreType.DMA(()),
        ],
        compiler_params=params(),
        cost_estimate=cost(2 * holders * capacity * rows * features, 4 * rows * features),
        name="far_rows",
    )(me.reshape(1), z.reshape(1), in_hbm(ids), in_hbm(table), in_hbm(x), in_hbm(weight))


def near_body(places_ref, x_ref, *outs):
    pick_rows(0, places_ref[0:1, :], places_ref[1:2, :].astype(f32), x_ref, outs)


def near_rows(spots, x, capacity):
    rows, features = x.shape
    return pl.pallas_call(
        near_body,
        out_shape=[part_shape(features)] * NEAR,
        compiler_params=params(),
        cost_estimate=cost(2 * NEAR * capacity * rows * features, 4 * rows * features),
        name="near_rows",
    )(spots, x)


def first_body(x_ref, w_ref, out):
    out[...] = dot(x_ref[...], w_ref[...]).astype(bf16)


def first_block(x, w):
    (rows, features), width = x.shape, w.shape[1]
    return pl.pallas_call(
        first_body,
        out_shape=jax.ShapeDtypeStruct((rows, width), bf16),
        compiler_params=params(),
        cost_estimate=cost(2 * rows * features * width, 2 * features * (rows + width)),
        name="first_block",
    )(x, w)


def rest_body(z_ref, spots_ref, x_ref, w_hbm, *refs):
    near, (second, third, own, unsort, w_buf, sem) = refs[:NEAR], refs[NEAR:]
    z = z_ref[0]
    width = own.shape[1]
    copies = []
    for k, block in enumerate((jnp.where(z < 2, 2, 1), z ^ 1, z)):
        column = pl.multiple_of(block * width, width)
        copies.append(pltpu.make_async_copy(w_hbm.at[:, pl.ds(column, width)], w_buf.at[k], sem.at[k]))
        copies[k].start()
    near_body(spots_ref, x_ref, *near)
    unsort_matrix(spots_ref, unsort)
    for k, out in enumerate((second, third, own)):
        copies[k].wait()
        out[...] = dot(x_ref[...], w_buf[k]).astype(bf16)


def unsort_matrix(place_ref, unsort):
    rows, total = unsort.shape
    place = jnp.broadcast_to(place_ref[0:1, :].astype(f32), (LANES, rows)).T
    lane = iota((rows, LANES), 1).astype(f32)
    for k in range(total // LANES):
        unsort[:, k * LANES:(k + 1) * LANES] = (place == lane + float(k * LANES)).astype(f32).astype(bf16)


def rest(z, spots, x, weight, width, total, capacity):
    rows, features = x.shape
    smem, vmem, hbm = (pl.BlockSpec(memory_space=m) for m in (pltpu.SMEM, pltpu.VMEM, pltpu.HBM))
    shapes = [part_shape(features)] * NEAR
    shapes += [jax.ShapeDtypeStruct((rows, width), bf16)] * 3 + [jax.ShapeDtypeStruct((rows, total), bf16)]
    return pl.pallas_call(
        rest_body,
        out_shape=shapes,
        in_specs=[smem, vmem, vmem, hbm],
        out_specs=[vmem] * len(shapes),
        scratch_shapes=[pltpu.VMEM((3, features, width), bf16), pltpu.SemaphoreType.DMA((3,))],
        compiler_params=params(),
        cost_estimate=cost(6 * rows * features * width, 2 * features * (rows + 4 * width)),
        name="rest",
    )(z.reshape(1), spots, x, in_hbm(weight))


def unsort_only(place, total):
    return pl.pallas_call(
        unsort_matrix,
        out_shape=jax.ShapeDtypeStruct((place.shape[1], total), bf16),
        compiler_params=params(),
        name="unsort",
    )(place)


def slot_mask(tag, group):
    lane = iota(tag.shape, 1)
    return tag == jnp.where(lane < ADAPTER_RANK, 2 * group + 1, 2 * group + 2).astype(f32)


def shrink_body(kept, down_ref, *refs):
    parts, out = refs[1 if kept else 0:-1], refs[-1]
    features, width = down_ref.shape
    half = LANES // 2
    first = iota((half, LANES), 1) < ADAPTER_RANK
    if kept:
        out[:kept, :] = refs[0][...]
    for k, part in enumerate(parts):
        tag = tag_lanes(part[features:, :])
        full = dot(part_rows(part, features), down_ref[...])
        total = jnp.zeros((LANES, LANES), f32)
        for group in range(width // LANES):
            total += jnp.where(slot_mask(tag, group), full[:, group * LANES:(group + 1) * LANES], 0.0)
        total += pltpu.roll(total, ADAPTER_RANK, 1)
        spot = slice(kept + k * half, kept + (k + 1) * half)
        out[spot, :] = jnp.where(first, total[:half], total[half:]).astype(bf16)


def shrink_partial(down, parts, done=()):
    features, width = down.shape
    total = len(parts) * LANES
    kept = sum(d.shape[0] for d in done)
    return pl.pallas_call(
        functools.partial(shrink_body, kept),
        out_shape=jax.ShapeDtypeStruct((kept + total // 2, LANES), bf16),
        compiler_params=params(),
        cost_estimate=cost(2 * total * features * width, 2 * features * (total + width)),
        name="shrink_partial",
    )(down, *done, *parts)


def expand_body(count, one_ref, two_ref, up_ref, *refs):
    tags, outs = refs[:count], refs[count:]
    capacity = outs[0].shape[0]
    half = capacity // 2
    up = up_ref[...]
    first = iota((half, LANES), 1) < ADAPTER_RANK
    for k in range(count):
        part = pl.ds(k * half, half)
        shrink = (one_ref[part, :].astype(f32) + two_ref[part, :].astype(f32)).astype(bf16).astype(f32)
        turned = pltpu.roll(shrink, ADAPTER_RANK, 1)
        rows = jnp.concatenate([jnp.where(first, shrink, turned), jnp.where(first, turned, shrink)], axis=0)
        tag = tag_lanes(tags[k][...])
        spread = [
            jnp.where(slot_mask(tag, group), rows, 0.0).astype(bf16) for group in range(up.shape[0] // LANES)
        ]
        outs[k][...] = dot(jnp.concatenate(spread, axis=1), up).astype(bf16)


def expand(one, two, up, parts):
    capacity, count = LANES, len(parts)
    last = parts[0].shape[0] // TAG_ROWS - 1
    tag_block = pl.BlockSpec((TAG_ROWS, LANES), lambda i: (last, 0))
    whole = lambda a: pl.BlockSpec(a.shape, lambda i: (0, 0))
    columns = up.shape[1]
    return pl.pallas_call(
        functools.partial(expand_body, count),
        grid=(1,),
        out_shape=[jax.ShapeDtypeStruct((capacity, columns), bf16)] * count,
        in_specs=[whole(one), whole(two), whole(up)] + [tag_block] * count,
        out_specs=[pl.BlockSpec((capacity, columns), lambda i: (0, 0))] * count,
        compiler_params=params(),
        cost_estimate=cost(80 * count * capacity * up.size, 80 * (up.size + count * capacity * columns)),
        name="expand",
    )(one, two, up, *parts)


def deltas_body(unsort_ref, own_ref, *refs):
    deltas, out = refs[:-1], refs[-1]
    placed = dot(unsort_ref[...], jnp.concatenate([d[...] for d in deltas], axis=0))
    out[...] = own_ref[...].astype(f32) + placed


def with_deltas(unsort, deltas, own):
    rows, columns = own.shape
    return pl.pallas_call(
        deltas_body,
        out_shape=jax.ShapeDtypeStruct((rows, columns), f32),
        compiler_params=params(),
        cost_estimate=cost(2 * rows * unsort.shape[1] * columns, 12 * rows * columns),
        name="with_deltas",
    )(unsort, own, *deltas)


def finish_body(start_ref, *refs):
    terms, (out_hbm, out_buf, sem) = refs[:-3], refs[-3:]
    pieces = sem.shape[0]
    step = out_buf.shape[0] // pieces
    copies = []
    for k in range(pieces):
        part = pl.ds(k * step, step)
        total = start_ref[part, :]
        for term in terms:
            total += term[part, :].astype(f32)
        out_buf[part, :] = total.astype(bf16)
        copies.append(pltpu.make_async_copy(out_buf.at[part, :], out_hbm.at[part, :], sem.at[k]))
        copies[k].start()
    for copy in copies:
        copy.wait()


def finish(start, terms):
    vmem, hbm = (pl.BlockSpec(memory_space=m) for m in (pltpu.VMEM, pltpu.HBM))
    return pl.pallas_call(
        finish_body,
        out_shape=jax.ShapeDtypeStruct(start.shape, bf16),
        in_specs=[vmem] * (1 + len(terms)),
        out_specs=hbm,
        scratch_shapes=[pltpu.VMEM(start.shape, bf16), pltpu.SemaphoreType.DMA((4,))],
        compiler_params=params(),
        cost_estimate=cost(start.size, 8 * start.size),
        name="finish",
    )(start, *terms)


def both(a, b):
    return (a.astype(f32) + b.astype(f32)).astype(bf16)


def after(value, *others):
    return lax.optimization_barrier((value,) + others)[0]


def swap(value, axis, bit):
    return lax.ppermute(value, axis, [(i, i ^ bit) for i in range(lax.axis_size(axis))])


EDGE = [(0, 1), (3, 2)]
MIDDLE = [(1, 2), (2, 1)]


def tp_sums(mine, *before):
    sums, bit = [mine], 1
    while True:
        other = swap(sums[-1], "tp", bit)
        bit *= 2
        if bit >= lax.axis_size("tp"):
            return sums, other
        sums.append(both(after(sums[-1], *before), other))


def shards(x, ids, table, weight, down, up):
    holders = lax.axis_size("ad")
    capacity = x.shape[0] // 4
    assert capacity == LANES
    slots = up.shape[0] // ADAPTER_RANK
    width = up.shape[1]
    total = holders * capacity
    me, z = lax.axis_index("ad"), lax.axis_index("tp")
    spots, *far, x, w = far_rows(me, z, ids, table, x, weight, holders, slots, capacity, width)
    far = [swap(rows, "ad", j + NEAR) for j, rows in enumerate(far)]
    if lax.axis_size("tp") == 4 and holders == 4:
        first = first_block(x, w)
        edge0 = lax.ppermute(first, "tp", EDGE)
        *near, second, third, own, unsort = rest(z, after(spots, first), x, weight, width, total, capacity)
        edge1 = lax.ppermute(second, "tp", EDGE)
        early = shrink_partial(down, [near[0], far[0]])
        partner = swap(after(near[1], early), "ad", 1)
        inner0 = both(after(first, early), edge0)
        middle0 = lax.ppermute(inner0, "tp", MIDDLE)
        mine = shrink_partial(down, [after(partner, inner0), after(far[1], inner0)], [early])
        parts, order = [near[0], far[0], partner, far[1]], (0, 2, 1, 3)
        inner1 = both(after(second, mine), edge1)
        steps, other = tp_sums(mine, inner1)
        inner2 = both(after(third, steps[-1]), middle0)
        last = swap(inner2, "tp", 1)
        middle1 = lax.ppermute(after(inner1, inner2), "tp", MIDDLE)
        sums = [middle1, last]
    else:
        near = near_rows(spots, x, capacity)
        near = [near[0], swap(near[1], "ad", 1)]
        parts, order = near + far, range(holders)
        unsort = unsort_only(spots, total)
        full = dot(x, weight).astype(bf16)
        own, sums = lax.psum_scatter(full, "tp", scatter_dimension=1, tiled=True), []
        steps, other = tp_sums(shrink_partial(down, parts))
    deltas = expand(steps[-1], other, up, parts)
    back = [None] * holders
    for j, delta in zip(order, deltas):
        back[j] = swap(delta, "ad", j) if j else delta
    return finish(with_deltas(unsort, back, own), sums)


def solution(mesh):
    in_specs = (
        P(("rep", "ad"), "tp"),
        P(("rep", "ad")),
        P("rep"),
        P("tp", None),
        P(("rep", "tp"), "ad"),
        P(("rep", "ad"), "tp"),
    )
    out_specs = P(("rep", "ad"), "tp")
    return jax.shard_map(shards, mesh=mesh, in_specs=in_specs, out_specs=out_specs, check_vma=False)
```

```python
import functools

import jax
import jax.numpy as jnp
from jax import lax
from jax.experimental import pallas as pl
from jax.experimental.pallas import tpu as pltpu
from jax.sharding import PartitionSpec as P

ADAPTER_RANK = 64
LANES = 128
NEAR = 2
TAG_ROWS = 16
VMEM_BYTES = 32 * 1024 * 1024

bf16 = jnp.bfloat16
f32 = jnp.float32
i32 = jnp.int32


def params():
    return pltpu.CompilerParams(vmem_limit_bytes=VMEM_BYTES)


def cost(flops, nbytes):
    return pl.CostEstimate(flops=flops, bytes_accessed=nbytes, transcendentals=0)


def dot(a, b, contract=((1,), (0,))):
    return lax.dot_general(a, b, (contract, ((), ())), preferred_element_type=f32)


def in_hbm(a):
    return pltpu.with_memory_space_constraint(a, pltpu.HBM)


def iota(shape, dim):
    return lax.broadcasted_iota(i32, shape, dim)


def places(slots, capacity, holders, me, ids, table):
    rows = ids.shape[1]
    low = (iota((LANES, rows), 0) == (ids & (LANES - 1))).astype(f32).astype(bf16)
    high = iota((table.shape[0], rows), 0) == lax.shift_right_logical(ids, 7)
    found = dot(table.astype(f32).astype(bf16), low)
    slot = jnp.sum(jnp.where(high, found, 0.0), axis=0, keepdims=True).astype(i32)
    holder = split_slot(slot, slots)
    tag = (slot - holder * slots + 1).astype(f32)
    partner = holder ^ me
    mine = iota((max(8, holders), rows), 0) == partner
    ones = mine.astype(f32)
    groups = [ones[:, k:k + LANES] for k in range(0, rows, LANES)]
    earlier = (iota((LANES, LANES), 0) < iota((LANES, LANES), 1)).astype(f32).astype(bf16)
    before = dot(jnp.concatenate(groups, axis=0).astype(bf16), earlier)
    count = ones.shape[0]
    ranks, passed = [], jnp.zeros((count, 1), f32)
    for k, group in enumerate(groups):
        ranks.append(jnp.sum(group * (before[k * count:(k + 1) * count] + passed), axis=0, keepdims=True))
        passed += jnp.sum(group, axis=1, keepdims=True)
    return partner * capacity + jnp.concatenate(ranks, axis=1).astype(i32), tag


def split_slot(slot, slots):
    if slots & (slots - 1):
        return lax.div(slot, slots)
    return lax.shift_right_logical(slot, slots.bit_length() - 1)


def pick_rows(start, place, tag, x, outs):
    rows, features = x.shape
    pick = iota((len(outs) * LANES, rows), 0) + start * LANES == place
    pick = pick.astype(f32).astype(bf16)
    tags = dot(jnp.broadcast_to(tag, (TAG_ROWS, rows)).astype(bf16), pick, ((1,), (1,))).astype(bf16)
    step = min(512, features)
    for c in range(0, features, step):
        moved = dot(pick, x[:, c:c + step]).astype(bf16)
        for j, out in enumerate(outs):
            for i in range(0, step, LANES):
                out[c + i:c + i + LANES, :] = moved[j * LANES:(j + 1) * LANES, i:i + LANES]
    for j, out in enumerate(outs):
        out[features:, :] = tags[:, j * LANES:(j + 1) * LANES]


def part_rows(part, features):
    return jnp.concatenate([part[c:c + LANES, :] for c in range(0, features, LANES)], axis=1)


def tag_lanes(tags):
    return jnp.broadcast_to(tags[0:1, :].astype(f32), (LANES, LANES)).T


def part_shape(features):
    return jax.ShapeDtypeStruct((features + TAG_ROWS, LANES), bf16)


def far_body(slots, capacity, holders, me_ref, z_ref, ids_hbm, table_hbm, x_hbm, w_hbm, places_ref, *refs):
    outs, (x_buf, w_buf, ids_buf, table_buf, small_sem, x_sem, w_sem) = refs[:holders - NEAR], refs[holders - NEAR:]
    width = w_buf.shape[1]
    small = [
        pltpu.make_async_copy(ids_hbm, ids_buf, small_sem.at[0]),
        pltpu.make_async_copy(table_hbm, table_buf, small_sem.at[1]),
    ]
    x_copy = pltpu.make_async_copy(x_hbm, x_buf, x_sem)
    column = pl.multiple_of(jnp.where(z_ref[0] < 2, 3, 0) * width, width)
    w_copy = pltpu.make_async_copy(w_hbm.at[:, pl.ds(column, width)], w_buf, w_sem)
    for copy in small + [x_copy, w_copy]:
        copy.start()
    for copy in small:
        copy.wait()
    place, tag = places(slots, capacity, holders, me_ref[0], ids_buf[...], table_buf[...])
    row = iota(places_ref.shape, 0)
    places_ref[...] = jnp.where(row == 0, place, jnp.where(row == 1, tag.astype(i32), 0))
    x_copy.wait()
    pick_rows(NEAR, place, tag, x_buf, outs)
    w_copy.wait()


def far_rows(me, z, ids, table, x, weight, holders, slots, capacity, width):
    rows, features = x.shape
    ids, table = ids.reshape(1, rows), table.reshape(-1, LANES)
    smem, vmem, hbm = (pl.BlockSpec(memory_space=m) for m in (pltpu.SMEM, pltpu.VMEM, pltpu.HBM))
    shapes = [jax.ShapeDtypeStruct((8, rows), i32)]
    shapes += [part_shape(features)] * (holders - NEAR)
    shapes += [jax.ShapeDtypeStruct((rows, features), bf16), jax.ShapeDtypeStruct((features, width), bf16)]
    return pl.pallas_call(
        functools.partial(far_body, slots, capacity, holders),
        out_shape=shapes,
        in_specs=[smem, smem, hbm, hbm, hbm, hbm],
        out_specs=[vmem] * len(shapes),
        scratch_shapes=[
            pltpu.VMEM(ids.shape, i32),
            pltpu.VMEM(table.shape, i32),
            pltpu.SemaphoreType.DMA((2,)),
            pltpu.SemaphoreType.DMA(()),
            pltpu.SemaphoreType.DMA(()),
        ],
        compiler_params=params(),
        cost_estimate=cost(2 * holders * capacity * rows * features, 4 * rows * features),
        name="far_rows",
    )(me.reshape(1), z.reshape(1), in_hbm(ids), in_hbm(table), in_hbm(x), in_hbm(weight))


def near_body(places_ref, x_ref, *outs):
    pick_rows(0, places_ref[0:1, :], places_ref[1:2, :].astype(f32), x_ref, outs)


def near_rows(spots, x, capacity):
    rows, features = x.shape
    return pl.pallas_call(
        near_body,
        out_shape=[part_shape(features)] * NEAR,
        compiler_params=params(),
        cost_estimate=cost(2 * NEAR * capacity * rows * features, 4 * rows * features),
        name="near_rows",
    )(spots, x)


def first_body(x_ref, w_ref, out):
    out[...] = dot(x_ref[...], w_ref[...]).astype(bf16)


def first_block(x, w):
    (rows, features), width = x.shape, w.shape[1]
    return pl.pallas_call(
        first_body,
        out_shape=jax.ShapeDtypeStruct((rows, width), bf16),
        compiler_params=params(),
        cost_estimate=cost(2 * rows * features * width, 2 * features * (rows + width)),
        name="first_block",
    )(x, w)


def second_body(z_ref, spots_ref, x_ref, w_hbm, *refs):
    near, (second, unsort, w_buf, sem) = refs[:NEAR], refs[NEAR:]
    copies = weight_copies((jnp.where(z_ref[0] < 2, 2, 1),), w_hbm, w_buf, sem)
    near_body(spots_ref, x_ref, *near)
    unsort_matrix(spots_ref, unsort)
    copies[0].wait()
    second[...] = dot(x_ref[...], w_buf[0]).astype(bf16)


def late_body(z_ref, x_ref, w_hbm, third, own, w_buf, sem):
    z = z_ref[0]
    copies = weight_copies((z ^ 1, z), w_hbm, w_buf, sem)
    for k, out in enumerate((third, own)):
        copies[k].wait()
        out[...] = dot(x_ref[...], w_buf[k]).astype(bf16)


def weight_copies(blocks, w_hbm, w_buf, sem):
    width = w_buf.shape[2]
    copies = []
    for k, block in enumerate(blocks):
        column = pl.multiple_of(block * width, width)
        copies.append(pltpu.make_async_copy(w_hbm.at[:, pl.ds(column, width)], w_buf.at[k], sem.at[k]))
        copies[k].start()
    return copies


def unsort_matrix(place_ref, unsort):
    rows, total = unsort.shape
    place = jnp.broadcast_to(place_ref[0:1, :].astype(f32), (LANES, rows)).T
    lane = iota((rows, LANES), 1).astype(f32)
    for k in range(total // LANES):
        unsort[:, k * LANES:(k + 1) * LANES] = (place == lane + float(k * LANES)).astype(f32).astype(bf16)


def second_block(z, spots, x, weight, width, total):
    rows, features = x.shape
    smem, vmem, hbm = (pl.BlockSpec(memory_space=m) for m in (pltpu.SMEM, pltpu.VMEM, pltpu.HBM))
    shapes = [part_shape(features)] * NEAR
    shapes += [jax.ShapeDtypeStruct((rows, width), bf16), jax.ShapeDtypeStruct((rows, total), bf16)]
    return pl.pallas_call(
        second_body,
        out_shape=shapes,
        in_specs=[smem, vmem, vmem, hbm],
        out_specs=[vmem] * len(shapes),
        scratch_shapes=[pltpu.VMEM((1, features, width), bf16), pltpu.SemaphoreType.DMA((1,))],
        compiler_params=params(),
        cost_estimate=cost(6 * rows * features * width, 2 * features * (rows + 4 * width)),
        name="second_block",
    )(z.reshape(1), spots, x, in_hbm(weight))


def late_blocks(z, x, weight, width):
    rows, features = x.shape
    smem, vmem, hbm = (pl.BlockSpec(memory_space=m) for m in (pltpu.SMEM, pltpu.VMEM, pltpu.HBM))
    return pl.pallas_call(
        late_body,
        out_shape=[jax.ShapeDtypeStruct((rows, width), bf16)] * 2,
        in_specs=[smem, vmem, hbm],
        out_specs=[vmem] * 2,
        scratch_shapes=[pltpu.VMEM((2, features, width), bf16), pltpu.SemaphoreType.DMA((2,))],
        compiler_params=params(),
        cost_estimate=cost(0, 0),
        name="late_blocks",
    )(z.reshape(1), x, in_hbm(weight))


def unsort_only(place, total):
    return pl.pallas_call(
        unsort_matrix,
        out_shape=jax.ShapeDtypeStruct((place.shape[1], total), bf16),
        compiler_params=params(),
        name="unsort",
    )(place)


def slot_mask(tag, group):
    lane = iota(tag.shape, 1)
    return tag == jnp.where(lane < ADAPTER_RANK, 2 * group + 1, 2 * group + 2).astype(f32)


def shrink_body(kept, down_ref, *refs):
    parts, out = refs[1 if kept else 0:-1], refs[-1]
    features, width = down_ref.shape
    half = LANES // 2
    first = iota((half, LANES), 1) < ADAPTER_RANK
    if kept:
        out[:kept, :] = refs[0][...]
    for k, part in enumerate(parts):
        tag = tag_lanes(part[features:, :])
        full = dot(part_rows(part, features), down_ref[...])
        total = jnp.zeros((LANES, LANES), f32)
        for group in range(width // LANES):
            total += jnp.where(slot_mask(tag, group), full[:, group * LANES:(group + 1) * LANES], 0.0)
        total += pltpu.roll(total, ADAPTER_RANK, 1)
        spot = slice(kept + k * half, kept + (k + 1) * half)
        out[spot, :] = jnp.where(first, total[:half], total[half:]).astype(bf16)


def shrink_partial(down, parts, done=()):
    features, width = down.shape
    total = len(parts) * LANES
    kept = sum(d.shape[0] for d in done)
    return pl.pallas_call(
        functools.partial(shrink_body, kept),
        out_shape=jax.ShapeDtypeStruct((kept + total // 2, LANES), bf16),
        compiler_params=params(),
        cost_estimate=cost(2 * total * features * width, 2 * features * (total + width)),
        name="shrink_partial",
    )(down, *done, *parts)


def expand_body(count, one_ref, two_ref, up_ref, *refs):
    tags, outs = refs[:count], refs[count:]
    capacity = outs[0].shape[0]
    half = capacity // 2
    up = up_ref[...]
    first = iota((half, LANES), 1) < ADAPTER_RANK
    for k in range(count):
        part = pl.ds(k * half, half)
        shrink = (one_ref[part, :].astype(f32) + two_ref[part, :].astype(f32)).astype(bf16).astype(f32)
        turned = pltpu.roll(shrink, ADAPTER_RANK, 1)
        rows = jnp.concatenate([jnp.where(first, shrink, turned), jnp.where(first, turned, shrink)], axis=0)
        tag = tag_lanes(tags[k][...])
        spread = [
            jnp.where(slot_mask(tag, group), rows, 0.0).astype(bf16) for group in range(up.shape[0] // LANES)
        ]
        outs[k][...] = dot(jnp.concatenate(spread, axis=1), up).astype(bf16)


def expand(one, two, up, parts):
    capacity, count = LANES, len(parts)
    last = parts[0].shape[0] // TAG_ROWS - 1
    tag_block = pl.BlockSpec((TAG_ROWS, LANES), lambda i: (last, 0))
    whole = lambda a: pl.BlockSpec(a.shape, lambda i: (0, 0))
    columns = up.shape[1]
    return pl.pallas_call(
        functools.partial(expand_body, count),
        grid=(1,),
        out_shape=[jax.ShapeDtypeStruct((capacity, columns), bf16)] * count,
        in_specs=[whole(one), whole(two), whole(up)] + [tag_block] * count,
        out_specs=[pl.BlockSpec((capacity, columns), lambda i: (0, 0))] * count,
        compiler_params=params(),
        cost_estimate=cost(80 * count * capacity * up.size, 80 * (up.size + count * capacity * columns)),
        name="expand",
    )(one, two, up, *parts)


def deltas_body(unsort_ref, own_ref, *refs):
    deltas, out = refs[:-1], refs[-1]
    placed = dot(unsort_ref[...], jnp.concatenate([d[...] for d in deltas], axis=0))
    out[...] = own_ref[...].astype(f32) + placed


def with_deltas(unsort, deltas, own):
    rows, columns = own.shape
    return pl.pallas_call(
        deltas_body,
        out_shape=jax.ShapeDtypeStruct((rows, columns), f32),
        compiler_params=params(),
        cost_estimate=cost(2 * rows * unsort.shape[1] * columns, 12 * rows * columns),
        name="with_deltas",
    )(unsort, own, *deltas)


def finish_body(start_ref, *refs):
    terms, (out_hbm, out_buf, sem) = refs[:-3], refs[-3:]
    pieces = sem.shape[0]
    step = out_buf.shape[0] // pieces
    copies = []
    for k in range(pieces):
        part = pl.ds(k * step, step)
        total = start_ref[part, :]
        for term in terms:
            total += term[part, :].astype(f32)
        out_buf[part, :] = total.astype(bf16)
        copies.append(pltpu.make_async_copy(out_buf.at[part, :], out_hbm.at[part, :], sem.at[k]))
        copies[k].start()
    for copy in copies:
        copy.wait()


def finish(start, terms):
    vmem, hbm = (pl.BlockSpec(memory_space=m) for m in (pltpu.VMEM, pltpu.HBM))
    return pl.pallas_call(
        finish_body,
        out_shape=jax.ShapeDtypeStruct(start.shape, bf16),
        in_specs=[vmem] * (1 + len(terms)),
        out_specs=hbm,
        scratch_shapes=[pltpu.VMEM(start.shape, bf16), pltpu.SemaphoreType.DMA((4,))],
        compiler_params=params(),
        cost_estimate=cost(start.size, 8 * start.size),
        name="finish",
    )(start, *terms)


def both(a, b):
    return (a.astype(f32) + b.astype(f32)).astype(bf16)


def after(value, *others):
    return lax.optimization_barrier((value,) + others)[0]


def swap(value, axis, bit):
    return lax.ppermute(value, axis, [(i, i ^ bit) for i in range(lax.axis_size(axis))])


EDGE = [(0, 1), (3, 2)]
MIDDLE = [(1, 2), (2, 1)]


def tp_sums(mine, *before):
    sums, bit = [mine], 1
    while True:
        other = swap(sums[-1], "tp", bit)
        bit *= 2
        if bit >= lax.axis_size("tp"):
            return sums, other
        sums.append(both(after(sums[-1], *before), other))


def shards(x, ids, table, weight, down, up):
    holders = lax.axis_size("ad")
    capacity = x.shape[0] // 4
    assert capacity == LANES
    slots = up.shape[0] // ADAPTER_RANK
    width = up.shape[1]
    total = holders * capacity
    me, z = lax.axis_index("ad"), lax.axis_index("tp")
    spots, *far, x, w = far_rows(me, z, ids, table, x, weight, holders, slots, capacity, width)
    far = [swap(rows, "ad", j + NEAR) for j, rows in enumerate(far)]
    if lax.axis_size("tp") == 4 and holders == 4:
        first = first_block(x, w)
        edge0 = lax.ppermute(first, "tp", EDGE)
        *near, second, unsort = second_block(z, after(spots, first), x, weight, width, total)
        near = [near[0], swap(near[1], "ad", 1)]
        edge1 = lax.ppermute(second, "tp", EDGE)
        early = shrink_partial(down, [near[0], far[0]])
        inner0 = both(after(first, early), edge0)
        middle0 = lax.ppermute(inner0, "tp", MIDDLE)
        early = shrink_partial(down, [after(near[1], inner0)], [early])
        mine = shrink_partial(down, [after(far[1], early)], [early])
        parts, order = [near[0], far[0], near[1], far[1]], (0, 2, 1, 3)
        third, own = late_blocks(z, after(x, mine), weight, width)
        inner1 = both(after(second, mine, third), edge1)
        steps, other = tp_sums(mine, inner1)
        inner2 = both(after(third, steps[-1]), middle0)
        last = swap(inner2, "tp", 1)
        middle1 = lax.ppermute(after(inner1, inner2), "tp", MIDDLE)
        sums = [middle1, last]
    else:
        near = near_rows(spots, x, capacity)
        near = [near[0], swap(near[1], "ad", 1)]
        parts, order = near + far, range(holders)
        unsort = unsort_only(spots, total)
        full = dot(x, weight).astype(bf16)
        own, sums = lax.psum_scatter(full, "tp", scatter_dimension=1, tiled=True), []
        steps, other = tp_sums(shrink_partial(down, parts))
    deltas = expand(steps[-1], other, up, parts)
    back = [None] * holders
    for j, delta in zip(order, deltas):
        back[j] = swap(delta, "ad", j) if j else delta
    return finish(with_deltas(unsort, back, own), sums)


def solution(mesh):
    in_specs = (
        P(("rep", "ad"), "tp"),
        P(("rep", "ad")),
        P("rep"),
        P("tp", None),
        P(("rep", "tp"), "ad"),
        P(("rep", "ad"), "tp"),
    )
    out_specs = P(("rep", "ad"), "tp")
    return jax.shard_map(shards, mesh=mesh, in_specs=in_specs, out_specs=out_specs, check_vma=False)
```

```python
import functools

import jax
import jax.numpy as jnp
from jax import lax
from jax.experimental import pallas as pl
from jax.experimental.pallas import tpu as pltpu
from jax.sharding import PartitionSpec as P

ADAPTER_RANK = 64
LANES = 128
NEAR = 2
TAG_ROWS = 16
VMEM_BYTES = 32 * 1024 * 1024

bf16 = jnp.bfloat16
f32 = jnp.float32
i32 = jnp.int32


def params():
    return pltpu.CompilerParams(vmem_limit_bytes=VMEM_BYTES)


def cost(flops, nbytes):
    return pl.CostEstimate(flops=flops, bytes_accessed=nbytes, transcendentals=0)


def dot(a, b, contract=((1,), (0,))):
    return lax.dot_general(a, b, (contract, ((), ())), preferred_element_type=f32)


def in_hbm(a):
    return pltpu.with_memory_space_constraint(a, pltpu.HBM)


def iota(shape, dim):
    return lax.broadcasted_iota(i32, shape, dim)


def places(slots, capacity, holders, me, ids, table):
    rows = ids.shape[1]
    low = (iota((LANES, rows), 0) == (ids & (LANES - 1))).astype(f32).astype(bf16)
    high = iota((table.shape[0], rows), 0) == lax.shift_right_logical(ids, 7)
    found = dot(table.astype(f32).astype(bf16), low)
    slot = jnp.sum(jnp.where(high, found, 0.0), axis=0, keepdims=True).astype(i32)
    holder = split_slot(slot, slots)
    tag = (slot - holder * slots + 1).astype(f32)
    partner = holder ^ me
    mine = iota((max(8, holders), rows), 0) == partner
    ones = mine.astype(f32)
    groups = [ones[:, k:k + LANES] for k in range(0, rows, LANES)]
    earlier = (iota((LANES, LANES), 0) < iota((LANES, LANES), 1)).astype(f32).astype(bf16)
    before = dot(jnp.concatenate(groups, axis=0).astype(bf16), earlier)
    count = ones.shape[0]
    ranks, passed = [], jnp.zeros((count, 1), f32)
    for k, group in enumerate(groups):
        ranks.append(jnp.sum(group * (before[k * count:(k + 1) * count] + passed), axis=0, keepdims=True))
        passed += jnp.sum(group, axis=1, keepdims=True)
    return partner * capacity + jnp.concatenate(ranks, axis=1).astype(i32), tag


def split_slot(slot, slots):
    if slots & (slots - 1):
        return lax.div(slot, slots)
    return lax.shift_right_logical(slot, slots.bit_length() - 1)


def pick_rows(start, place, tag, x, outs):
    rows, features = x.shape
    pick = iota((len(outs) * LANES, rows), 0) + start * LANES == place
    pick = pick.astype(f32).astype(bf16)
    tags = dot(jnp.broadcast_to(tag, (TAG_ROWS, rows)).astype(bf16), pick, ((1,), (1,))).astype(bf16)
    step = min(512, features)
    for c in range(0, features, step):
        moved = dot(pick, x[:, c:c + step]).astype(bf16)
        for j, out in enumerate(outs):
            for i in range(0, step, LANES):
                out[c + i:c + i + LANES, :] = moved[j * LANES:(j + 1) * LANES, i:i + LANES]
    for j, out in enumerate(outs):
        out[features:, :] = tags[:, j * LANES:(j + 1) * LANES]


def part_rows(part, features):
    return jnp.concatenate([part[c:c + LANES, :] for c in range(0, features, LANES)], axis=1)


def tag_lanes(tags):
    return jnp.broadcast_to(tags[0:1, :].astype(f32), (LANES, LANES)).T


def part_shape(features):
    return jax.ShapeDtypeStruct((features + TAG_ROWS, LANES), bf16)


def far_body(slots, capacity, holders, me_ref, z_ref, ids_hbm, table_hbm, x_hbm, w_hbm, places_ref, *refs):
    outs, (x_buf, w_buf, ids_buf, table_buf, small_sem, x_sem, w_sem) = refs[:holders - NEAR], refs[holders - NEAR:]
    width = w_buf.shape[1]
    small = [
        pltpu.make_async_copy(ids_hbm, ids_buf, small_sem.at[0]),
        pltpu.make_async_copy(table_hbm, table_buf, small_sem.at[1]),
    ]
    x_copy = pltpu.make_async_copy(x_hbm, x_buf, x_sem)
    column = pl.multiple_of(jnp.where(z_ref[0] < 2, 3, 0) * width, width)
    w_copy = pltpu.make_async_copy(w_hbm.at[:, pl.ds(column, width)], w_buf, w_sem)
    for copy in small + [x_copy, w_copy]:
        copy.start()
    for copy in small:
        copy.wait()
    place, tag = places(slots, capacity, holders, me_ref[0], ids_buf[...], table_buf[...])
    row = iota(places_ref.shape, 0)
    places_ref[...] = jnp.where(row == 0, place, jnp.where(row == 1, tag.astype(i32), 0))
    x_copy.wait()
    pick_rows(NEAR, place, tag, x_buf, outs)
    w_copy.wait()


def far_rows(me, z, ids, table, x, weight, holders, slots, capacity, width):
    rows, features = x.shape
    ids, table = ids.reshape(1, rows), table.reshape(-1, LANES)
    smem, vmem, hbm = (pl.BlockSpec(memory_space=m) for m in (pltpu.SMEM, pltpu.VMEM, pltpu.HBM))
    shapes = [jax.ShapeDtypeStruct((8, rows), i32)]
    shapes += [part_shape(features)] * (holders - NEAR)
    shapes += [jax.ShapeDtypeStruct((rows, features), bf16), jax.ShapeDtypeStruct((features, width), bf16)]
    return pl.pallas_call(
        functools.partial(far_body, slots, capacity, holders),
        out_shape=shapes,
        in_specs=[smem, smem, hbm, hbm, hbm, hbm],
        out_specs=[vmem] * len(shapes),
        scratch_shapes=[
            pltpu.VMEM(ids.shape, i32),
            pltpu.VMEM(table.shape, i32),
            pltpu.SemaphoreType.DMA((2,)),
            pltpu.SemaphoreType.DMA(()),
            pltpu.SemaphoreType.DMA(()),
        ],
        compiler_params=params(),
        cost_estimate=cost(2 * holders * capacity * rows * features, 4 * rows * features),
        name="far_rows",
    )(me.reshape(1), z.reshape(1), in_hbm(ids), in_hbm(table), in_hbm(x), in_hbm(weight))


def near_body(places_ref, x_ref, *outs):
    pick_rows(0, places_ref[0:1, :], places_ref[1:2, :].astype(f32), x_ref, outs)


def near_rows(spots, x, capacity):
    rows, features = x.shape
    return pl.pallas_call(
        near_body,
        out_shape=[part_shape(features)] * NEAR,
        compiler_params=params(),
        cost_estimate=cost(2 * NEAR * capacity * rows * features, 4 * rows * features),
        name="near_rows",
    )(spots, x)


def first_body(x_ref, w_ref, out):
    out[...] = dot(x_ref[...], w_ref[...]).astype(bf16)


def first_block(x, w):
    (rows, features), width = x.shape, w.shape[1]
    return pl.pallas_call(
        first_body,
        out_shape=jax.ShapeDtypeStruct((rows, width), bf16),
        compiler_params=params(),
        cost_estimate=cost(2 * rows * features * width, 2 * features * (rows + width)),
        name="first_block",
    )(x, w)


def rest_body(z_ref, spots_ref, x_ref, w_hbm, *refs):
    near, (second, third, own, unsort, w_buf, sem) = refs[:NEAR], refs[NEAR:]
    z = z_ref[0]
    width = own.shape[1]
    copies = []
    for k, block in enumerate((jnp.where(z < 2, 2, 1), z ^ 1, z)):
        column = pl.multiple_of(block * width, width)
        copies.append(pltpu.make_async_copy(w_hbm.at[:, pl.ds(column, width)], w_buf.at[k], sem.at[k]))
        copies[k].start()
    near_body(spots_ref, x_ref, *near)
    unsort_matrix(spots_ref, unsort)
    for k, out in enumerate((second, third, own)):
        copies[k].wait()
        out[...] = dot(x_ref[...], w_buf[k]).astype(bf16)


def unsort_matrix(place_ref, unsort):
    rows, total = unsort.shape
    place = jnp.broadcast_to(place_ref[0:1, :].astype(f32), (LANES, rows)).T
    lane = iota((rows, LANES), 1).astype(f32)
    for k in range(total // LANES):
        unsort[:, k * LANES:(k + 1) * LANES] = (place == lane + float(k * LANES)).astype(f32).astype(bf16)


def rest(z, spots, x, weight, width, total, capacity):
    rows, features = x.shape
    smem, vmem, hbm = (pl.BlockSpec(memory_space=m) for m in (pltpu.SMEM, pltpu.VMEM, pltpu.HBM))
    shapes = [part_shape(features)] * NEAR
    shapes += [jax.ShapeDtypeStruct((rows, width), bf16)] * 3 + [jax.ShapeDtypeStruct((rows, total), bf16)]
    return pl.pallas_call(
        rest_body,
        out_shape=shapes,
        in_specs=[smem, vmem, vmem, hbm],
        out_specs=[vmem] * len(shapes),
        scratch_shapes=[pltpu.VMEM((3, features, width), bf16), pltpu.SemaphoreType.DMA((3,))],
        compiler_params=params(),
        cost_estimate=cost(6 * rows * features * width, 2 * features * (rows + 4 * width)),
        name="rest",
    )(z.reshape(1), spots, x, in_hbm(weight))


def unsort_only(place, total):
    return pl.pallas_call(
        unsort_matrix,
        out_shape=jax.ShapeDtypeStruct((place.shape[1], total), bf16),
        compiler_params=params(),
        name="unsort",
    )(place)


def slot_mask(tag, group):
    lane = iota(tag.shape, 1)
    return tag == jnp.where(lane < ADAPTER_RANK, 2 * group + 1, 2 * group + 2).astype(f32)


def shrink_body(kept, down_ref, *refs):
    parts, out = refs[1 if kept else 0:-1], refs[-1]
    features, width = down_ref.shape
    half = LANES // 2
    first = iota((half, LANES), 1) < ADAPTER_RANK
    if kept:
        out[:kept, :] = refs[0][...]
    for k, part in enumerate(parts):
        tag = tag_lanes(part[features:, :])
        full = dot(part_rows(part, features), down_ref[...])
        total = jnp.zeros((LANES, LANES), f32)
        for group in range(width // LANES):
            total += jnp.where(slot_mask(tag, group), full[:, group * LANES:(group + 1) * LANES], 0.0)
        total += pltpu.roll(total, ADAPTER_RANK, 1)
        spot = slice(kept + k * half, kept + (k + 1) * half)
        out[spot, :] = jnp.where(first, total[:half], total[half:]).astype(bf16)


def shrink_partial(down, parts, done=()):
    features, width = down.shape
    total = len(parts) * LANES
    kept = sum(d.shape[0] for d in done)
    return pl.pallas_call(
        functools.partial(shrink_body, kept),
        out_shape=jax.ShapeDtypeStruct((kept + total // 2, LANES), bf16),
        compiler_params=params(),
        cost_estimate=cost(2 * total * features * width, 2 * features * (total + width)),
        name="shrink_partial",
    )(down, *done, *parts)


def expand_body(count, one_ref, two_ref, up_ref, *refs):
    tags, outs = refs[:count], refs[count:]
    capacity = outs[0].shape[0]
    half = capacity // 2
    up = up_ref[...]
    first = iota((half, LANES), 1) < ADAPTER_RANK
    for k in range(count):
        part = pl.ds(k * half, half)
        shrink = (one_ref[part, :].astype(f32) + two_ref[part, :].astype(f32)).astype(bf16).astype(f32)
        turned = pltpu.roll(shrink, ADAPTER_RANK, 1)
        rows = jnp.concatenate([jnp.where(first, shrink, turned), jnp.where(first, turned, shrink)], axis=0)
        tag = tag_lanes(tags[k][...])
        spread = [
            jnp.where(slot_mask(tag, group), rows, 0.0).astype(bf16) for group in range(up.shape[0] // LANES)
        ]
        outs[k][...] = dot(jnp.concatenate(spread, axis=1), up).astype(bf16)


def expand(one, two, up, parts):
    capacity, count = LANES, len(parts)
    last = parts[0].shape[0] // TAG_ROWS - 1
    tag_block = pl.BlockSpec((TAG_ROWS, LANES), lambda i: (last, 0))
    whole = lambda a: pl.BlockSpec(a.shape, lambda i: (0, 0))
    columns = up.shape[1]
    return pl.pallas_call(
        functools.partial(expand_body, count),
        grid=(1,),
        out_shape=[jax.ShapeDtypeStruct((capacity, columns), bf16)] * count,
        in_specs=[whole(one), whole(two), whole(up)] + [tag_block] * count,
        out_specs=[pl.BlockSpec((capacity, columns), lambda i: (0, 0))] * count,
        compiler_params=params(),
        cost_estimate=cost(80 * count * capacity * up.size, 80 * (up.size + count * capacity * columns)),
        name="expand",
    )(one, two, up, *parts)


def deltas_body(unsort_ref, own_ref, *refs):
    deltas, out = refs[:-1], refs[-1]
    placed = dot(unsort_ref[...], jnp.concatenate([d[...] for d in deltas], axis=0))
    out[...] = own_ref[...].astype(f32) + placed


def with_deltas(unsort, deltas, own):
    rows, columns = own.shape
    return pl.pallas_call(
        deltas_body,
        out_shape=jax.ShapeDtypeStruct((rows, columns), f32),
        compiler_params=params(),
        cost_estimate=cost(2 * rows * unsort.shape[1] * columns, 12 * rows * columns),
        name="with_deltas",
    )(unsort, own, *deltas)


def finish_body(start_ref, *refs):
    terms, (out_hbm, out_buf, sem) = refs[:-3], refs[-3:]
    pieces = sem.shape[0]
    step = out_buf.shape[0] // pieces
    copies = []
    for k in range(pieces):
        part = pl.ds(k * step, step)
        total = start_ref[part, :]
        for term in terms:
            total += term[part, :].astype(f32)
        out_buf[part, :] = total.astype(bf16)
        copies.append(pltpu.make_async_copy(out_buf.at[part, :], out_hbm.at[part, :], sem.at[k]))
        copies[k].start()
    for copy in copies:
        copy.wait()


def finish(start, terms):
    vmem, hbm = (pl.BlockSpec(memory_space=m) for m in (pltpu.VMEM, pltpu.HBM))
    return pl.pallas_call(
        finish_body,
        out_shape=jax.ShapeDtypeStruct(start.shape, bf16),
        in_specs=[vmem] * (1 + len(terms)),
        out_specs=hbm,
        scratch_shapes=[pltpu.VMEM(start.shape, bf16), pltpu.SemaphoreType.DMA((4,))],
        compiler_params=params(),
        cost_estimate=cost(start.size, 8 * start.size),
        name="finish",
    )(start, *terms)


def both(a, b):
    return (a.astype(f32) + b.astype(f32)).astype(bf16)


def after(value, *others):
    return lax.optimization_barrier((value,) + others)[0]


def swap(value, axis, bit):
    return lax.ppermute(value, axis, [(i, i ^ bit) for i in range(lax.axis_size(axis))])


EDGE = [(0, 1), (3, 2)]
MIDDLE = [(1, 2), (2, 1)]


def tp_sums(mine, *before):
    sums, bit = [mine], 1
    while True:
        other = swap(sums[-1], "tp", bit)
        bit *= 2
        if bit >= lax.axis_size("tp"):
            return sums, other
        sums.append(both(after(sums[-1], *before), other))


def shards(x, ids, table, weight, down, up):
    holders = lax.axis_size("ad")
    capacity = x.shape[0] // 4
    assert capacity == LANES
    slots = up.shape[0] // ADAPTER_RANK
    width = up.shape[1]
    total = holders * capacity
    me, z = lax.axis_index("ad"), lax.axis_index("tp")
    spots, *far, x, w = far_rows(me, z, ids, table, x, weight, holders, slots, capacity, width)
    far = [swap(rows, "ad", j + NEAR) for j, rows in enumerate(far)]
    if lax.axis_size("tp") == 4 and holders == 4:
        first = first_block(x, w)
        edge0 = lax.ppermute(first, "tp", EDGE)
        *near, second, third, own, unsort = rest(z, after(spots, first), x, weight, width, total, capacity)
        near = [near[0], swap(near[1], "ad", 1)]
        edge1 = lax.ppermute(second, "tp", EDGE)
        early = shrink_partial(down, [near[0], far[1]])
        inner0 = both(after(first, early), edge0)
        middle0 = lax.ppermute(inner0, "tp", MIDDLE)
        early = shrink_partial(down, [after(near[1], inner0)], [early])
        mine = shrink_partial(down, [after(far[0], early)], [early])
        parts, order = [near[0], far[1], near[1], far[0]], (0, 3, 1, 2)
        inner1 = both(after(second, mine), edge1)
        steps, other = tp_sums(mine, inner1)
        inner2 = both(after(third, steps[-1]), middle0)
        last = swap(inner2, "tp", 1)
        middle1 = lax.ppermute(after(inner1, inner2), "tp", MIDDLE)
        sums = [middle1, last]
    else:
        near = near_rows(spots, x, capacity)
        near = [near[0], swap(near[1], "ad", 1)]
        parts, order = near + far, range(holders)
        unsort = unsort_only(spots, total)
        full = dot(x, weight).astype(bf16)
        own, sums = lax.psum_scatter(full, "tp", scatter_dimension=1, tiled=True), []
        steps, other = tp_sums(shrink_partial(down, parts))
    deltas = expand(steps[-1], other, up, parts)
    back = [None] * holders
    for j, delta in zip(order, deltas):
        back[j] = swap(delta, "ad", j) if j else delta
    return finish(with_deltas(unsort, back, own), sums)


def solution(mesh):
    in_specs = (
        P(("rep", "ad"), "tp"),
        P(("rep", "ad")),
        P("rep"),
        P("tp", None),
        P(("rep", "tp"), "ad"),
        P(("rep", "ad"), "tp"),
    )
    out_specs = P(("rep", "ad"), "tp")
    return jax.shard_map(shards, mesh=mesh, in_specs=in_specs, out_specs=out_specs, check_vma=False)
```

```python
import functools

import jax
import jax.numpy as jnp
from jax import lax
from jax.experimental import pallas as pl
from jax.experimental.pallas import tpu as pltpu
from jax.sharding import PartitionSpec as P

ADAPTER_RANK = 64
LANES = 128
NEAR = 2
TAG_ROWS = 16
VMEM_BYTES = 32 * 1024 * 1024

bf16 = jnp.bfloat16
f32 = jnp.float32
i32 = jnp.int32


def params():
    return pltpu.CompilerParams(vmem_limit_bytes=VMEM_BYTES)


def cost(flops, nbytes):
    return pl.CostEstimate(flops=flops, bytes_accessed=nbytes, transcendentals=0)


def dot(a, b, contract=((1,), (0,))):
    return lax.dot_general(a, b, (contract, ((), ())), preferred_element_type=f32)


def in_hbm(a):
    return pltpu.with_memory_space_constraint(a, pltpu.HBM)


def iota(shape, dim):
    return lax.broadcasted_iota(i32, shape, dim)


def places(slots, capacity, holders, me, ids, table):
    rows = ids.shape[1]
    low = (iota((LANES, rows), 0) == (ids & (LANES - 1))).astype(f32).astype(bf16)
    high = iota((table.shape[0], rows), 0) == lax.shift_right_logical(ids, 7)
    found = dot(table.astype(f32).astype(bf16), low)
    slot = jnp.sum(jnp.where(high, found, 0.0), axis=0, keepdims=True).astype(i32)
    holder = split_slot(slot, slots)
    tag = (slot - holder * slots + 1).astype(f32)
    partner = holder ^ me
    mine = iota((max(8, holders), rows), 0) == partner
    ones = mine.astype(f32)
    groups = [ones[:, k:k + LANES] for k in range(0, rows, LANES)]
    earlier = (iota((LANES, LANES), 0) < iota((LANES, LANES), 1)).astype(f32).astype(bf16)
    before = dot(jnp.concatenate(groups, axis=0).astype(bf16), earlier)
    count = ones.shape[0]
    ranks, passed = [], jnp.zeros((count, 1), f32)
    for k, group in enumerate(groups):
        ranks.append(jnp.sum(group * (before[k * count:(k + 1) * count] + passed), axis=0, keepdims=True))
        passed += jnp.sum(group, axis=1, keepdims=True)
    return partner * capacity + jnp.concatenate(ranks, axis=1).astype(i32), tag


def split_slot(slot, slots):
    if slots & (slots - 1):
        return lax.div(slot, slots)
    return lax.shift_right_logical(slot, slots.bit_length() - 1)


def pick_rows(start, place, tag, x, outs):
    rows, features = x.shape
    pick = iota((len(outs) * LANES, rows), 0) + start * LANES == place
    pick = pick.astype(f32).astype(bf16)
    tags = dot(jnp.broadcast_to(tag, (TAG_ROWS, rows)).astype(bf16), pick, ((1,), (1,))).astype(bf16)
    step = min(512, features)
    for c in range(0, features, step):
        moved = dot(pick, x[:, c:c + step]).astype(bf16)
        for j, out in enumerate(outs):
            for i in range(0, step, LANES):
                out[c + i:c + i + LANES, :] = moved[j * LANES:(j + 1) * LANES, i:i + LANES]
    for j, out in enumerate(outs):
        out[features:, :] = tags[:, j * LANES:(j + 1) * LANES]


def part_rows(part, features):
    return jnp.concatenate([part[c:c + LANES, :] for c in range(0, features, LANES)], axis=1)


def tag_lanes(tags):
    return jnp.broadcast_to(tags[0:1, :].astype(f32), (LANES, LANES)).T


def part_shape(features):
    return jax.ShapeDtypeStruct((features + TAG_ROWS, LANES), bf16)


def far_body(slots, capacity, holders, me_ref, z_ref, ids_hbm, table_hbm, x_hbm, w_hbm, places_ref, *refs):
    outs, (x_buf, w_buf, ids_buf, table_buf, small_sem, x_sem, w_sem) = refs[:holders - NEAR], refs[holders - NEAR:]
    width = w_buf.shape[1]
    small = [
        pltpu.make_async_copy(ids_hbm, ids_buf, small_sem.at[0]),
        pltpu.make_async_copy(table_hbm, table_buf, small_sem.at[1]),
    ]
    x_copy = pltpu.make_async_copy(x_hbm, x_buf, x_sem)
    column = pl.multiple_of(jnp.where(z_ref[0] < 2, 3, 0) * width, width)
    w_copy = pltpu.make_async_copy(w_hbm.at[:, pl.ds(column, width)], w_buf, w_sem)
    for copy in small + [x_copy, w_copy]:
        copy.start()
    for copy in small:
        copy.wait()
    place, tag = places(slots, capacity, holders, me_ref[0], ids_buf[...], table_buf[...])
    row = iota(places_ref.shape, 0)
    places_ref[...] = jnp.where(row == 0, place, jnp.where(row == 1, tag.astype(i32), 0))
    x_copy.wait()
    pick_rows(NEAR, place, tag, x_buf, outs)
    w_copy.wait()


def far_rows(me, z, ids, table, x, weight, holders, slots, capacity, width):
    rows, features = x.shape
    ids, table = ids.reshape(1, rows), table.reshape(-1, LANES)
    smem, vmem, hbm = (pl.BlockSpec(memory_space=m) for m in (pltpu.SMEM, pltpu.VMEM, pltpu.HBM))
    shapes = [jax.ShapeDtypeStruct((8, rows), i32)]
    shapes += [part_shape(features)] * (holders - NEAR)
    shapes += [jax.ShapeDtypeStruct((rows, features), bf16), jax.ShapeDtypeStruct((features, width), bf16)]
    return pl.pallas_call(
        functools.partial(far_body, slots, capacity, holders),
        out_shape=shapes,
        in_specs=[smem, smem, hbm, hbm, hbm, hbm],
        out_specs=[vmem] * len(shapes),
        scratch_shapes=[
            pltpu.VMEM(ids.shape, i32),
            pltpu.VMEM(table.shape, i32),
            pltpu.SemaphoreType.DMA((2,)),
            pltpu.SemaphoreType.DMA(()),
            pltpu.SemaphoreType.DMA(()),
        ],
        compiler_params=params(),
        cost_estimate=cost(2 * holders * capacity * rows * features, 4 * rows * features),
        name="far_rows",
    )(me.reshape(1), z.reshape(1), in_hbm(ids), in_hbm(table), in_hbm(x), in_hbm(weight))


def near_body(places_ref, x_ref, *outs):
    pick_rows(0, places_ref[0:1, :], places_ref[1:2, :].astype(f32), x_ref, outs)


def near_rows(spots, x, capacity):
    rows, features = x.shape
    return pl.pallas_call(
        near_body,
        out_shape=[part_shape(features)] * NEAR,
        compiler_params=params(),
        cost_estimate=cost(2 * NEAR * capacity * rows * features, 4 * rows * features),
        name="near_rows",
    )(spots, x)


def first_body(x_ref, w_ref, out):
    out[...] = dot(x_ref[...], w_ref[...]).astype(bf16)


def first_block(x, w):
    (rows, features), width = x.shape, w.shape[1]
    return pl.pallas_call(
        first_body,
        out_shape=jax.ShapeDtypeStruct((rows, width), bf16),
        compiler_params=params(),
        cost_estimate=cost(2 * rows * features * width, 2 * features * (rows + width)),
        name="first_block",
    )(x, w)


def second_body(z_ref, spots_ref, x_ref, w_hbm, *refs):
    near, (second, unsort, w_buf, sem) = refs[:NEAR], refs[NEAR:]
    copies = weight_copies((jnp.where(z_ref[0] < 2, 2, 1),), w_hbm, w_buf, sem)
    near_body(spots_ref, x_ref, *near)
    unsort_matrix(spots_ref, unsort)
    copies[0].wait()
    second[...] = dot(x_ref[...], w_buf[0]).astype(bf16)


def late_body(z_ref, x_ref, w_hbm, third, own, w_buf, sem):
    z = z_ref[0]
    copies = weight_copies((z ^ 1, z), w_hbm, w_buf, sem)
    for k, out in enumerate((third, own)):
        copies[k].wait()
        out[...] = dot(x_ref[...], w_buf[k]).astype(bf16)


def weight_copies(blocks, w_hbm, w_buf, sem):
    width = w_buf.shape[2]
    copies = []
    for k, block in enumerate(blocks):
        column = pl.multiple_of(block * width, width)
        copies.append(pltpu.make_async_copy(w_hbm.at[:, pl.ds(column, width)], w_buf.at[k], sem.at[k]))
        copies[k].start()
    return copies


def unsort_matrix(place_ref, unsort):
    rows, total = unsort.shape
    place = jnp.broadcast_to(place_ref[0:1, :].astype(f32), (LANES, rows)).T
    lane = iota((rows, LANES), 1).astype(f32)
    for k in range(total // LANES):
        unsort[:, k * LANES:(k + 1) * LANES] = (place == lane + float(k * LANES)).astype(f32).astype(bf16)


def second_block(z, spots, x, weight, width, total):
    rows, features = x.shape
    smem, vmem, hbm = (pl.BlockSpec(memory_space=m) for m in (pltpu.SMEM, pltpu.VMEM, pltpu.HBM))
    shapes = [part_shape(features)] * NEAR
    shapes += [jax.ShapeDtypeStruct((rows, width), bf16), jax.ShapeDtypeStruct((rows, total), bf16)]
    return pl.pallas_call(
        second_body,
        out_shape=shapes,
        in_specs=[smem, vmem, vmem, hbm],
        out_specs=[vmem] * len(shapes),
        scratch_shapes=[pltpu.VMEM((1, features, width), bf16), pltpu.SemaphoreType.DMA((1,))],
        compiler_params=params(),
        cost_estimate=cost(6 * rows * features * width, 2 * features * (rows + 4 * width)),
        name="second_block",
    )(z.reshape(1), spots, x, in_hbm(weight))


def late_blocks(z, x, weight, width):
    rows, features = x.shape
    smem, vmem, hbm = (pl.BlockSpec(memory_space=m) for m in (pltpu.SMEM, pltpu.VMEM, pltpu.HBM))
    return pl.pallas_call(
        late_body,
        out_shape=[jax.ShapeDtypeStruct((rows, width), bf16)] * 2,
        in_specs=[smem, vmem, hbm],
        out_specs=[vmem] * 2,
        scratch_shapes=[pltpu.VMEM((2, features, width), bf16), pltpu.SemaphoreType.DMA((2,))],
        compiler_params=params(),
        cost_estimate=cost(4 * rows * features * width, 2 * features * (rows + 2 * width)),
        name="late_blocks",
    )(z.reshape(1), x, in_hbm(weight))


def unsort_only(place, total):
    return pl.pallas_call(
        unsort_matrix,
        out_shape=jax.ShapeDtypeStruct((place.shape[1], total), bf16),
        compiler_params=params(),
        name="unsort",
    )(place)


def slot_mask(tag, group):
    lane = iota(tag.shape, 1)
    return tag == jnp.where(lane < ADAPTER_RANK, 2 * group + 1, 2 * group + 2).astype(f32)


def shrink_body(kept, down_ref, *refs):
    parts, out = refs[1 if kept else 0:-1], refs[-1]
    features, width = down_ref.shape
    half = LANES // 2
    first = iota((half, LANES), 1) < ADAPTER_RANK
    if kept:
        out[:kept, :] = refs[0][...]
    for k, part in enumerate(parts):
        tag = tag_lanes(part[features:, :])
        full = dot(part_rows(part, features), down_ref[...])
        total = jnp.zeros((LANES, LANES), f32)
        for group in range(width // LANES):
            total += jnp.where(slot_mask(tag, group), full[:, group * LANES:(group + 1) * LANES], 0.0)
        total += pltpu.roll(total, ADAPTER_RANK, 1)
        spot = slice(kept + k * half, kept + (k + 1) * half)
        out[spot, :] = jnp.where(first, total[:half], total[half:]).astype(bf16)


def shrink_partial(down, parts, done=()):
    features, width = down.shape
    total = len(parts) * LANES
    kept = sum(d.shape[0] for d in done)
    return pl.pallas_call(
        functools.partial(shrink_body, kept),
        out_shape=jax.ShapeDtypeStruct((kept + total // 2, LANES), bf16),
        compiler_params=params(),
        cost_estimate=cost(2 * total * features * width, 2 * features * (total + width)),
        name="shrink_partial",
    )(down, *done, *parts)


def expand_body(count, one_ref, two_ref, up_ref, *refs):
    tags, outs = refs[:count], refs[count:]
    capacity = outs[0].shape[0]
    half = capacity // 2
    up = up_ref[...]
    first = iota((half, LANES), 1) < ADAPTER_RANK
    for k in range(count):
        part = pl.ds(k * half, half)
        shrink = (one_ref[part, :].astype(f32) + two_ref[part, :].astype(f32)).astype(bf16).astype(f32)
        turned = pltpu.roll(shrink, ADAPTER_RANK, 1)
        rows = jnp.concatenate([jnp.where(first, shrink, turned), jnp.where(first, turned, shrink)], axis=0)
        tag = tag_lanes(tags[k][...])
        spread = [
            jnp.where(slot_mask(tag, group), rows, 0.0).astype(bf16) for group in range(up.shape[0] // LANES)
        ]
        outs[k][...] = dot(jnp.concatenate(spread, axis=1), up).astype(bf16)


def expand(one, two, up, parts):
    capacity, count = LANES, len(parts)
    last = parts[0].shape[0] // TAG_ROWS - 1
    tag_block = pl.BlockSpec((TAG_ROWS, LANES), lambda i: (last, 0))
    whole = lambda a: pl.BlockSpec(a.shape, lambda i: (0, 0))
    columns = up.shape[1]
    return pl.pallas_call(
        functools.partial(expand_body, count),
        grid=(1,),
        out_shape=[jax.ShapeDtypeStruct((capacity, columns), bf16)] * count,
        in_specs=[whole(one), whole(two), whole(up)] + [tag_block] * count,
        out_specs=[pl.BlockSpec((capacity, columns), lambda i: (0, 0))] * count,
        compiler_params=params(),
        cost_estimate=cost(80 * count * capacity * up.size, 80 * (up.size + count * capacity * columns)),
        name="expand",
    )(one, two, up, *parts)


def deltas_body(unsort_ref, own_ref, *refs):
    deltas, out = refs[:-1], refs[-1]
    placed = dot(unsort_ref[...], jnp.concatenate([d[...] for d in deltas], axis=0))
    out[...] = own_ref[...].astype(f32) + placed


def with_deltas(unsort, deltas, own):
    rows, columns = own.shape
    return pl.pallas_call(
        deltas_body,
        out_shape=jax.ShapeDtypeStruct((rows, columns), f32),
        compiler_params=params(),
        cost_estimate=cost(2 * rows * unsort.shape[1] * columns, 12 * rows * columns),
        name="with_deltas",
    )(unsort, own, *deltas)


def finish_body(start_ref, *refs):
    terms, (out_hbm, out_buf, sem) = refs[:-3], refs[-3:]
    pieces = sem.shape[0]
    step = out_buf.shape[0] // pieces
    copies = []
    for k in range(pieces):
        part = pl.ds(k * step, step)
        total = start_ref[part, :]
        for term in terms:
            total += term[part, :].astype(f32)
        out_buf[part, :] = total.astype(bf16)
        copies.append(pltpu.make_async_copy(out_buf.at[part, :], out_hbm.at[part, :], sem.at[k]))
        copies[k].start()
    for copy in copies:
        copy.wait()


def finish(start, terms):
    vmem, hbm = (pl.BlockSpec(memory_space=m) for m in (pltpu.VMEM, pltpu.HBM))
    return pl.pallas_call(
        finish_body,
        out_shape=jax.ShapeDtypeStruct(start.shape, bf16),
        in_specs=[vmem] * (1 + len(terms)),
        out_specs=hbm,
        scratch_shapes=[pltpu.VMEM(start.shape, bf16), pltpu.SemaphoreType.DMA((4,))],
        compiler_params=params(),
        cost_estimate=cost(start.size, 8 * start.size),
        name="finish",
    )(start, *terms)


def both(a, b):
    return (a.astype(f32) + b.astype(f32)).astype(bf16)


def after(value, *others):
    return lax.optimization_barrier((value,) + others)[0]


def swap(value, axis, bit):
    return lax.ppermute(value, axis, [(i, i ^ bit) for i in range(lax.axis_size(axis))])


EDGE = [(0, 1), (3, 2)]
MIDDLE = [(1, 2), (2, 1)]


def tp_sums(mine, *before):
    sums, bit = [mine], 1
    while True:
        other = swap(sums[-1], "tp", bit)
        bit *= 2
        if bit >= lax.axis_size("tp"):
            return sums, other
        sums.append(both(after(sums[-1], *before), other))


def shards(x, ids, table, weight, down, up):
    holders = lax.axis_size("ad")
    capacity = x.shape[0] // 4
    assert capacity == LANES
    slots = up.shape[0] // ADAPTER_RANK
    width = up.shape[1]
    total = holders * capacity
    me, z = lax.axis_index("ad"), lax.axis_index("tp")
    spots, *far, x, w = far_rows(me, z, ids, table, x, weight, holders, slots, capacity, width)
    far = [swap(rows, "ad", j + NEAR) for j, rows in enumerate(far)]
    if lax.axis_size("tp") == 4 and holders == 4:
        first = first_block(x, w)
        edge0 = lax.ppermute(first, "tp", EDGE)
        *near, second, unsort = second_block(z, after(spots, first), x, weight, width, total)
        near = [near[0], swap(near[1], "ad", 1)]
        edge1 = lax.ppermute(second, "tp", EDGE)
        early = shrink_partial(down, [near[0], far[0]])
        inner0 = both(after(first, early), edge0)
        middle0 = lax.ppermute(inner0, "tp", MIDDLE)
        early = shrink_partial(down, [after(near[1], inner0)], [early])
        mine = shrink_partial(down, [after(far[1], early)], [early])
        parts, order = [near[0], far[0], near[1], far[1]], (0, 2, 1, 3)
        third, own = late_blocks(z, after(x, early), weight, width)
        inner1 = both(after(second, mine, third), edge1)
        steps, other = tp_sums(mine, inner1)
        inner2 = both(after(third, steps[-1]), middle0)
        last = swap(inner2, "tp", 1)
        middle1 = lax.ppermute(after(inner1, inner2), "tp", MIDDLE)
        sums = [middle1, last]
    else:
        near = near_rows(spots, x, capacity)
        near = [near[0], swap(near[1], "ad", 1)]
        parts, order = near + far, range(holders)
        unsort = unsort_only(spots, total)
        full = dot(x, weight).astype(bf16)
        own, sums = lax.psum_scatter(full, "tp", scatter_dimension=1, tiled=True), []
        steps, other = tp_sums(shrink_partial(down, parts))
    deltas = expand(steps[-1], other, up, parts)
    back = [None] * holders
    for j, delta in zip(order, deltas):
        back[j] = swap(delta, "ad", j) if j else delta
    return finish(with_deltas(unsort, back, own), sums)


def solution(mesh):
    in_specs = (
        P(("rep", "ad"), "tp"),
        P(("rep", "ad")),
        P("rep"),
        P("tp", None),
        P(("rep", "tp"), "ad"),
        P(("rep", "ad"), "tp"),
    )
    out_specs = P(("rep", "ad"), "tp")
    return jax.shard_map(shards, mesh=mesh, in_specs=in_specs, out_specs=out_specs, check_vma=False)
```

```python
import functools

import jax
import jax.numpy as jnp
from jax import lax
from jax.experimental import pallas as pl
from jax.experimental.pallas import tpu as pltpu
from jax.sharding import PartitionSpec as P

ADAPTER_RANK = 64
LANES = 128
NEAR = 2
TAG_ROWS = 16
VMEM_BYTES = 32 * 1024 * 1024

bf16 = jnp.bfloat16
f32 = jnp.float32
i32 = jnp.int32


def params():
    return pltpu.CompilerParams(vmem_limit_bytes=VMEM_BYTES)


def cost(flops, nbytes):
    return pl.CostEstimate(flops=flops, bytes_accessed=nbytes, transcendentals=0)


def dot(a, b, contract=((1,), (0,))):
    return lax.dot_general(a, b, (contract, ((), ())), preferred_element_type=f32)


def in_hbm(a):
    return pltpu.with_memory_space_constraint(a, pltpu.HBM)


def iota(shape, dim):
    return lax.broadcasted_iota(i32, shape, dim)


def places(slots, capacity, holders, me, ids, table):
    rows = ids.shape[1]
    low = (iota((LANES, rows), 0) == (ids & (LANES - 1))).astype(f32).astype(bf16)
    high = iota((table.shape[0], rows), 0) == lax.shift_right_logical(ids, 7)
    found = dot(table.astype(f32).astype(bf16), low)
    slot = jnp.sum(jnp.where(high, found, 0.0), axis=0, keepdims=True).astype(i32)
    holder = split_slot(slot, slots)
    tag = (slot - holder * slots + 1).astype(f32)
    partner = holder ^ me
    mine = iota((max(8, holders), rows), 0) == partner
    ones = mine.astype(f32)
    groups = [ones[:, k:k + LANES] for k in range(0, rows, LANES)]
    earlier = (iota((LANES, LANES), 0) < iota((LANES, LANES), 1)).astype(f32).astype(bf16)
    before = dot(jnp.concatenate(groups, axis=0).astype(bf16), earlier)
    count = ones.shape[0]
    ranks, passed = [], jnp.zeros((count, 1), f32)
    for k, group in enumerate(groups):
        ranks.append(jnp.sum(group * (before[k * count:(k + 1) * count] + passed), axis=0, keepdims=True))
        passed += jnp.sum(group, axis=1, keepdims=True)
    return partner * capacity + jnp.concatenate(ranks, axis=1).astype(i32), tag


def split_slot(slot, slots):
    if slots & (slots - 1):
        return lax.div(slot, slots)
    return lax.shift_right_logical(slot, slots.bit_length() - 1)


def pick_rows(start, place, tag, x, outs):
    rows, features = x.shape
    pick = iota((len(outs) * LANES, rows), 0) + start * LANES == place
    pick = pick.astype(f32).astype(bf16)
    tags = dot(jnp.broadcast_to(tag, (TAG_ROWS, rows)).astype(bf16), pick, ((1,), (1,))).astype(bf16)
    step = min(512, features)
    for c in range(0, features, step):
        moved = dot(pick, x[:, c:c + step]).astype(bf16)
        for j, out in enumerate(outs):
            for i in range(0, step, LANES):
                out[c + i:c + i + LANES, :] = moved[j * LANES:(j + 1) * LANES, i:i + LANES]
    for j, out in enumerate(outs):
        out[features:, :] = tags[:, j * LANES:(j + 1) * LANES]


def part_rows(part, features):
    return jnp.concatenate([part[c:c + LANES, :] for c in range(0, features, LANES)], axis=1)


def tag_lanes(tags):
    return jnp.broadcast_to(tags[0:1, :].astype(f32), (LANES, LANES)).T


def part_shape(features):
    return jax.ShapeDtypeStruct((features + TAG_ROWS, LANES), bf16)


def far_body(slots, capacity, holders, me_ref, z_ref, ids_hbm, table_hbm, x_hbm, w_hbm, places_ref, *refs):
    outs, (x_buf, w_buf, ids_buf, table_buf, small_sem, x_sem, w_sem) = refs[:holders - NEAR], refs[holders - NEAR:]
    width = w_buf.shape[1]
    small = [
        pltpu.make_async_copy(ids_hbm, ids_buf, small_sem.at[0]),
        pltpu.make_async_copy(table_hbm, table_buf, small_sem.at[1]),
    ]
    x_copy = pltpu.make_async_copy(x_hbm, x_buf, x_sem)
    column = pl.multiple_of(jnp.where(z_ref[0] < 2, 3, 0) * width, width)
    w_copy = pltpu.make_async_copy(w_hbm.at[:, pl.ds(column, width)], w_buf, w_sem)
    for copy in small + [x_copy, w_copy]:
        copy.start()
    for copy in small:
        copy.wait()
    place, tag = places(slots, capacity, holders, me_ref[0], ids_buf[...], table_buf[...])
    row = iota(places_ref.shape, 0)
    places_ref[...] = jnp.where(row == 0, place, jnp.where(row == 1, tag.astype(i32), 0))
    x_copy.wait()
    pick_rows(NEAR, place, tag, x_buf, outs)
    w_copy.wait()


def far_rows(me, z, ids, table, x, weight, holders, slots, capacity, width):
    rows, features = x.shape
    ids, table = ids.reshape(1, rows), table.reshape(-1, LANES)
    smem, vmem, hbm = (pl.BlockSpec(memory_space=m) for m in (pltpu.SMEM, pltpu.VMEM, pltpu.HBM))
    shapes = [jax.ShapeDtypeStruct((8, rows), i32)]
    shapes += [part_shape(features)] * (holders - NEAR)
    shapes += [jax.ShapeDtypeStruct((rows, features), bf16), jax.ShapeDtypeStruct((features, width), bf16)]
    return pl.pallas_call(
        functools.partial(far_body, slots, capacity, holders),
        out_shape=shapes,
        in_specs=[smem, smem, hbm, hbm, hbm, hbm],
        out_specs=[vmem] * len(shapes),
        scratch_shapes=[
            pltpu.VMEM(ids.shape, i32),
            pltpu.VMEM(table.shape, i32),
            pltpu.SemaphoreType.DMA((2,)),
            pltpu.SemaphoreType.DMA(()),
            pltpu.SemaphoreType.DMA(()),
        ],
        compiler_params=params(),
        cost_estimate=cost(2 * holders * capacity * rows * features, 4 * rows * features),
        name="far_rows",
    )(me.reshape(1), z.reshape(1), in_hbm(ids), in_hbm(table), in_hbm(x), in_hbm(weight))


def near_body(places_ref, x_ref, *outs):
    pick_rows(0, places_ref[0:1, :], places_ref[1:2, :].astype(f32), x_ref, outs)


def near_rows(spots, x, capacity):
    rows, features = x.shape
    return pl.pallas_call(
        near_body,
        out_shape=[part_shape(features)] * NEAR,
        compiler_params=params(),
        cost_estimate=cost(2 * NEAR * capacity * rows * features, 4 * rows * features),
        name="near_rows",
    )(spots, x)


def first_body(x_ref, w_ref, out):
    out[...] = dot(x_ref[...], w_ref[...]).astype(bf16)


def first_block(x, w):
    (rows, features), width = x.shape, w.shape[1]
    return pl.pallas_call(
        first_body,
        out_shape=jax.ShapeDtypeStruct((rows, width), bf16),
        compiler_params=params(),
        cost_estimate=cost(2 * rows * features * width, 2 * features * (rows + width)),
        name="first_block",
    )(x, w)


def second_body(z_ref, spots_ref, x_ref, w_hbm, *refs):
    near, (second, unsort, w_buf, sem) = refs[:NEAR], refs[NEAR:]
    copies = weight_copies((jnp.where(z_ref[0] < 2, 2, 1),), w_hbm, w_buf, sem)
    near_body(spots_ref, x_ref, *near)
    unsort_matrix(spots_ref, unsort)
    copies[0].wait()
    second[...] = dot(x_ref[...], w_buf[0]).astype(bf16)


def late_body(z_ref, x_ref, w_hbm, third, own, w_buf, sem):
    z = z_ref[0]
    copies = weight_copies((z ^ 1, z), w_hbm, w_buf, sem)
    for k, out in enumerate((third, own)):
        copies[k].wait()
        out[...] = dot(x_ref[...], w_buf[k]).astype(bf16)


def weight_copies(blocks, w_hbm, w_buf, sem):
    width = w_buf.shape[2]
    copies = []
    for k, block in enumerate(blocks):
        column = pl.multiple_of(block * width, width)
        copies.append(pltpu.make_async_copy(w_hbm.at[:, pl.ds(column, width)], w_buf.at[k], sem.at[k]))
        copies[k].start()
    return copies


def unsort_matrix(place_ref, unsort):
    rows, total = unsort.shape
    place = jnp.broadcast_to(place_ref[0:1, :].astype(f32), (LANES, rows)).T
    lane = iota((rows, LANES), 1).astype(f32)
    for k in range(total // LANES):
        unsort[:, k * LANES:(k + 1) * LANES] = (place == lane + float(k * LANES)).astype(f32).astype(bf16)


def second_block(z, spots, x, weight, width, total):
    rows, features = x.shape
    smem, vmem, hbm = (pl.BlockSpec(memory_space=m) for m in (pltpu.SMEM, pltpu.VMEM, pltpu.HBM))
    shapes = [part_shape(features)] * NEAR
    shapes += [jax.ShapeDtypeStruct((rows, width), bf16), jax.ShapeDtypeStruct((rows, total), bf16)]
    return pl.pallas_call(
        second_body,
        out_shape=shapes,
        in_specs=[smem, vmem, vmem, hbm],
        out_specs=[vmem] * len(shapes),
        scratch_shapes=[pltpu.VMEM((1, features, width), bf16), pltpu.SemaphoreType.DMA((1,))],
        compiler_params=params(),
        cost_estimate=cost(6 * rows * features * width, 2 * features * (rows + 4 * width)),
        name="second_block",
    )(z.reshape(1), spots, x, in_hbm(weight))


def late_blocks(z, x, weight, width):
    rows, features = x.shape
    smem, vmem, hbm = (pl.BlockSpec(memory_space=m) for m in (pltpu.SMEM, pltpu.VMEM, pltpu.HBM))
    return pl.pallas_call(
        late_body,
        out_shape=[jax.ShapeDtypeStruct((rows, width), bf16)] * 2,
        in_specs=[smem, vmem, hbm],
        out_specs=[vmem] * 2,
        scratch_shapes=[pltpu.VMEM((2, features, width), bf16), pltpu.SemaphoreType.DMA((2,))],
        compiler_params=params(),
        cost_estimate=cost(4 * rows * features * width, 2 * features * (rows + 2 * width)),
        name="late_blocks",
    )(z.reshape(1), x, in_hbm(weight))


def unsort_only(place, total):
    return pl.pallas_call(
        unsort_matrix,
        out_shape=jax.ShapeDtypeStruct((place.shape[1], total), bf16),
        compiler_params=params(),
        name="unsort",
    )(place)


def slot_mask(tag, group):
    lane = iota(tag.shape, 1)
    return tag == jnp.where(lane < ADAPTER_RANK, 2 * group + 1, 2 * group + 2).astype(f32)


def shrink_body(kept, down_ref, *refs):
    parts, out = refs[1 if kept else 0:-1], refs[-1]
    features, width = down_ref.shape
    half = LANES // 2
    first = iota((half, LANES), 1) < ADAPTER_RANK
    if kept:
        out[:kept, :] = refs[0][...]
    for k, part in enumerate(parts):
        tag = tag_lanes(part[features:, :])
        full = dot(part_rows(part, features), down_ref[...])
        total = jnp.zeros((LANES, LANES), f32)
        for group in range(width // LANES):
            total += jnp.where(slot_mask(tag, group), full[:, group * LANES:(group + 1) * LANES], 0.0)
        total += pltpu.roll(total, ADAPTER_RANK, 1)
        spot = slice(kept + k * half, kept + (k + 1) * half)
        out[spot, :] = jnp.where(first, total[:half], total[half:]).astype(bf16)


def shrink_partial(down, parts, done=()):
    features, width = down.shape
    total = len(parts) * LANES
    kept = sum(d.shape[0] for d in done)
    return pl.pallas_call(
        functools.partial(shrink_body, kept),
        out_shape=jax.ShapeDtypeStruct((kept + total // 2, LANES), bf16),
        compiler_params=params(),
        cost_estimate=cost(2 * total * features * width, 2 * features * (total + width)),
        name="shrink_partial",
    )(down, *done, *parts)


def expand_body(count, one_ref, two_ref, up_ref, *refs):
    tags, outs = refs[:count], refs[count:]
    capacity = outs[0].shape[0]
    half = capacity // 2
    up = up_ref[...]
    first = iota((half, LANES), 1) < ADAPTER_RANK
    for k in range(count):
        part = pl.ds(k * half, half)
        shrink = (one_ref[part, :].astype(f32) + two_ref[part, :].astype(f32)).astype(bf16).astype(f32)
        turned = pltpu.roll(shrink, ADAPTER_RANK, 1)
        rows = jnp.concatenate([jnp.where(first, shrink, turned), jnp.where(first, turned, shrink)], axis=0)
        tag = tag_lanes(tags[k][...])
        spread = [
            jnp.where(slot_mask(tag, group), rows, 0.0).astype(bf16) for group in range(up.shape[0] // LANES)
        ]
        outs[k][...] = dot(jnp.concatenate(spread, axis=1), up).astype(bf16)


def expand(one, two, up, parts):
    capacity, count = LANES, len(parts)
    last = parts[0].shape[0] // TAG_ROWS - 1
    tag_block = pl.BlockSpec((TAG_ROWS, LANES), lambda i: (last, 0))
    whole = lambda a: pl.BlockSpec(a.shape, lambda i: (0, 0))
    columns = up.shape[1]
    return pl.pallas_call(
        functools.partial(expand_body, count),
        grid=(1,),
        out_shape=[jax.ShapeDtypeStruct((capacity, columns), bf16)] * count,
        in_specs=[whole(one), whole(two), whole(up)] + [tag_block] * count,
        out_specs=[pl.BlockSpec((capacity, columns), lambda i: (0, 0))] * count,
        compiler_params=params(),
        cost_estimate=cost(80 * count * capacity * up.size, 80 * (up.size + count * capacity * columns)),
        name="expand",
    )(one, two, up, *parts)


def deltas_body(unsort_ref, own_ref, *refs):
    deltas, out = refs[:-1], refs[-1]
    placed = dot(unsort_ref[...], jnp.concatenate([d[...] for d in deltas], axis=0))
    out[...] = own_ref[...].astype(f32) + placed


def with_deltas(unsort, deltas, own):
    rows, columns = own.shape
    return pl.pallas_call(
        deltas_body,
        out_shape=jax.ShapeDtypeStruct((rows, columns), f32),
        compiler_params=params(),
        cost_estimate=cost(2 * rows * unsort.shape[1] * columns, 12 * rows * columns),
        name="with_deltas",
    )(unsort, own, *deltas)


def finish_body(start_ref, *refs):
    terms, (out_hbm, out_buf, sem) = refs[:-3], refs[-3:]
    pieces = sem.shape[0]
    step = out_buf.shape[0] // pieces
    copies = []
    for k in range(pieces):
        part = pl.ds(k * step, step)
        total = start_ref[part, :]
        for term in terms:
            total += term[part, :].astype(f32)
        out_buf[part, :] = total.astype(bf16)
        copies.append(pltpu.make_async_copy(out_buf.at[part, :], out_hbm.at[part, :], sem.at[k]))
        copies[k].start()
    for copy in copies:
        copy.wait()


def finish(start, terms):
    vmem, hbm = (pl.BlockSpec(memory_space=m) for m in (pltpu.VMEM, pltpu.HBM))
    return pl.pallas_call(
        finish_body,
        out_shape=jax.ShapeDtypeStruct(start.shape, bf16),
        in_specs=[vmem] * (1 + len(terms)),
        out_specs=hbm,
        scratch_shapes=[pltpu.VMEM(start.shape, bf16), pltpu.SemaphoreType.DMA((4,))],
        compiler_params=params(),
        cost_estimate=cost(start.size, 8 * start.size),
        name="finish",
    )(start, *terms)


def both(a, b):
    return (a.astype(f32) + b.astype(f32)).astype(bf16)


def after(value, *others):
    return lax.optimization_barrier((value,) + others)[0]


def swap(value, axis, bit):
    return lax.ppermute(value, axis, [(i, i ^ bit) for i in range(lax.axis_size(axis))])


EDGE = [(0, 1), (3, 2)]
MIDDLE = [(1, 2), (2, 1)]


def tp_sums(mine, *before):
    sums, bit = [mine], 1
    while True:
        other = swap(sums[-1], "tp", bit)
        bit *= 2
        if bit >= lax.axis_size("tp"):
            return sums, other
        sums.append(both(after(sums[-1], *before), other))


def shards(x, ids, table, weight, down, up):
    holders = lax.axis_size("ad")
    capacity = x.shape[0] // 4
    assert capacity == LANES
    slots = up.shape[0] // ADAPTER_RANK
    width = up.shape[1]
    total = holders * capacity
    me, z = lax.axis_index("ad"), lax.axis_index("tp")
    spots, *far, x, w = far_rows(me, z, ids, table, x, weight, holders, slots, capacity, width)
    far = [swap(rows, "ad", j + NEAR) for j, rows in enumerate(far)]
    if lax.axis_size("tp") == 4 and holders == 4:
        first = first_block(x, w)
        edge0 = lax.ppermute(first, "tp", EDGE)
        *near, second, unsort = second_block(z, after(spots, first), x, weight, width, total)
        near = [near[0], swap(near[1], "ad", 1)]
        edge1 = lax.ppermute(second, "tp", EDGE)
        early = shrink_partial(down, [near[0], far[0]])
        third, own = late_blocks(z, after(x, early), weight, width)
        inner0 = both(after(first, early, third), edge0)
        middle0 = lax.ppermute(inner0, "tp", MIDDLE)
        early = shrink_partial(down, [after(near[1], inner0)], [early])
        mine = shrink_partial(down, [after(far[1], early)], [early])
        parts, order = [near[0], far[0], near[1], far[1]], (0, 2, 1, 3)
        inner1 = both(after(second, mine), edge1)
        steps, other = tp_sums(mine, inner1)
        inner2 = both(after(third, steps[-1]), middle0)
        last = swap(inner2, "tp", 1)
        middle1 = lax.ppermute(after(inner1, inner2), "tp", MIDDLE)
        sums = [middle1, last]
    else:
        near = near_rows(spots, x, capacity)
        near = [near[0], swap(near[1], "ad", 1)]
        parts, order = near + far, range(holders)
        unsort = unsort_only(spots, total)
        full = dot(x, weight).astype(bf16)
        own, sums = lax.psum_scatter(full, "tp", scatter_dimension=1, tiled=True), []
        steps, other = tp_sums(shrink_partial(down, parts))
    deltas = expand(steps[-1], other, up, parts)
    back = [None] * holders
    for j, delta in zip(order, deltas):
        back[j] = swap(delta, "ad", j) if j else delta
    return finish(with_deltas(unsort, back, own), sums)


def solution(mesh):
    in_specs = (
        P(("rep", "ad"), "tp"),
        P(("rep", "ad")),
        P("rep"),
        P("tp", None),
        P(("rep", "tp"), "ad"),
        P(("rep", "ad"), "tp"),
    )
    out_specs = P(("rep", "ad"), "tp")
    return jax.shard_map(shards, mesh=mesh, in_specs=in_specs, out_specs=out_specs, check_vma=False)
```

```python
import functools

import jax
import jax.numpy as jnp
from jax import lax
from jax.experimental import pallas as pl
from jax.experimental.pallas import tpu as pltpu
from jax.sharding import PartitionSpec as P

ADAPTER_RANK = 64
LANES = 128
NEAR = 2
TAG_ROWS = 16
VMEM_BYTES = 32 * 1024 * 1024

bf16 = jnp.bfloat16
f32 = jnp.float32
i32 = jnp.int32


def params():
    return pltpu.CompilerParams(vmem_limit_bytes=VMEM_BYTES)


def cost(flops, nbytes):
    return pl.CostEstimate(flops=flops, bytes_accessed=nbytes, transcendentals=0)


def dot(a, b, contract=((1,), (0,))):
    return lax.dot_general(a, b, (contract, ((), ())), preferred_element_type=f32)


def in_hbm(a):
    return pltpu.with_memory_space_constraint(a, pltpu.HBM)


def iota(shape, dim):
    return lax.broadcasted_iota(i32, shape, dim)


def places(slots, capacity, holders, me, ids, table):
    rows = ids.shape[1]
    low = (iota((LANES, rows), 0) == (ids & (LANES - 1))).astype(f32).astype(bf16)
    high = iota((table.shape[0], rows), 0) == lax.shift_right_logical(ids, 7)
    found = dot(table.astype(f32).astype(bf16), low)
    slot = jnp.sum(jnp.where(high, found, 0.0), axis=0, keepdims=True).astype(i32)
    holder = split_slot(slot, slots)
    tag = (slot - holder * slots + 1).astype(f32)
    partner = holder ^ me
    mine = iota((max(8, holders), rows), 0) == partner
    ones = mine.astype(f32)
    groups = [ones[:, k:k + LANES] for k in range(0, rows, LANES)]
    earlier = (iota((LANES, LANES), 0) < iota((LANES, LANES), 1)).astype(f32).astype(bf16)
    before = dot(jnp.concatenate(groups, axis=0).astype(bf16), earlier)
    count = ones.shape[0]
    ranks, passed = [], jnp.zeros((count, 1), f32)
    for k, group in enumerate(groups):
        ranks.append(jnp.sum(group * (before[k * count:(k + 1) * count] + passed), axis=0, keepdims=True))
        passed += jnp.sum(group, axis=1, keepdims=True)
    return partner * capacity + jnp.concatenate(ranks, axis=1).astype(i32), tag


def split_slot(slot, slots):
    if slots & (slots - 1):
        return lax.div(slot, slots)
    return lax.shift_right_logical(slot, slots.bit_length() - 1)


def pick_rows(start, place, tag, x, outs):
    rows, features = x.shape
    pick = iota((len(outs) * LANES, rows), 0) + start * LANES == place
    pick = pick.astype(f32).astype(bf16)
    tags = dot(jnp.broadcast_to(tag, (TAG_ROWS, rows)).astype(bf16), pick, ((1,), (1,))).astype(bf16)
    step = min(512, features)
    for c in range(0, features, step):
        moved = dot(pick, x[:, c:c + step]).astype(bf16)
        for j, out in enumerate(outs):
            for i in range(0, step, LANES):
                out[c + i:c + i + LANES, :] = moved[j * LANES:(j + 1) * LANES, i:i + LANES]
    for j, out in enumerate(outs):
        out[features:, :] = tags[:, j * LANES:(j + 1) * LANES]


def part_rows(part, features):
    return jnp.concatenate([part[c:c + LANES, :] for c in range(0, features, LANES)], axis=1)


def tag_lanes(tags):
    return jnp.broadcast_to(tags[0:1, :].astype(f32), (LANES, LANES)).T


def part_shape(features):
    return jax.ShapeDtypeStruct((features + TAG_ROWS, LANES), bf16)


def far_body(slots, capacity, holders, me_ref, z_ref, ids_hbm, table_hbm, x_hbm, w_hbm, places_ref, *refs):
    outs, (x_buf, w_buf, ids_buf, table_buf, small_sem, x_sem, w_sem) = refs[:holders - NEAR], refs[holders - NEAR:]
    width = w_buf.shape[1]
    small = [
        pltpu.make_async_copy(ids_hbm, ids_buf, small_sem.at[0]),
        pltpu.make_async_copy(table_hbm, table_buf, small_sem.at[1]),
    ]
    x_copy = pltpu.make_async_copy(x_hbm, x_buf, x_sem)
    column = pl.multiple_of(jnp.where(z_ref[0] < 2, 3, 0) * width, width)
    w_copy = pltpu.make_async_copy(w_hbm.at[:, pl.ds(column, width)], w_buf, w_sem)
    for copy in small + [x_copy, w_copy]:
        copy.start()
    for copy in small:
        copy.wait()
    place, tag = places(slots, capacity, holders, me_ref[0], ids_buf[...], table_buf[...])
    row = iota(places_ref.shape, 0)
    places_ref[...] = jnp.where(row == 0, place, jnp.where(row == 1, tag.astype(i32), 0))
    x_copy.wait()
    pick_rows(NEAR, place, tag, x_buf, outs)
    w_copy.wait()


def far_rows(me, z, ids, table, x, weight, holders, slots, capacity, width):
    rows, features = x.shape
    ids, table = ids.reshape(1, rows), table.reshape(-1, LANES)
    smem, vmem, hbm = (pl.BlockSpec(memory_space=m) for m in (pltpu.SMEM, pltpu.VMEM, pltpu.HBM))
    shapes = [jax.ShapeDtypeStruct((8, rows), i32)]
    shapes += [part_shape(features)] * (holders - NEAR)
    shapes += [jax.ShapeDtypeStruct((rows, features), bf16), jax.ShapeDtypeStruct((features, width), bf16)]
    return pl.pallas_call(
        functools.partial(far_body, slots, capacity, holders),
        out_shape=shapes,
        in_specs=[smem, smem, hbm, hbm, hbm, hbm],
        out_specs=[vmem] * len(shapes),
        scratch_shapes=[
            pltpu.VMEM(ids.shape, i32),
            pltpu.VMEM(table.shape, i32),
            pltpu.SemaphoreType.DMA((2,)),
            pltpu.SemaphoreType.DMA(()),
            pltpu.SemaphoreType.DMA(()),
        ],
        compiler_params=params(),
        cost_estimate=cost(2 * holders * capacity * rows * features, 4 * rows * features),
        name="far_rows",
    )(me.reshape(1), z.reshape(1), in_hbm(ids), in_hbm(table), in_hbm(x), in_hbm(weight))


def near_body(places_ref, x_ref, *outs):
    pick_rows(0, places_ref[0:1, :], places_ref[1:2, :].astype(f32), x_ref, outs)


def near_rows(spots, x, capacity):
    rows, features = x.shape
    return pl.pallas_call(
        near_body,
        out_shape=[part_shape(features)] * NEAR,
        compiler_params=params(),
        cost_estimate=cost(2 * NEAR * capacity * rows * features, 4 * rows * features),
        name="near_rows",
    )(spots, x)


def first_body(x_ref, w_ref, out):
    out[...] = dot(x_ref[...], w_ref[...]).astype(bf16)


def first_block(x, w):
    (rows, features), width = x.shape, w.shape[1]
    return pl.pallas_call(
        first_body,
        out_shape=jax.ShapeDtypeStruct((rows, width), bf16),
        compiler_params=params(),
        cost_estimate=cost(2 * rows * features * width, 2 * features * (rows + width)),
        name="first_block",
    )(x, w)


def rest_body(z_ref, spots_ref, x_ref, w_hbm, *refs):
    near, (second, third, own, unsort, w_buf, sem) = refs[:NEAR], refs[NEAR:]
    z = z_ref[0]
    width = own.shape[1]
    copies = []
    for k, block in enumerate((jnp.where(z < 2, 2, 1), z ^ 1, z)):
        column = pl.multiple_of(block * width, width)
        copies.append(pltpu.make_async_copy(w_hbm.at[:, pl.ds(column, width)], w_buf.at[k], sem.at[k]))
        copies[k].start()
    near_body(spots_ref, x_ref, *near)
    unsort_matrix(spots_ref, unsort)
    for k, out in enumerate((second, third, own)):
        copies[k].wait()
        out[...] = dot(x_ref[...], w_buf[k]).astype(bf16)


def unsort_matrix(place_ref, unsort):
    rows, total = unsort.shape
    place = jnp.broadcast_to(place_ref[0:1, :].astype(f32), (LANES, rows)).T
    lane = iota((rows, LANES), 1).astype(f32)
    for k in range(total // LANES):
        unsort[:, k * LANES:(k + 1) * LANES] = (place == lane + float(k * LANES)).astype(f32).astype(bf16)


def rest(z, spots, x, weight, width, total, capacity):
    rows, features = x.shape
    smem, vmem, hbm = (pl.BlockSpec(memory_space=m) for m in (pltpu.SMEM, pltpu.VMEM, pltpu.HBM))
    shapes = [part_shape(features)] * NEAR
    shapes += [jax.ShapeDtypeStruct((rows, width), bf16)] * 3 + [jax.ShapeDtypeStruct((rows, total), bf16)]
    return pl.pallas_call(
        rest_body,
        out_shape=shapes,
        in_specs=[smem, vmem, vmem, hbm],
        out_specs=[vmem] * len(shapes),
        scratch_shapes=[pltpu.VMEM((3, features, width), bf16), pltpu.SemaphoreType.DMA((3,))],
        compiler_params=params(),
        cost_estimate=cost(6 * rows * features * width, 2 * features * (rows + 4 * width)),
        name="rest",
    )(z.reshape(1), spots, x, in_hbm(weight))


def unsort_only(place, total):
    return pl.pallas_call(
        unsort_matrix,
        out_shape=jax.ShapeDtypeStruct((place.shape[1], total), bf16),
        compiler_params=params(),
        name="unsort",
    )(place)


def slot_mask(tag, group):
    lane = iota(tag.shape, 1)
    return tag == jnp.where(lane < ADAPTER_RANK, 2 * group + 1, 2 * group + 2).astype(f32)


def shrink_body(kept, down_ref, *refs):
    parts, out = refs[1 if kept else 0:-1], refs[-1]
    features, width = down_ref.shape
    half = LANES // 2
    first = iota((half, LANES), 1) < ADAPTER_RANK
    if kept:
        out[:kept, :] = refs[0][...]
    for k, part in enumerate(parts):
        tag = tag_lanes(part[features:, :])
        full = dot(part_rows(part, features), down_ref[...])
        total = jnp.zeros((LANES, LANES), f32)
        for group in range(width // LANES):
            total += jnp.where(slot_mask(tag, group), full[:, group * LANES:(group + 1) * LANES], 0.0)
        total += pltpu.roll(total, ADAPTER_RANK, 1)
        spot = slice(kept + k * half, kept + (k + 1) * half)
        out[spot, :] = jnp.where(first, total[:half], total[half:]).astype(bf16)


def shrink_partial(down, parts, done=()):
    features, width = down.shape
    total = len(parts) * LANES
    kept = sum(d.shape[0] for d in done)
    return pl.pallas_call(
        functools.partial(shrink_body, kept),
        out_shape=jax.ShapeDtypeStruct((kept + total // 2, LANES), bf16),
        compiler_params=params(),
        cost_estimate=cost(2 * total * features * width, 2 * features * (total + width)),
        name="shrink_partial",
    )(down, *done, *parts)


def expand_body(count, one_ref, two_ref, up_ref, *refs):
    tags, outs = refs[:count], refs[count:]
    capacity = outs[0].shape[0]
    half = capacity // 2
    up = up_ref[...]
    first = iota((half, LANES), 1) < ADAPTER_RANK
    for k in range(count):
        part = pl.ds(k * half, half)
        shrink = (one_ref[part, :].astype(f32) + two_ref[part, :].astype(f32)).astype(bf16).astype(f32)
        turned = pltpu.roll(shrink, ADAPTER_RANK, 1)
        rows = jnp.concatenate([jnp.where(first, shrink, turned), jnp.where(first, turned, shrink)], axis=0)
        tag = tag_lanes(tags[k][...])
        spread = [
            jnp.where(slot_mask(tag, group), rows, 0.0).astype(bf16) for group in range(up.shape[0] // LANES)
        ]
        outs[k][...] = dot(jnp.concatenate(spread, axis=1), up).astype(bf16)


def expand(one, two, up, parts):
    capacity, count = LANES, len(parts)
    last = parts[0].shape[0] // TAG_ROWS - 1
    tag_block = pl.BlockSpec((TAG_ROWS, LANES), lambda i: (last, 0))
    whole = lambda a: pl.BlockSpec(a.shape, lambda i: (0, 0))
    columns = up.shape[1]
    return pl.pallas_call(
        functools.partial(expand_body, count),
        grid=(1,),
        out_shape=[jax.ShapeDtypeStruct((capacity, columns), bf16)] * count,
        in_specs=[whole(one), whole(two), whole(up)] + [tag_block] * count,
        out_specs=[pl.BlockSpec((capacity, columns), lambda i: (0, 0))] * count,
        compiler_params=params(),
        cost_estimate=cost(80 * count * capacity * up.size, 80 * (up.size + count * capacity * columns)),
        name="expand",
    )(one, two, up, *parts)


def deltas_body(unsort_ref, own_ref, *refs):
    deltas, out = refs[:-1], refs[-1]
    placed = dot(unsort_ref[...], jnp.concatenate([d[...] for d in deltas], axis=0))
    out[...] = own_ref[...].astype(f32) + placed


def with_deltas(unsort, deltas, own):
    rows, columns = own.shape
    return pl.pallas_call(
        deltas_body,
        out_shape=jax.ShapeDtypeStruct((rows, columns), f32),
        compiler_params=params(),
        cost_estimate=cost(2 * rows * unsort.shape[1] * columns, 12 * rows * columns),
        name="with_deltas",
    )(unsort, own, *deltas)


def finish_body(start_ref, *refs):
    terms, (out_hbm, out_buf, sem) = refs[:-3], refs[-3:]
    pieces = sem.shape[0]
    step = out_buf.shape[0] // pieces
    copies = []
    for k in range(pieces):
        part = pl.ds(k * step, step)
        total = start_ref[part, :]
        for term in terms:
            total += term[part, :].astype(f32)
        out_buf[part, :] = total.astype(bf16)
        copies.append(pltpu.make_async_copy(out_buf.at[part, :], out_hbm.at[part, :], sem.at[k]))
        copies[k].start()
    for copy in copies:
        copy.wait()


def finish(start, terms):
    vmem, hbm = (pl.BlockSpec(memory_space=m) for m in (pltpu.VMEM, pltpu.HBM))
    return pl.pallas_call(
        finish_body,
        out_shape=jax.ShapeDtypeStruct(start.shape, bf16),
        in_specs=[vmem] * (1 + len(terms)),
        out_specs=hbm,
        scratch_shapes=[pltpu.VMEM(start.shape, bf16), pltpu.SemaphoreType.DMA((4,))],
        compiler_params=params(),
        cost_estimate=cost(start.size, 8 * start.size),
        name="finish",
    )(start, *terms)


def both(a, b):
    return (a.astype(f32) + b.astype(f32)).astype(bf16)


def after(value, *others):
    return lax.optimization_barrier((value,) + others)[0]


def swap(value, axis, bit):
    return lax.ppermute(value, axis, [(i, i ^ bit) for i in range(lax.axis_size(axis))])


EDGE = [(0, 1), (3, 2)]
MIDDLE = [(1, 2), (2, 1)]


def tp_sums(mine, *before):
    sums, bit = [mine], 1
    while True:
        other = swap(sums[-1], "tp", bit)
        bit *= 2
        if bit >= lax.axis_size("tp"):
            return sums, other
        sums.append(both(after(sums[-1], *before), other))


def shards(x, ids, table, weight, down, up):
    holders = lax.axis_size("ad")
    capacity = x.shape[0] // 4
    assert capacity == LANES
    slots = up.shape[0] // ADAPTER_RANK
    width = up.shape[1]
    total = holders * capacity
    me, z = lax.axis_index("ad"), lax.axis_index("tp")
    spots, *far, x, w = far_rows(me, z, ids, table, x, weight, holders, slots, capacity, width)
    far = [swap(rows, "ad", j + NEAR) for j, rows in enumerate(far)]
    if lax.axis_size("tp") == 4 and holders == 4:
        first = first_block(x, w)
        edge0 = lax.ppermute(first, "tp", EDGE)
        *near, second, third, own, unsort = rest(z, after(spots, first), x, weight, width, total, capacity)
        near = [near[0], swap(near[1], "ad", 1)]
        edge1 = lax.ppermute(second, "tp", EDGE)
        early = shrink_partial(down, [near[0], far[0]])
        inner0 = both(after(first, early), edge0)
        middle0 = lax.ppermute(inner0, "tp", MIDDLE)
        early = shrink_partial(down, [after(near[1], inner0)], [early])
        mine = shrink_partial(down, [after(far[1], early)], [early])
        parts, order = [near[0], far[0], near[1], far[1]], (0, 2, 1, 3)
        inner1 = both(after(second, mine), edge1)
        steps, other = tp_sums(mine, inner1)
        inner2 = both(after(third, steps[-1]), middle0)
        middle1 = lax.ppermute(after(inner1, steps[-1]), "tp", MIDDLE)
        last = swap(inner2, "tp", 1)
        sums = [middle1, last]
    else:
        near = near_rows(spots, x, capacity)
        near = [near[0], swap(near[1], "ad", 1)]
        parts, order = near + far, range(holders)
        unsort = unsort_only(spots, total)
        full = dot(x, weight).astype(bf16)
        own, sums = lax.psum_scatter(full, "tp", scatter_dimension=1, tiled=True), []
        steps, other = tp_sums(shrink_partial(down, parts))
    deltas = expand(steps[-1], other, up, parts)
    back = [None] * holders
    for j, delta in zip(order, deltas):
        back[j] = swap(delta, "ad", j) if j else delta
    return finish(with_deltas(unsort, back, own), sums)


def solution(mesh):
    in_specs = (
        P(("rep", "ad"), "tp"),
        P(("rep", "ad")),
        P("rep"),
        P("tp", None),
        P(("rep", "tp"), "ad"),
        P(("rep", "ad"), "tp"),
    )
    out_specs = P(("rep", "ad"), "tp")
    return jax.shard_map(shards, mesh=mesh, in_specs=in_specs, out_specs=out_specs, check_vma=False)
```
